32 devices in a mesh: dp: 4 (over z), fsdp: 8 (over y, x, core).
Axes of the slice: x: 2, y: 2, z: 4, core: 2. Of those that a mesh axis runs over, the one named last changes fastest.
Arguments:
- features: float32 [98304, 512], P(('dp', 'fsdp')), may hold values from -6 to 6
- cotangent: float32 [3, 98304, 256], P(None, ('dp', 'fsdp')), may hold values from -6 to 6
- counts: int32 [32], P(('dp', 'fsdp')), may hold values from 1536 to 3072, as said below
- keep: int32 [98304], P(('dp', 'fsdp')), may hold values 0 or 1
- w_in: float32 [6, 512, 256], P(None, 'fsdp'), may hold values from -0.25 to 0.25
- in_bias: float32 [6, 256], P(None, 'fsdp'), may hold values from -3 to 3
- norm_gain: float32 [6, 256], P(None, 'fsdp'), may hold values from 0.1 to 1.9
- norm_bias: float32 [6, 256], P(None, 'fsdp'), may hold values from -3 to 3
- w_out: float32 [6, 256, 256], P(None, 'fsdp'), may hold values from -0.375 to 0.375
- out_bias: float32 [6, 256], P(None, 'fsdp'), may hold values from -3 to 3
- task_gate: float32 [2, 512, 4], P(None, 'fsdp'), may hold values from -0.125 to 0.125
- shared_gate: float32 [512, 6], P('fsdp'), may hold values from -0.125 to 0.125
Outputs:
- outputs: float32 [3, 98304, 256], P(None, ('dp', 'fsdp'))
- grad_features: float32 [98304, 512], P(('dp', 'fsdp'))
- grad_w_in: float32 [6, 512, 256], P(None, 'fsdp')
- grad_in_bias: float32 [6, 256], P(None, 'fsdp')
- grad_norm_gain: float32 [6, 256], P(None, 'fsdp')
- grad_norm_bias: float32 [6, 256], P(None, 'fsdp')
- grad_w_out: float32 [6, 256, 256], P(None, 'fsdp')
- grad_out_bias: float32 [6, 256], P(None, 'fsdp')
- grad_task_gate: float32 [2, 512, 4], P(None, 'fsdp')
- grad_shared_gate: float32 [512, 6], P('fsdp')
The draws below stay inside these ranges and needn't reach their ends.
Inputs may be any that keep to these rules, and one draw needn't show every extreme that they name: `counts`: each device's count is at least half of its 3072 slots; in every draw some device uses all of them.
All inputs are finite; a program needn't handle non-finite values. No bound on the sum of `keep` on one device may be relied on, other than what follows from the above.
Results may differ from the reference program's by a relative error of at most 0.0003.
Values sent between devices are 32-bit elements; how exact they have to be, the bound alone decides.
No kernel may reach another device: no remote copies, remote signals or barrier semaphores. Data moves between devices by JAX's collectives and lax.ppermute only.
A program may use at most 320 MiB of HBM per device.

```python
import jax
import jax.numpy as jnp
from jax import lax

D = 512
H = 256
TASKS = 2
SPEC = 2
SHARED = 2
EXPERTS = 6
ROWS_DEV = 3072
ROWS = 98304
N_DP = 4
N_FSDP = 8


def draw_counts(key, part):
    key = jax.random.fold_in(key, 11)
    first, second = jax.random.split(key)
    devices = N_DP * N_FSDP
    values = jax.random.randint(first, (devices,), ROWS_DEV // 2, ROWS_DEV + 1)
    fullest = jax.random.randint(second, (), 0, devices)
    return jnp.where(jnp.arange(devices, dtype=jnp.int32) == fullest, ROWS_DEV, values).astype(jnp.int32)


def with_ends(values, key, low, largest):
    longest = values.shape.index(max(values.shape))
    spots = []
    for shift in (0, 1):
        where = [jax.random.randint(jax.random.fold_in(key, axis), (), 0, length) for axis, length in enumerate(values.shape)]
        where[longest] = (where[longest] + shift) % values.shape[longest]
        spots.append(tuple(where))
    return values.at[spots[0]].set(low).at[spots[1]].set(largest)


def shard_levels(rng, shape, shards, least, top_value):
    gain = 1.0
    for dim, shards_of in shards:
        steps = jax.random.uniform(jax.random.fold_in(jax.random.fold_in(rng, 6), dim), (shards_of,), jnp.float32, least / len(shards), top_value / len(shards))
        gain = gain * jnp.repeat(jnp.exp(steps), shape[dim] // shards_of).reshape((-1,) + (1,) * (len(shape) - 1 - dim))
    return gain


def noise(key, extent, width, most, cuts=(), held_as=jnp.bfloat16):
    gain = shard_levels(key, extent, cuts, -0.22, 0.18) if cuts else 1.0
    array = jax.random.normal(key, extent, jnp.float32) * width * gain
    return jnp.minimum(jnp.maximum(array, -most), most).astype(held_as)


def setup_inputs(seed: int = 0) -> dict:
    arg_keys = jax.random.split(jax.random.key(seed), 13)
    return {
        "features": noise(arg_keys[0], (ROWS, D), 1.0, 6.0, ((0, 32),), jnp.float32),
        "cotangent": noise(arg_keys[1], (TASKS + 1, ROWS, H), 1.0, 6.0, ((1, 32),), jnp.float32),
        "counts": draw_counts(jax.random.fold_in(arg_keys[12], 71), 0),
        "keep": with_ends((jax.random.randint(arg_keys[3], (ROWS,), 0, 8) < 7).astype(jnp.int32), jax.random.fold_in(arg_keys[3], 1), 0, 1),
        "w_in": noise(arg_keys[4], (EXPERTS, D, H), D ** -0.5, 0.25, ((1, 8),), jnp.float32),
        "in_bias": noise(arg_keys[5], (EXPERTS, H), 0.5, 3.0, ((1, 8),), jnp.float32),
        "norm_gain": jnp.clip(1.0 + 0.18 * jax.random.normal(arg_keys[6], (EXPERTS, H), jnp.float32), 0.1, 1.9),
        "norm_bias": noise(arg_keys[7], (EXPERTS, H), 0.5, 3.0, ((1, 8),), jnp.float32),
        "w_out": noise(arg_keys[8], (EXPERTS, H, H), H ** -0.5, 0.375, ((1, 8),), jnp.float32),
        "out_bias": noise(arg_keys[9], (EXPERTS, H), 0.5, 3.0, ((1, 8),), jnp.float32),
        "task_gate": noise(arg_keys[10], (TASKS, D, SPEC + SHARED), (4 * D) ** -0.5, 0.125, ((1, 8),), jnp.float32),
        "shared_gate": noise(arg_keys[11], (D, EXPERTS), (4 * D) ** -0.5, 0.125, ((0, 8),), jnp.float32),
    }


EPSILON = 1e-05

@jax.custom_vjp
def low(v):
    return lax.optimization_barrier(v.astype(jnp.bfloat16)).astype(jnp.float32)

@jax.custom_vjp
def low_back(v):
    return v

def low_keep(v):
    return (low(v), None)

def low_pass(kept, grad):
    return (grad,)

def back_keep(v):
    return (v, None)

def back_low(kept, grad):
    return (low(grad),)
low.defvjp(low_keep, low_pass)
low_back.defvjp(back_keep, back_low)

def forward(features, w_in, in_bias, norm_gain, norm_bias, w_out, out_bias, task_gate, shared_gate):
    highest = lax.Precision.HIGHEST
    preact = jnp.einsum('bd,edh->ebh', features, w_in, precision=highest) + in_bias[:, None, :]
    active = jax.nn.silu(preact)
    centred = active - lax.optimization_barrier(jnp.mean(active, -1, keepdims=True))
    spread = lax.optimization_barrier(jnp.mean(centred * centred, -1, keepdims=True))
    normed = centred * lax.rsqrt(spread + EPSILON) * norm_gain[:, None, :] + norm_bias[:, None, :]
    expert = jax.nn.silu(jnp.einsum('ebh,ehk->ebk', normed, w_out, precision=highest) + out_bias[:, None, :])
    results = []
    for index_task in range(TASKS):
        weights = jax.nn.softmax(jnp.dot(features, task_gate[index_task], precision=highest), axis=-1)
        chosen = jnp.concatenate([expert[index_task * SPEC:(index_task + 1) * SPEC], expert[TASKS * SPEC:]], 0)
        results.append(jnp.einsum('be,ebh->bh', weights, chosen, precision=highest))
    shared_weights = jax.nn.softmax(jnp.dot(features, shared_gate, precision=highest), axis=-1)
    results.append(jnp.einsum('be,ebh->bh', shared_weights, expert, precision=highest))
    return jnp.stack(results)

def reference(features, cotangent, counts, keep, w_in, in_bias, norm_gain, norm_bias, w_out, out_bias, task_gate, shared_gate):
    blocks = N_DP * N_FSDP
    params = (w_in, in_bias, norm_gain, norm_bias, w_out, out_bias, task_gate, shared_gate)
    feat_blocks = features.reshape(blocks, ROWS_DEV, D)
    cot_blocks = cotangent.reshape(TASKS + 1, blocks, ROWS_DEV, H).transpose(1, 0, 2, 3)
    keep_blocks = keep.reshape(blocks, ROWS_DEV)

    def step_block(carry, block):
        feat, cot, count, flags = block
        valid = ((jnp.arange(ROWS_DEV, dtype=jnp.int32) < count) & (flags > 0)).astype(jnp.float32)
        result, pull = jax.vjp(forward, feat, *params)
        pulled = pull(cot * valid[None, :, None])
        carry = jax.tree.map(jnp.add, carry, tuple(pulled[1:]))
        return (carry, (result, pulled[0]))
    zeros = jax.tree.map(jnp.zeros_like, params)
    grads, (result, grad_feat) = lax.scan(step_block, zeros, (feat_blocks, cot_blocks, counts, keep_blocks))
    outputs = result.transpose(1, 0, 2, 3).reshape(TASKS + 1, ROWS, H)
    grad_features = grad_feat.reshape(ROWS, D)
    return (outputs, grad_features, grads[0], grads[1], grads[2], grads[3], grads[4], grads[5], grads[6], grads[7])
```

```python
import functools

import jax
import jax.numpy as jnp
from jax import lax
from jax.experimental import pallas as pl
from jax.experimental.pallas import tpu as pltpu
from jax.sharding import PartitionSpec as P

TASKS = 2
SPEC = 2
SHARED = 2
EXPERTS = 6
EPSILON = 1e-05
GROUPS = ((0, 1), (2, 3), (4, 5))
TILE = 512
STEP = 16
LANES = 128
GATES = 16
F32 = jnp.float32
BF16 = jnp.bfloat16
VMEM_BYTES = 58 << 20

NN = (((1,), (0,)), ((), ()))
NT = (((1,), (1,)), ((), ()))
TN = (((0,), (0,)), ((), ()))


def uses(expert):
    if expert >= TASKS * SPEC:
        shared = expert - TASKS * SPEC
        first = [(t, t * (SPEC + SHARED) + SPEC + shared) for t in range(TASKS)]
    else:
        t = expert // SPEC
        first = [(t, t * (SPEC + SHARED) + expert % SPEC)]
    return first + [(TASKS, TASKS * (SPEC + SHARED) + expert)]


def halves(v):
    high = v.astype(BF16)
    return high, (v - high.astype(F32)).astype(BF16)


def dot(a, b, dims):
    return lax.dot_general(a, b, dims, preferred_element_type=F32)


def dot3(a_high, a_low, b_high, b_low, dims):
    return dot(a_high, b_high, dims) + dot(a_low, b_high, dims) + dot(a_high, b_low, dims)


def column(row):
    return jnp.broadcast_to(row, (LANES, row.shape[1])).T


def wide(block, width):
    return jnp.concatenate([block] * (width // LANES), axis=1)


def prep_kernel(x_ref, c_ref, valid_ref, xh_ref, xl_ref, ct_ref):
    depth = x_ref.shape[1]
    high, low = halves(x_ref[...].T)
    xh_ref[0:depth] = high
    xh_ref[depth:] = jnp.ones((xh_ref.shape[0] - depth, xh_ref.shape[1]), BF16)
    xl_ref[...] = low
    valid = valid_ref[...]
    for o in range(c_ref.shape[0]):
        ct_ref[o] = c_ref[o].T * valid


def prep(features, cotangent, valid):
    rows, depth = features.shape
    outs, _, units = cotangent.shape
    return pl.pallas_call(
        prep_kernel,
        grid=(rows // TILE,),
        in_specs=[
            pl.BlockSpec((TILE, depth), lambda i: (i, 0)),
            pl.BlockSpec((outs, TILE, units), lambda i: (0, i, 0)),
            pl.BlockSpec((1, TILE), lambda i: (0, i)),
        ],
        out_specs=[
            pl.BlockSpec((depth + STEP, TILE), lambda i: (0, i)),
            pl.BlockSpec((depth, TILE), lambda i: (0, i)),
            pl.BlockSpec((outs, units, TILE), lambda i: (0, 0, i)),
        ],
        out_shape=[
            jax.ShapeDtypeStruct((depth + STEP, rows), BF16),
            jax.ShapeDtypeStruct((depth, rows), BF16),
            jax.ShapeDtypeStruct((outs, units, rows), F32),
        ],
        compiler_params=pltpu.CompilerParams(vmem_limit_bytes=VMEM_BYTES),
        cost_estimate=pl.CostEstimate(flops=0, bytes_accessed=32000000, transcendentals=0),
    )(features, cotangent, valid)


def softmax_rows(v):
    e = jnp.exp(v - jnp.max(v, axis=0, keepdims=True))
    return e / jnp.sum(e, axis=0, keepdims=True)


def expert_kernel(group, first, last, n_in, *refs):
    names = ["core", "own", "other", "small", "xh", "xl", "ct"]
    names += ["gates"] if first else ["prob"]
    if last:
        names += [f"dp{k}" for k in range(len(GROUPS) - 1)]
    names += ["dah", "dal", "ex", "keep", "send", "wih", "wil"]
    if first:
        names += ["prob"]
    names += ["dl", "gate_keep", "gate_send"] if last else ["dp"]
    names += ["win_t", "win_t_low", "wp", "wp_low", "wp_t", "wp_t_low", "b_in", "b_out", "acc_w", "acc_g"]
    names += ["h", "u", "a", "xhat", "h2", "g", "xhh", "xhl", "dzh", "dzl"]
    if last:
        names += ["all_dp", "acc_gate"]
    r = dict(zip(names, refs, strict=True))
    step = pl.program_id(0)
    count = len(group)
    units = r["acc_w"].shape[2]
    depth = r["xl"].shape[0]
    pairs = r["own"].shape[0]
    devices = 2 * pairs
    rows_in, rows_out = depth // devices, units // devices
    rows_all = rows_in + rows_out
    core = r["core"][0]
    tile = r["xl"].shape[1]
    chunks = [slice(k, k + STEP) for k in range(0, units, STEP)]

    @pl.when(step == 0)
    def _():
        for l, e in enumerate(group):
            base = l * rows_all
            for q in range(pairs):
                for src, at in ((r["own"], core), (r["other"], 1 - core)):
                    place = q * 2 + at
                    r["acc_w"][l, pl.ds(place * rows_in, rows_in)] = src[q, base : base + rows_in]
                    r["acc_g"][l, pl.ds(place * rows_out, rows_out)] = src[
                        q, base + rows_in : base + rows_all
                    ]
            w_in = r["acc_w"][l, 0:depth]
            high, low = halves(w_in)
            r["wih"][l] = high
            r["wil"][l] = low
            high, low = halves((0.5 * w_in).T)
            r["win_t"][l, 0:units] = high
            r["win_t_low"][l, 0:units] = low
            w_out = r["acc_g"][l, 0:units]
            b_in, gain, shift, b_out = (r["small"][k * EXPERTS + e : k * EXPERTS + e + 1] for k in range(4))
            scaled = w_out * wide(column(gain), units)
            high, low = halves(scaled)
            r["wp"][l] = high
            r["wp_low"][l] = low
            high, low = halves((0.5 * scaled).T)
            r["wp_t"][l] = high
            r["wp_t_low"][l] = low
            b_out = b_out + jnp.sum(w_out * wide(column(shift), units), axis=0, keepdims=True)
            r["b_in"][l] = column(0.5 * b_in)
            r["b_out"][l] = column(0.5 * b_out)
            r["xhh"][l, units:] = jnp.ones((STEP, tile), BF16)
        if first:
            high, low = halves(r["gates"][...])
            r["win_t"][0, units:] = high
            r["win_t_low"][0, units:] = low
        r["acc_w"][...] = jnp.zeros_like(r["acc_w"])
        r["acc_g"][...] = jnp.zeros_like(r["acc_g"])
        if last:
            r["acc_gate"][...] = jnp.zeros_like(r["acc_gate"])

    stats = {}

    def project_in(l):
        top = units + (GATES if first and l == 0 else 0)
        r["h"][l, 0:top] = dot3(
            r["win_t"][l, 0:top], r["win_t_low"][l, 0:top], r["xh"][0:depth], r["xl"][...], NN
        )

    def gate_weights():
        z = r["h"][0, units:]
        for lower, upper in ((0, 4), (4, 8), (8, 14)):
            r["prob"][lower:upper] = softmax_rows(z[lower:upper])
        r["prob"][14:16] = jnp.zeros((2, tile), F32)

    def normalise(l):
        total = jnp.zeros((STEP, tile), F32)
        for c in chunks:
            h = r["h"][l, c] + wide(r["b_in"][l, c], tile)
            u = 1.0 + jnp.tanh(h)
            a = h * u
            r["u"][l, c] = u
            r["a"][l, c] = a
            total = total + a
        mean = jnp.sum(total, axis=0, keepdims=True) * (1.0 / units)
        total = jnp.zeros((STEP, tile), F32)
        for c in chunks:
            d = r["a"][l, c] - mean
            total = total + d * d
        scale = lax.rsqrt(jnp.sum(total, axis=0, keepdims=True) * (1.0 / units) + EPSILON)
        stats[l] = scale
        for c in chunks:
            x = (r["a"][l, c] - mean) * scale
            r["xhat"][l, c] = x
            r["xhh"][l, c], r["xhl"][l, c] = halves(x)

    def project_out(l):
        r["h2"][l] = dot3(r["wp_t"][l], r["wp_t_low"][l], r["xhh"][l, 0:units], r["xhl"][l], NN)

    def combine(l):
        taken = uses(group[l])
        prob = [0.5 * r["prob"][row : row + 1] for _, row in taken]
        sums = [jnp.zeros((STEP, tile), F32) for _ in taken]
        for c in chunks:
            h = r["h2"][l, c] + wide(r["b_out"][l, c], tile)
            u = 1.0 + jnp.tanh(h)
            ex = h * u
            r["ex"][l * units + c.start : l * units + c.stop] = ex
            slope = u + ex * (2.0 - u)
            d = None
            for k, (o, _) in enumerate(taken):
                cot = r["ct"][o, c]
                sums[k] = sums[k] + cot * ex
                term = prob[k] * cot
                d = term if d is None else d + term
            r["dzh"][l, c], r["dzl"][l, c] = halves(d * slope)
        for k, (_, row) in enumerate(taken):
            value = jnp.sum(sums[k], axis=0, keepdims=True)
            if last:
                r["all_dp"][row : row + 1] = value
            else:
                at = l * len(taken) + k
                r["dp"][at : at + 1] = value

    def back_out(l):
        r["g"][l] = dot3(r["wp"][l], r["wp_low"][l], r["dzh"][l], r["dzl"][l], NN)

    def grad_out(l):
        r["acc_g"][l] += dot(r["xhh"][l], r["dzh"][l], NT) + dot(r["xhh"][l], r["dzl"][l], NT)
        r["acc_g"][l, 0:units] += dot(r["xhl"][l], r["dzh"][l], NT)

    def back_norm(l):
        total, along = jnp.zeros((STEP, tile), F32), jnp.zeros((STEP, tile), F32)
        for c in chunks:
            g = r["g"][l, c]
            total = total + g
            along = along + g * r["xhat"][l, c]
        mean = jnp.sum(total, axis=0, keepdims=True) * (1.0 / units)
        along = jnp.sum(along, axis=0, keepdims=True) * (1.0 / units)
        scale = 0.5 * stats[l]
        for c in chunks:
            u, a = r["u"][l, c], r["a"][l, c]
            slope = (u + a * (2.0 - u)) * scale
            da = (r["g"][l, c] - mean - r["xhat"][l, c] * along) * slope
            at = slice(l * units + c.start, l * units + c.stop)
            r["dah"][at], r["dal"][at] = halves(da)

    def grad_in(l):
        at = slice(l * units, (l + 1) * units)
        r["acc_w"][l] += dot(r["xh"][...], r["dah"][at], NT) + dot(r["xh"][...], r["dal"][at], NT)
        r["acc_w"][l, 0:depth] += dot(r["xl"][...], r["dah"][at], NT)

    project_in(0)
    if first:
        gate_weights()
    for l in range(count):
        if l + 1 < count:
            project_in(l + 1)
        normalise(l)
    for l in range(count):
        project_out(l)
        combine(l)
    for l in range(count):
        back_out(l)
        grad_out(l)
        back_norm(l)
    for l in range(count):
        grad_in(l)

    if last:
        for k, g in enumerate(GROUPS[:-1]):
            at = 0
            for e in g:
                for _, row in uses(e):
                    r["all_dp"][row : row + 1] = r[f"dp{k}"][at : at + 1]
                    at += 1
        for lower, upper in ((0, 4), (4, 8), (8, 14)):
            p, d = r["prob"][lower:upper], r["all_dp"][lower:upper]
            r["dl"][lower:upper] = p * (d - jnp.sum(p * d, axis=0, keepdims=True))
        r["dl"][14:16] = jnp.zeros((2, tile), F32)
        high, low = halves(r["dl"][...])
        r["acc_gate"][...] += (
            dot(r["xh"][0:depth], high, NT) + dot(r["xh"][0:depth], low, NT) + dot(r["xl"][...], high, NT)
        )

    @pl.when(step == pl.num_programs(0) - 1)
    def _():
        for l in range(count):
            base = l * (rows_all + 8)
            tail = jnp.concatenate([r["acc_g"][l, units : units + 1], r["acc_w"][l, depth : depth + 1]], 0)
            tail = jnp.concatenate([tail] * 4, 0)
            for q in range(pairs):
                for dst, at in ((r["keep"], core), (r["send"], 1 - core)):
                    place = q * 2 + at
                    dst[q, base : base + rows_in] = r["acc_w"][l, pl.ds(place * rows_in, rows_in)]
                    dst[q, base + rows_in : base + rows_all] = r["acc_g"][l, pl.ds(place * rows_out, rows_out)]
                    dst[q, base + rows_all : base + rows_all + 8] = tail
        if last:
            for q in range(pairs):
                for dst, at in ((r["gate_keep"], core), (r["gate_send"], 1 - core)):
                    dst[q] = r["acc_gate"][pl.ds((q * 2 + at) * rows_in, rows_in)]


def expert_call(group, core, own, other, small, xh, xl, ct, prob, gates, dps, last):
    first = gates is not None
    pairs, _, units = own.shape
    depth, rows = xl.shape
    devices = 2 * pairs
    rows_in, rows_out = depth // devices, units // devices
    count = len(group)
    whole = lambda shape: pl.BlockSpec(shape, lambda i: (0,) * len(shape))
    along = lambda n: pl.BlockSpec((n, TILE), lambda i: (0, i))
    ins = [core, own, other, small, xh, xl, ct]
    in_specs = [
        pl.BlockSpec(memory_space=pltpu.SMEM),
        whole(own.shape),
        whole(other.shape),
        whole(small.shape),
        along(xh.shape[0]),
        along(depth),
        pl.BlockSpec((ct.shape[0], units, TILE), lambda i: (0, 0, i)),
    ]
    if first:
        ins.append(gates)
        in_specs.append(whole(gates.shape))
    else:
        ins.append(prob)
        in_specs.append(along(GATES))
    if last:
        ins += dps
        in_specs += [along(8)] * len(dps)
    packed = count * (rows_in + rows_out + 8)
    shape = jax.ShapeDtypeStruct
    outs = [
        (along(count * units), shape((count * units, rows), BF16)),
        (along(count * units), shape((count * units, rows), BF16)),
        (along(count * units), shape((count * units, rows), F32)),
        (whole((pairs, packed, units)), shape((pairs, packed, units), F32)),
        (whole((pairs, packed, units)), shape((pairs, packed, units), F32)),
        (whole((count, depth, units)), shape((count, depth, units), BF16)),
        (whole((count, depth, units)), shape((count, depth, units), BF16)),
    ]
    if first:
        outs.append((along(GATES), shape((GATES, rows), F32)))
    if last:
        outs.append((along(GATES), shape((GATES, rows), F32)))
        outs += [(whole((pairs, rows_in, GATES)), shape((pairs, rows_in, GATES), F32))] * 2
    else:
        outs.append((along(8), shape((8, rows), F32)))
    top = units + (GATES if first else 0)
    full = lambda n, t: pltpu.VMEM((count, n, TILE), t)
    scratch = [
        pltpu.VMEM((count, top, depth), BF16),
        pltpu.VMEM((count, top, depth), BF16),
        pltpu.VMEM((count, units, units), BF16),
        pltpu.VMEM((count, units, units), BF16),
        pltpu.VMEM((count, units, units), BF16),
        pltpu.VMEM((count, units, units), BF16),
        pltpu.VMEM((count, units, LANES), F32),
        pltpu.VMEM((count, units, LANES), F32),
        pltpu.VMEM((count, depth + STEP, units), F32),
        pltpu.VMEM((count, units + STEP, units), F32),
        full(top, F32),
        full(units, F32),
        full(units, F32),
        full(units, F32),
        full(units, F32),
        full(units, F32),
        full(units + STEP, BF16),
        full(units, BF16),
        full(units, BF16),
        full(units, BF16),
    ]
    if last:
        scratch += [pltpu.VMEM((GATES, TILE), F32), pltpu.VMEM((depth, GATES), F32)]
    return pl.pallas_call(
        functools.partial(expert_kernel, group, first, last, len(ins)),
        grid=(rows // TILE,),
        in_specs=in_specs,
        out_specs=[o[0] for o in outs],
        out_shape=[o[1] for o in outs],
        scratch_shapes=scratch,
        compiler_params=pltpu.CompilerParams(vmem_limit_bytes=VMEM_BYTES),
        cost_estimate=pl.CostEstimate(
            flops=20000000000 * count // 2, bytes_accessed=30000000, transcendentals=0
        ),
    )(*ins)


def final_kernel(*refs):
    n = len(GROUPS)
    dahs, dals, exs, wihs, wils = (refs[k * n : (k + 1) * n] for k in range(5))
    prob_ref, dl_ref, gates_ref, out_ref, gf_ref, gate_ref = refs[5 * n :]
    units = out_ref.shape[2]

    @pl.when(pl.program_id(0) == 0)
    def _():
        high, low = halves(gates_ref[...])
        gate_ref[0:GATES] = high
        gate_ref[GATES : 2 * GATES] = low
        gate_ref[2 * GATES :] = high

    high, low = halves(dl_ref[...])
    total = dot(gate_ref[...], jnp.concatenate([high, high, low], 0), TN)
    for k, group in enumerate(GROUPS):
        for l in range(len(group)):
            at = slice(l * units, (l + 1) * units)
            total = total + dot3(wihs[k][l], wils[k][l], dahs[k][at], dals[k][at], NN)
    gf_ref[...] = total.T
    sums = [None] * (TASKS + 1)
    for k, group in enumerate(GROUPS):
        for l, e in enumerate(group):
            ex = exs[k][l * units : (l + 1) * units]
            for o, row in uses(e):
                term = prob_ref[row : row + 1] * ex
                sums[o] = term if sums[o] is None else sums[o] + term
    for o in range(TASKS + 1):
        out_ref[o] = sums[o].T


def final_call(dahs, dals, exs, wihs, wils, prob, dl, gates):
    rows = prob.shape[1]
    _, depth, units = wihs[0].shape
    whole = lambda a: pl.BlockSpec(a.shape, lambda i: (0,) * a.ndim)
    along = lambda a: pl.BlockSpec((a.shape[0], TILE), lambda i: (0, i))
    return pl.pallas_call(
        final_kernel,
        grid=(rows // TILE,),
        in_specs=[along(a) for a in (*dahs, *dals, *exs)]
        + [whole(a) for a in (*wihs, *wils)]
        + [along(prob), along(dl), whole(gates)],
        out_specs=[
            pl.BlockSpec((TASKS + 1, TILE, units), lambda i: (0, i, 0)),
            pl.BlockSpec((TILE, depth), lambda i: (i, 0)),
        ],
        out_shape=[
            jax.ShapeDtypeStruct((TASKS + 1, rows, units), F32),
            jax.ShapeDtypeStruct((rows, depth), F32),
        ],
        scratch_shapes=[pltpu.VMEM((3 * GATES, depth), BF16)],
        compiler_params=pltpu.CompilerParams(vmem_limit_bytes=VMEM_BYTES),
        cost_estimate=pl.CostEstimate(flops=15000000000, bytes_accessed=50000000, transcendentals=0),
    )(*dahs, *dals, *exs, *wihs, *wils, prob, dl, gates)


def local(features, cotangent, valid, core, owns, others, small, gates):
    xh, xl, ct = prep(features, cotangent, valid)
    prob, dps = None, []
    kept, sent, dahs, dals, exs, wihs, wils = [], [], [], [], [], [], []
    for k, group in enumerate(GROUPS):
        last = k == len(GROUPS) - 1
        got = expert_call(
            group, core, owns[k], others[k], small, xh, xl, ct, prob, None if k else gates, dps, last
        )
        dah, dal, ex, keep, send, wih, wil = got[:7]
        rest = list(got[7:])
        if k == 0:
            prob = rest.pop(0)
        kept.append([keep])
        sent.append([send])
        if last:
            dl = rest[0]
            kept[-1].append(rest[1])
            sent[-1].append(rest[2])
        else:
            dps.append(rest[0])
        for to, what in ((dahs, dah), (dals, dal), (exs, ex), (wihs, wih), (wils, wil)):
            to.append(what)
    outputs, grad_features = final_call(dahs, dals, exs, wihs, wils, prob, dl, gates)
    return outputs, grad_features, kept, sent


def make(mesh):
    n_fsdp, n_dp = mesh.shape["fsdp"], mesh.shape["dp"]
    pairs = n_fsdp // 2
    across = [[q * 2 + c for q in range(pairs)] for c in range(2)]
    twin = [(i, i ^ 1) for i in range(n_fsdp)]

    def gather(x):
        spread = jnp.broadcast_to(x[None], (pairs, *x.shape))
        own = lax.all_to_all(spread, "fsdp", 0, 0, axis_index_groups=across)
        return own, lax.ppermute(own, "fsdp", twin)

    def scatter(keep, send):
        got = keep + lax.ppermute(send, "fsdp", twin)
        return jnp.sum(lax.all_to_all(got, "fsdp", 0, 0, axis_index_groups=across), 0)

    def replicas(x):
        bit = 1
        while bit < n_dp:
            x = x + lax.ppermute(x, "dp", [(i, i ^ bit) for i in range(n_dp)])
            bit *= 2
        return x

    def on_device(
        features, cotangent, counts, keep, w_in, in_bias, norm_gain, norm_bias, w_out, out_bias, task_gate, shared_gate
    ):
        rows = features.shape[0]
        depth = features.shape[1]
        experts, rows_in, units = w_in.shape
        rows_out = w_out.shape[1]
        valid = (lax.broadcasted_iota(jnp.int32, (1, rows), 1) < counts[0]) & (keep.reshape(1, rows) > 0)
        me = lax.axis_index("fsdp")
        core = (me % 2).astype(jnp.int32).reshape(1)
        biases = jnp.concatenate([in_bias, norm_gain, norm_bias, out_bias], 0)
        gate = jnp.concatenate([task_gate[0].T, task_gate[1].T, shared_gate.T], 0)
        gate = jnp.pad(gate, ((0, GATES - gate.shape[0]), (0, units - rows_in)))
        extra = jnp.concatenate([jnp.pad(biases, ((0, 0), (0, units - rows_out))), gate], 0)
        owns, others = [], []
        for k, group in enumerate(GROUPS):
            parts = []
            for e in group:
                parts += [w_in[e], w_out[e]]
            if k == 0:
                parts.append(extra)
            own, other = gather(jnp.concatenate(parts, 0))
            owns.append(own)
            others.append(other)
        begin = len(GROUPS[0]) * (rows_in + rows_out)
        mine, theirs = owns[0][:, begin:], others[0][:, begin:]
        both = jnp.where(core[0] == 0, jnp.stack([mine, theirs], 1), jnp.stack([theirs, mine], 1))
        both = both.reshape(n_fsdp, *both.shape[2:])
        n_bias = biases.shape[0]
        small = both[:, :n_bias, :rows_out].transpose(1, 0, 2).reshape(n_bias, units)
        gates = both[:, n_bias:, :rows_in].transpose(1, 0, 2).reshape(GATES, depth)

        outputs, grad_features, kept, sent = local(
            features, cotangent, valid.astype(F32), core, owns, others, small, gates
        )

        g_in, g_in_bias, g_gain, g_shift, g_out, g_out_bias = [], [], [], [], [], []
        for k, group in enumerate(GROUPS):
            total = replicas(scatter(kept[k][0], sent[k][0]))
            for l, e in enumerate(group):
                base = l * (rows_in + rows_out + 8)
                g_in.append(total[base : base + rows_in])
                raw = total[base + rows_in : base + rows_in + rows_out]
                tail = total[base + rows_in + rows_out :]
                column_sum = tail[0]
                g_in_bias.append(lax.dynamic_slice(tail[1], (me * rows_out,), (rows_out,)))
                g_out_bias.append(lax.dynamic_slice(column_sum, (me * rows_out,), (rows_out,)))
                g_out.append(norm_gain[e][:, None] * raw + norm_bias[e][:, None] * column_sum[None])
                g_gain.append(jnp.sum(w_out[e] * raw, 1))
                g_shift.append(jnp.sum(w_out[e] * column_sum[None], 1))
        gate_sum = replicas(scatter(kept[-1][1], sent[-1][1]))
        n_task = SPEC + SHARED
        g_task = jnp.stack([gate_sum[:, t * n_task : (t + 1) * n_task] for t in range(TASKS)])
        g_shared = gate_sum[:, TASKS * n_task : TASKS * n_task + EXPERTS]
        return (
            outputs,
            grad_features,
            jnp.stack(g_in),
            jnp.stack(g_in_bias),
            jnp.stack(g_gain),
            jnp.stack(g_shift),
            jnp.stack(g_out),
            jnp.stack(g_out_bias),
            g_task,
            g_shared,
        )

    return on_device


def solution(mesh):
    placed = (
        P(("dp", "fsdp"), None),
        P(None, ("dp", "fsdp"), None),
        P(("dp", "fsdp")),
        P(("dp", "fsdp")),
        P(None, "fsdp", None),
        P(None, "fsdp"),
        P(None, "fsdp"),
        P(None, "fsdp"),
        P(None, "fsdp", None),
        P(None, "fsdp"),
        P(None, "fsdp", None),
        P("fsdp", None),
    )
    return jax.shard_map(
        make(mesh),
        mesh=mesh,
        in_specs=placed,
        out_specs=(
            P(None, ("dp", "fsdp"), None),
            P(("dp", "fsdp"), None),
            P(None, "fsdp", None),
            P(None, "fsdp"),
            P(None, "fsdp"),
            P(None, "fsdp"),
            P(None, "fsdp", None),
            P(None, "fsdp"),
            P(None, "fsdp", None),
            P("fsdp", None),
        ),
        check_vma=False,
    )
```

```python
import functools

import jax
import jax.numpy as jnp
from jax import lax
from jax.experimental import pallas as pl
from jax.experimental.pallas import tpu as pltpu
from jax.sharding import PartitionSpec as P

TASKS = 2
SPEC = 2
SHARED = 2
EXPERTS = 6
EPSILON = 1e-05
GROUPS = ((0, 1), (2, 3), (4, 5))
TILE = 512
STEP = 16
LANES = 128
GATES = 16
F32 = jnp.float32
BF16 = jnp.bfloat16
VMEM_BYTES = 58 << 20

NN = (((1,), (0,)), ((), ()))
NT = (((1,), (1,)), ((), ()))
TN = (((0,), (0,)), ((), ()))


def uses(expert):
    if expert >= TASKS * SPEC:
        shared = expert - TASKS * SPEC
        first = [(t, t * (SPEC + SHARED) + SPEC + shared) for t in range(TASKS)]
    else:
        t = expert // SPEC
        first = [(t, t * (SPEC + SHARED) + expert % SPEC)]
    return first + [(TASKS, TASKS * (SPEC + SHARED) + expert)]


def halves(v):
    high = v.astype(BF16)
    return high, (v - high.astype(F32)).astype(BF16)


def dot(a, b, dims):
    return lax.dot_general(a, b, dims, preferred_element_type=F32)


def dot3(a_high, a_low, b_high, b_low, dims):
    return dot(a_high, b_high, dims) + dot(a_low, b_high, dims) + dot(a_high, b_low, dims)


def column(row):
    return jnp.broadcast_to(row, (LANES, row.shape[1])).T


def wide(block, width):
    return jnp.concatenate([block] * (width // LANES), axis=1)


def tie(x, after):
    return pl.pallas_call(
        lambda *refs: None,
        in_specs=[pl.BlockSpec(memory_space=pl.ANY)] * (1 + len(after)),
        out_specs=pl.BlockSpec(memory_space=pl.ANY),
        out_shape=jax.ShapeDtypeStruct(x.shape, x.dtype),
        input_output_aliases={0: 0},
    )(x, *after)


def pack_weights(groups, w_in_ref, w_out_ref, to_ref):
    rows_in, rows_out = w_in_ref.shape[1], w_out_ref.shape[1]
    at = 0
    for e in (e for group in groups for e in group):
        for q in range(to_ref.shape[0]):
            to_ref[q, at : at + rows_in] = w_in_ref[e]
            to_ref[q, at + rows_in : at + rows_in + rows_out] = w_out_ref[e]
        at += rows_in + rows_out
    return at


def pack_kernel(in_bias, gain, shift, out_bias, task_gate, shared_gate, w_in_ref, w_out_ref, to_ref):
    rows_in, rows_out = w_in_ref.shape[1], w_out_ref.shape[1]
    at = pack_weights(GROUPS[:1], w_in_ref, w_out_ref, to_ref)
    n = SPEC + SHARED
    for q in range(to_ref.shape[0]):
        to_ref[q, at:] = jnp.zeros((to_ref.shape[1] - at, to_ref.shape[2]), F32)
        for k, bias in enumerate((in_bias, gain, shift, out_bias)):
            to_ref[q, at + k * EXPERTS : at + (k + 1) * EXPERTS, 0:rows_out] = bias[...]
        base = at + 4 * EXPERTS
        for t in range(TASKS):
            to_ref[q, base + t * n : base + (t + 1) * n, 0:rows_in] = task_gate[t]
        base += TASKS * n
        to_ref[q, base : base + EXPERTS, 0:rows_in] = shared_gate[...]


def pack(pairs, w_in, in_bias, gain, shift, w_out, out_bias, task_gate, shared_gate):
    rows = len(GROUPS[0]) * (w_in.shape[1] + w_out.shape[1]) + 4 * EXPERTS + GATES
    return pl.pallas_call(
        pack_kernel,
        out_shape=jax.ShapeDtypeStruct((pairs, rows, w_in.shape[2]), F32),
        compiler_params=pltpu.CompilerParams(vmem_limit_bytes=VMEM_BYTES),
    )(in_bias, gain, shift, out_bias, task_gate.transpose(0, 2, 1), shared_gate.T, w_in, w_out)


def prep_kernel(x_ref, c_ref, valid_ref, w_in_ref, w_out_ref, xh_ref, xl_ref, ct_ref, to_ref):
    depth = x_ref.shape[1]

    @pl.when(pl.program_id(0) == 0)
    def _():
        pack_weights(GROUPS[1:], w_in_ref, w_out_ref, to_ref)

    high, low = halves(x_ref[...].T)
    xh_ref[0:depth] = high
    xh_ref[depth:] = jnp.ones((xh_ref.shape[0] - depth, xh_ref.shape[1]), BF16)
    xl_ref[...] = low
    valid = valid_ref[...]
    for o in range(c_ref.shape[0]):
        ct_ref[o] = c_ref[o].T * valid


def prep(features, cotangent, valid, w_in, w_out, pairs):
    rows, depth = features.shape
    packed = sum(len(g) for g in GROUPS[1:]) * (w_in.shape[1] + w_out.shape[1])
    outs, _, units = cotangent.shape
    return pl.pallas_call(
        prep_kernel,
        grid=(rows // TILE,),
        in_specs=[
            pl.BlockSpec((TILE, depth), lambda i: (i, 0)),
            pl.BlockSpec((outs, TILE, units), lambda i: (0, i, 0)),
            pl.BlockSpec((1, TILE), lambda i: (0, i)),
            pl.BlockSpec(w_in.shape, lambda i: (0, 0, 0)),
            pl.BlockSpec(w_out.shape, lambda i: (0, 0, 0)),
        ],
        out_specs=[
            pl.BlockSpec((depth + STEP, TILE), lambda i: (0, i)),
            pl.BlockSpec((depth, TILE), lambda i: (0, i)),
            pl.BlockSpec((outs, units, TILE), lambda i: (0, 0, i)),
            pl.BlockSpec((pairs, packed, units), lambda i: (0, 0, 0)),
        ],
        out_shape=[
            jax.ShapeDtypeStruct((depth + STEP, rows), BF16),
            jax.ShapeDtypeStruct((depth, rows), BF16),
            jax.ShapeDtypeStruct((outs, units, rows), F32),
            jax.ShapeDtypeStruct((pairs, packed, units), F32),
        ],
        compiler_params=pltpu.CompilerParams(vmem_limit_bytes=VMEM_BYTES),
        cost_estimate=pl.CostEstimate(flops=0, bytes_accessed=32000000, transcendentals=0),
    )(features, cotangent, valid, w_in, w_out)


def softmax_rows(v):
    e = jnp.exp(v - jnp.max(v, axis=0, keepdims=True))
    return e / jnp.sum(e, axis=0, keepdims=True)


def expert_kernel(group, first, last, n_after, skip_rows, *refs):
    names = ["core", "own", "other", "small", "xh", "xl", "ct"]
    names += ["gates"] if first else ["prob"]
    if last:
        names += [f"dp{k}" for k in range(len(GROUPS) - 1)]
    names += [f"after{k}" for k in range(n_after)]
    names += ["dah", "dal", "ex", "wih", "wil"]
    names += ["keep", "send"] if last else ["grads"]
    if first:
        names += ["prob"]
    names += ["dl"] if last else ["dp"]
    names += ["win_t", "win_t_low", "wp", "wp_low", "wp_t", "wp_t_low", "b_in", "b_out", "acc_w", "acc_g"]
    names += ["h", "u", "a", "xhat", "h2", "g", "xhh", "xhl", "dzh", "dzl"]
    if last:
        names += ["all_dp", "acc_gate"]
    r = dict(zip(names, refs, strict=True))
    step = pl.program_id(0)
    count = len(group)
    units = r["acc_w"].shape[2]
    depth = r["xl"].shape[0]
    pairs = r["own"].shape[0]
    devices = 2 * pairs
    rows_in, rows_out = depth // devices, units // devices
    rows_all = rows_in + rows_out
    core = r["core"][0]
    skip = skip_rows * rows_all
    tile = r["xl"].shape[1]
    chunks = [slice(k, k + STEP) for k in range(0, units, STEP)]

    @pl.when(step == 0)
    def _():
        for l, e in enumerate(group):
            base = (e - group[0]) * rows_all + skip
            for q in range(pairs):
                for src, at in ((r["own"], core), (r["other"], 1 - core)):
                    place = q * 2 + at
                    r["acc_w"][l, pl.ds(place * rows_in, rows_in)] = src[q, base : base + rows_in]
                    r["acc_g"][l, pl.ds(place * rows_out, rows_out)] = src[
                        q, base + rows_in : base + rows_all
                    ]
            w_in = r["acc_w"][l, 0:depth]
            high, low = halves(w_in)
            r["wih"][l] = high
            r["wil"][l] = low
            high, low = halves((0.5 * w_in).T)
            r["win_t"][l, 0:units] = high
            r["win_t_low"][l, 0:units] = low
            w_out = r["acc_g"][l, 0:units]
            b_in, gain, shift, b_out = (r["small"][k * EXPERTS + e : k * EXPERTS + e + 1] for k in range(4))
            scaled = w_out * wide(column(gain), units)
            high, low = halves(scaled)
            r["wp"][l] = high
            r["wp_low"][l] = low
            high, low = halves((0.5 * scaled).T)
            r["wp_t"][l] = high
            r["wp_t_low"][l] = low
            b_out = b_out + jnp.sum(w_out * wide(column(shift), units), axis=0, keepdims=True)
            r["b_in"][l] = column(0.5 * b_in)
            r["b_out"][l] = column(0.5 * b_out)
            r["xhh"][l, units:] = jnp.ones((STEP, tile), BF16)
        if first:
            high, low = halves(r["gates"][...])
            r["win_t"][0, units:] = high
            r["win_t_low"][0, units:] = low
        r["acc_w"][...] = jnp.zeros_like(r["acc_w"])
        r["acc_g"][...] = jnp.zeros_like(r["acc_g"])
        if last:
            r["acc_gate"][...] = jnp.zeros_like(r["acc_gate"])

    stats = {}

    def project_in(l):
        top = units + (GATES if first and l == 0 else 0)
        r["h"][l, 0:top] = dot3(
            r["win_t"][l, 0:top], r["win_t_low"][l, 0:top], r["xh"][0:depth], r["xl"][...], NN
        )

    def gate_weights():
        z = r["h"][0, units:]
        for lower, upper in ((0, 4), (4, 8), (8, 14)):
            r["prob"][lower:upper] = softmax_rows(z[lower:upper])
        r["prob"][14:16] = jnp.zeros((2, tile), F32)

    def normalise(l):
        total = jnp.zeros((STEP, tile), F32)
        for c in chunks:
            h = r["h"][l, c] + wide(r["b_in"][l, c], tile)
            u = 1.0 + jnp.tanh(h)
            a = h * u
            r["u"][l, c] = u
            r["a"][l, c] = a
            total = total + a
        mean = jnp.sum(total, axis=0, keepdims=True) * (1.0 / units)
        total = jnp.zeros((STEP, tile), F32)
        for c in chunks:
            d = r["a"][l, c] - mean
            total = total + d * d
        scale = lax.rsqrt(jnp.sum(total, axis=0, keepdims=True) * (1.0 / units) + EPSILON)
        stats[l] = scale
        for c in chunks:
            x = (r["a"][l, c] - mean) * scale
            r["xhat"][l, c] = x
            r["xhh"][l, c], r["xhl"][l, c] = halves(x)

    def project_out(l):
        r["h2"][l] = dot3(r["wp_t"][l], r["wp_t_low"][l], r["xhh"][l, 0:units], r["xhl"][l], NN)

    def combine(l):
        taken = uses(group[l])
        prob = [0.5 * r["prob"][row : row + 1] for _, row in taken]
        sums = [jnp.zeros((STEP, tile), F32) for _ in taken]
        for c in chunks:
            h = r["h2"][l, c] + wide(r["b_out"][l, c], tile)
            u = 1.0 + jnp.tanh(h)
            ex = h * u
            r["ex"][l * units + c.start : l * units + c.stop] = ex
            slope = u + ex * (2.0 - u)
            d = None
            for k, (o, _) in enumerate(taken):
                cot = r["ct"][o, c]
                sums[k] = sums[k] + cot * ex
                term = prob[k] * cot
                d = term if d is None else d + term
            r["dzh"][l, c], r["dzl"][l, c] = halves(d * slope)
        for k, (_, row) in enumerate(taken):
            value = jnp.sum(sums[k], axis=0, keepdims=True)
            if last:
                r["all_dp"][row : row + 1] = value
            else:
                at = l * len(taken) + k
                r["dp"][at : at + 1] = value

    def back_out(l):
        r["g"][l] = dot3(r["wp"][l], r["wp_low"][l], r["dzh"][l], r["dzl"][l], NN)

    def grad_out(l):
        r["acc_g"][l] += dot(r["xhh"][l], r["dzh"][l], NT) + dot(r["xhh"][l], r["dzl"][l], NT)
        r["acc_g"][l, 0:units] += dot(r["xhl"][l], r["dzh"][l], NT)

    def back_norm(l):
        total, along = jnp.zeros((STEP, tile), F32), jnp.zeros((STEP, tile), F32)
        for c in chunks:
            g = r["g"][l, c]
            total = total + g
            along = along + g * r["xhat"][l, c]
        mean = jnp.sum(total, axis=0, keepdims=True) * (1.0 / units)
        along = jnp.sum(along, axis=0, keepdims=True) * (1.0 / units)
        scale = 0.5 * stats[l]
        for c in chunks:
            u, a = r["u"][l, c], r["a"][l, c]
            slope = (u + a * (2.0 - u)) * scale
            da = (r["g"][l, c] - mean - r["xhat"][l, c] * along) * slope
            at = slice(l * units + c.start, l * units + c.stop)
            r["dah"][at], r["dal"][at] = halves(da)

    def grad_in(l):
        at = slice(l * units, (l + 1) * units)
        r["acc_w"][l] += dot(r["xh"][...], r["dah"][at], NT) + dot(r["xh"][...], r["dal"][at], NT)
        r["acc_w"][l, 0:depth] += dot(r["xl"][...], r["dah"][at], NT)

    project_in(0)
    if first:
        gate_weights()
    for l in range(count):
        if l + 1 < count:
            project_in(l + 1)
        normalise(l)
    for l in range(count):
        project_out(l)
        combine(l)
    for l in range(count):
        back_out(l)
        grad_out(l)
        back_norm(l)
    for l in range(count):
        grad_in(l)

    if last:
        for k, g in enumerate(GROUPS[:-1]):
            at = 0
            for e in g:
                for _, row in uses(e):
                    r["all_dp"][row : row + 1] = r[f"dp{k}"][at : at + 1]
                    at += 1
        for lower, upper in ((0, 4), (4, 8), (8, 14)):
            p, d = r["prob"][lower:upper], r["all_dp"][lower:upper]
            r["dl"][lower:upper] = p * (d - jnp.sum(p * d, axis=0, keepdims=True))
        r["dl"][14:16] = jnp.zeros((2, tile), F32)
        high, low = halves(r["dl"][...])
        r["acc_gate"][:, 0:GATES] += (
            dot(r["xh"][0:depth], high, NT) + dot(r["xh"][0:depth], low, NT) + dot(r["xl"][...], high, NT)
        )

    @pl.when(step == pl.num_programs(0) - 1)
    def _():
        for l in range(count):
            base = l * (rows_all + 8)
            tail = jnp.concatenate([r["acc_g"][l, units : units + 1], r["acc_w"][l, depth : depth + 1]], 0)
            tail = jnp.concatenate([tail] * 4, 0)
            if last:
                places = [
                    (dst, q, q * 2 + at)
                    for q in range(pairs)
                    for dst, at in ((r["keep"], core), (r["send"], 1 - core))
                ]
            else:
                places = [(r["grads"], k, k) for k in range(devices)]
            for dst, q, place in places:
                dst[q, base : base + rows_in] = r["acc_w"][l, pl.ds(place * rows_in, rows_in)]
                dst[q, base + rows_in : base + rows_all] = r["acc_g"][l, pl.ds(place * rows_out, rows_out)]
                dst[q, base + rows_all : base + rows_all + 8] = tail
        if last:
            gate = r["acc_gate"][...].T[0:GATES]
            base = count * (rows_all + 8)
            for q in range(pairs):
                even = gate[:, 2 * q * rows_in : (2 * q + 1) * rows_in]
                odd = gate[:, (2 * q + 1) * rows_in : (2 * q + 2) * rows_in]
                for dst, at in ((r["keep"], core), (r["send"], 1 - core)):
                    dst[q, base:, 0:rows_in] = jnp.where(at == 0, even, odd)


def expert_call(group, core, own, other, small, xh, xl, ct, prob, gates, dps, last, after, skip):
    first = gates is not None
    pairs, _, units = own.shape
    depth, rows = xl.shape
    devices = 2 * pairs
    rows_in, rows_out = depth // devices, units // devices
    count = len(group)
    whole = lambda shape: pl.BlockSpec(shape, lambda i: (0,) * len(shape))
    along = lambda n: pl.BlockSpec((n, TILE), lambda i: (0, i))
    ins = [core, own, other, small, xh, xl, ct]
    in_specs = [
        pl.BlockSpec(memory_space=pltpu.SMEM),
        whole(own.shape),
        whole(other.shape),
        whole(small.shape),
        along(xh.shape[0]),
        along(depth),
        pl.BlockSpec((ct.shape[0], units, TILE), lambda i: (0, 0, i)),
    ]
    if first:
        ins.append(gates)
        in_specs.append(whole(gates.shape))
    else:
        ins.append(prob)
        in_specs.append(along(GATES))
    if last:
        ins += dps
        in_specs += [along(8)] * len(dps)
    ins += after
    in_specs += [pl.BlockSpec(memory_space=pl.ANY)] * len(after)
    packed = count * (rows_in + rows_out + 8)
    shape = jax.ShapeDtypeStruct
    outs = [
        (along(count * units), shape((count * units, rows), BF16)),
        (along(count * units), shape((count * units, rows), BF16)),
        (along(count * units), shape((count * units, rows), F32)),
        (whole((count, depth, units)), shape((count, depth, units), BF16)),
        (whole((count, depth, units)), shape((count, depth, units), BF16)),
    ]
    if last:
        packed += GATES
        outs += [(whole((pairs, packed, units)), shape((pairs, packed, units), F32))] * 2
    else:
        outs.append((whole((devices, packed, units)), shape((devices, packed, units), F32)))
    if first:
        outs.append((along(GATES), shape((GATES, rows), F32)))
    if last:
        outs.append((along(GATES), shape((GATES, rows), F32)))
    else:
        outs.append((along(8), shape((8, rows), F32)))
    top = units + (GATES if first else 0)
    full = lambda n, t: pltpu.VMEM((count, n, TILE), t)
    scratch = [
        pltpu.VMEM((count, top, depth), BF16),
        pltpu.VMEM((count, top, depth), BF16),
        pltpu.VMEM((count, units, units), BF16),
        pltpu.VMEM((count, units, units), BF16),
        pltpu.VMEM((count, units, units), BF16),
        pltpu.VMEM((count, units, units), BF16),
        pltpu.VMEM((count, units, LANES), F32),
        pltpu.VMEM((count, units, LANES), F32),
        pltpu.VMEM((count, depth + STEP, units), F32),
        pltpu.VMEM((count, units + STEP, units), F32),
        full(top, F32),
        full(units, F32),
        full(units, F32),
        full(units, F32),
        full(units, F32),
        full(units, F32),
        full(units + STEP, BF16),
        full(units, BF16),
        full(units, BF16),
        full(units, BF16),
    ]
    if last:
        scratch += [pltpu.VMEM((GATES, TILE), F32), pltpu.VMEM((depth, LANES), F32)]
    return pl.pallas_call(
        functools.partial(expert_kernel, group, first, last, len(after), skip),
        grid=(rows // TILE,),
        in_specs=in_specs,
        out_specs=[o[0] for o in outs],
        out_shape=[o[1] for o in outs],
        scratch_shapes=scratch,
        compiler_params=pltpu.CompilerParams(vmem_limit_bytes=VMEM_BYTES),
        cost_estimate=pl.CostEstimate(
            flops=20000000000 * count // 2, bytes_accessed=30000000, transcendentals=0
        ),
    )(*ins)


def final_kernel(*refs):
    n = len(GROUPS)
    dahs, dals, exs, wihs, wils = (refs[k * n : (k + 1) * n] for k in range(5))
    prob_ref, dl_ref, gates_ref = refs[5 * n : 5 * n + 3]
    out_ref, gf_ref, gate_ref = refs[-3:]
    units = out_ref.shape[2]

    @pl.when(pl.program_id(0) == 0)
    def _():
        high, low = halves(gates_ref[...])
        gate_ref[0:GATES] = high
        gate_ref[GATES : 2 * GATES] = low
        gate_ref[2 * GATES :] = high

    high, low = halves(dl_ref[...])
    total = dot(gate_ref[...], jnp.concatenate([high, high, low], 0), TN)
    for k, group in enumerate(GROUPS):
        for l in range(len(group)):
            at = slice(l * units, (l + 1) * units)
            total = total + dot3(wihs[k][l], wils[k][l], dahs[k][at], dals[k][at], NN)
    gf_ref[...] = total.T
    sums = [None] * (TASKS + 1)
    for k, group in enumerate(GROUPS):
        for l, e in enumerate(group):
            ex = exs[k][l * units : (l + 1) * units]
            for o, row in uses(e):
                term = prob_ref[row : row + 1] * ex
                sums[o] = term if sums[o] is None else sums[o] + term
    for o in range(TASKS + 1):
        out_ref[o] = sums[o].T


def final_call(dahs, dals, exs, wihs, wils, prob, dl, gates, part, parts, before, after):
    rows = prob.shape[1]
    _, depth, units = wihs[0].shape
    steps = rows // TILE // parts
    skip = part * steps
    whole = lambda a: pl.BlockSpec(a.shape, lambda i: (0,) * a.ndim)
    along = lambda a: pl.BlockSpec((a.shape[0], TILE), lambda i: (0, i + skip))
    ins = [*dahs, *dals, *exs, *wihs, *wils, prob, dl, gates, *before, *after]
    n = 5 * len(GROUPS) + 3
    return pl.pallas_call(
        final_kernel,
        grid=(steps,),
        in_specs=[along(a) for a in (*dahs, *dals, *exs)]
        + [whole(a) for a in (*wihs, *wils)]
        + [along(prob), along(dl), whole(gates)]
        + [pl.BlockSpec(memory_space=pl.ANY)] * (len(before) + len(after)),
        out_specs=[
            pl.BlockSpec((TASKS + 1, TILE, units), lambda i: (0, i + skip, 0)),
            pl.BlockSpec((TILE, depth), lambda i: (i + skip, 0)),
        ],
        out_shape=[
            jax.ShapeDtypeStruct((TASKS + 1, rows, units), F32),
            jax.ShapeDtypeStruct((rows, depth), F32),
        ],
        scratch_shapes=[pltpu.VMEM((3 * GATES, depth), BF16)],
        input_output_aliases={n + k: k for k in range(len(before))},
        compiler_params=pltpu.CompilerParams(vmem_limit_bytes=VMEM_BYTES),
        cost_estimate=pl.CostEstimate(
            flops=15000000000 // parts, bytes_accessed=50000000 // parts, transcendentals=0
        ),
    )(*ins)


def finish_kernel(me_ref, *refs):
    n = len(GROUPS)
    halves_of = refs[: 2 * n]
    w_out_ref, gain_ref, shift_ref = refs[2 * n : 2 * n + 3]
    g_in, g_in_bias, g_gain, g_shift, g_out, g_out_bias, g_task, g_shared = refs[2 * n + 3 :]
    rows_in, rows_out, units = g_in.shape[1], g_out.shape[1], g_in.shape[2]
    me = me_ref[0]

    def own(row):
        value = row[:, 0:rows_out]
        for p in range(1, units // rows_out):
            value = jnp.where(me == p, row[:, p * rows_out : (p + 1) * rows_out], value)
        return value

    def as_row(col):
        return jnp.broadcast_to(col, (rows_out, LANES)).T[0:1]

    for k, group in enumerate(GROUPS):
        a, b = halves_of[2 * k], halves_of[2 * k + 1]
        add = lambda lower, upper: a[lower:upper] + b[lower:upper]
        at = 0
        for e in group:
            g_in[e] = add(at, at + rows_in)
            at += rows_in
            raw = add(at, at + rows_out)
            at += rows_out
            tail = add(at, at + 8)
            at += 8
            total = tail[0:1]
            gain = wide(column(gain_ref[e : e + 1]), units)
            shift = wide(column(shift_ref[e : e + 1]), units)
            g_out[e] = gain * raw + shift * total
            w = w_out_ref[e]
            g_gain[e : e + 1] = as_row(jnp.sum(w * raw, axis=1, keepdims=True))
            g_shift[e : e + 1] = as_row(jnp.sum(w * total, axis=1, keepdims=True))
            g_in_bias[e : e + 1] = own(tail[1:2])
            g_out_bias[e : e + 1] = own(total)
    gate = add(at, at + GATES)[:, 0:rows_in]
    m = SPEC + SHARED
    for t in range(TASKS):
        g_task[t] = gate[t * m : (t + 1) * m]
    g_shared[...] = gate[TASKS * m : TASKS * m + EXPERTS]


def finish(me, totals, w_in, w_out, gain, shift):
    experts, rows_in, units = w_in.shape
    rows_out = w_out.shape[1]
    shape = lambda *s: jax.ShapeDtypeStruct(s, F32)
    vector = shape(experts, rows_out)
    outs = [
        shape(*w_in.shape),
        vector,
        vector,
        vector,
        shape(*w_out.shape),
        vector,
        shape(TASKS, SPEC + SHARED, rows_in),
        shape(EXPERTS, rows_in),
    ]
    vmem = pl.BlockSpec(memory_space=pltpu.VMEM)
    got = pl.pallas_call(
        finish_kernel,
        in_specs=[pl.BlockSpec(memory_space=pltpu.SMEM)] + [vmem] * (len(totals) + 3),
        out_specs=[vmem] * len(outs),
        out_shape=outs,
        compiler_params=pltpu.CompilerParams(vmem_limit_bytes=VMEM_BYTES),
    )(me, *totals, w_out, gain, shift)
    return (*got[:6], got[6].transpose(0, 2, 1), got[7].T)


def make(mesh):
    n_fsdp, n_dp = mesh.shape["fsdp"], mesh.shape["dp"]
    pairs = n_fsdp // 2
    across = [[q * 2 + c for q in range(pairs)] for c in range(2)]
    twin = [(i, i ^ 1) for i in range(n_fsdp)]

    def spread_out(x):
        return lax.all_to_all(x, "fsdp", 0, 0, axis_index_groups=across)

    def swap(x, bit):
        return lax.ppermute(x, "dp", [(i, i ^ bit) for i in range(n_dp)])

    def reduce_some(x, some, beside):
        for bit in some:
            x = x + tie(swap(x, bit), beside)
        return x

    bits = [1 << k for k in range(n_dp.bit_length() - 1)]

    def on_device(
        features, cotangent, counts, keep, w_in, in_bias, norm_gain, norm_bias, w_out, out_bias, task_gate, shared_gate
    ):
        rows = features.shape[0]
        depth = features.shape[1]
        experts, rows_in, units = w_in.shape
        rows_out = w_out.shape[1]
        valid = (lax.broadcasted_iota(jnp.int32, (1, rows), 1) < counts[0]) & (keep.reshape(1, rows) > 0)
        me = lax.axis_index("fsdp")
        core = (me % 2).astype(jnp.int32).reshape(1)
        xh, xl, ct, spread = prep(features, cotangent, valid.astype(F32), w_in, w_out, pairs)
        own0 = tie(
            spread_out(
                pack(pairs, w_in, in_bias, norm_gain, norm_bias, w_out, out_bias, task_gate, shared_gate)
            ),
            [xh],
        )
        other0 = lax.ppermute(own0, "fsdp", twin)
        begin = len(GROUPS[0]) * (rows_in + rows_out)
        mine, theirs = own0[:, begin:], other0[:, begin:]
        both = jnp.where(core[0] == 0, jnp.stack([mine, theirs], 1), jnp.stack([theirs, mine], 1))
        both = both.reshape(n_fsdp, *both.shape[2:])
        n_bias = 4 * EXPERTS
        small = both[:, :n_bias, :rows_out].transpose(1, 0, 2).reshape(n_bias, units)
        gates = both[:, n_bias:, :rows_in].transpose(1, 0, 2).reshape(GATES, depth)

        first = expert_call(GROUPS[0], core, own0, other0, small, xh, xl, ct, None, gates, [], False, [], 0)
        prob = first[6]
        own1 = tie(spread_out(spread), [first[7]])
        other1 = lax.ppermute(own1, "fsdp", twin)
        second = expert_call(GROUPS[1], core, own1, other1, small, xh, xl, ct, prob, None, [], False, [], 0)
        sum0 = jnp.sum(tie(lax.all_to_all(first[5], "fsdp", 0, 0), [second[6]]), 0)
        third = expert_call(
            GROUPS[2], core, own1, other1, small, xh, xl, ct, prob, None, [first[7], second[6]], True, [sum0], len(GROUPS[1])
        )
        dl = third[7]
        sum1 = jnp.sum(tie(lax.all_to_all(second[5], "fsdp", 0, 0), [dl]), 0)
        sum0 = reduce_some(sum0, bits[:-1], [dl])
        dahs, dals, exs, wihs, wils = zip(first[:5], second[:5], third[:5])
        kept = third[5] + lax.ppermute(tie(third[6], [sum0, sum1]), "fsdp", twin)
        part = final_call(dahs, dals, exs, wihs, wils, prob, dl, gates, 0, 2, [], [])
        sum2 = jnp.sum(tie(spread_out(kept), [part[1]]), 0)
        pair0 = (sum0, tie(swap(sum0, bits[-1]), [part[1]]))
        sum1 = reduce_some(sum1, bits[:-1], [part[1]])
        outputs, grad_features = final_call(
            dahs, dals, exs, wihs, wils, prob, dl, gates, 1, 2, part, [pair0[1], sum1, sum2]
        )
        pair1 = (sum1, tie(swap(sum1, bits[-1]), [grad_features]))
        sum2 = tie(reduce_some(sum2, bits[:-1], [grad_features]), [pair1[1]])
        pair2 = (sum2, swap(sum2, bits[-1]))
        rest = finish(me.astype(jnp.int32).reshape(1), (*pair0, *pair1, *pair2), w_in, w_out, norm_gain, norm_bias)
        return (outputs, grad_features, *rest)

    return on_device


def solution(mesh):
    placed = (
        P(("dp", "fsdp"), None),
        P(None, ("dp", "fsdp"), None),
        P(("dp", "fsdp")),
        P(("dp", "fsdp")),
        P(None, "fsdp", None),
        P(None, "fsdp"),
        P(None, "fsdp"),
        P(None, "fsdp"),
        P(None, "fsdp", None),
        P(None, "fsdp"),
        P(None, "fsdp", None),
        P("fsdp", None),
    )
    return jax.shard_map(
        make(mesh),
        mesh=mesh,
        in_specs=placed,
        out_specs=(
            P(None, ("dp", "fsdp"), None),
            P(("dp", "fsdp"), None),
            P(None, "fsdp", None),
            P(None, "fsdp"),
            P(None, "fsdp"),
            P(None, "fsdp"),
            P(None, "fsdp", None),
            P(None, "fsdp"),
            P(None, "fsdp", None),
            P("fsdp", None),
        ),
        check_vma=False,
    )
```

```python
import functools

import jax
import jax.numpy as jnp
from jax import lax
from jax.experimental import pallas as pl
from jax.experimental.pallas import tpu as pltpu
from jax.sharding import PartitionSpec as P

TASKS = 2
SPEC = 2
SHARED = 2
EXPERTS = 6
EPSILON = 1e-05
GROUPS = ((0, 1), (2, 3), (4, 5))
TILE = 512
STEP = 16
TOKEN = (8, 128)
SPAN = 256
ORDER = (('in', 0), ('in', 1), ('norm', 0), ('in', 2), ('norm', 1), ('in', 3), ('out', 0), ('norm', 2), ('out', 1), ('norm', 3), ('comb', 0), ('out', 2), ('comb', 1), ('out', 3), ('back', 0), ('comb', 2), ('back', 1), ('comb', 3), ('go', 0), ('bnorm', 0), ('back', 2), ('bnorm', 1), ('back', 3), ('gi', 0), ('bnorm', 2), ('go', 1), ('bnorm', 3), ('gi', 1))
LANES = 128
GATES = 16
F32 = jnp.float32
BF16 = jnp.bfloat16
VMEM_BYTES = 58 << 20

NN = (((1,), (0,)), ((), ()))
NT = (((1,), (1,)), ((), ()))
TN = (((0,), (0,)), ((), ()))


def uses(expert):
    if expert >= TASKS * SPEC:
        shared = expert - TASKS * SPEC
        first = [(t, t * (SPEC + SHARED) + SPEC + shared) for t in range(TASKS)]
    else:
        t = expert // SPEC
        first = [(t, t * (SPEC + SHARED) + expert % SPEC)]
    return first + [(TASKS, TASKS * (SPEC + SHARED) + expert)]


def halves(v):
    high = v.astype(BF16)
    return high, (v - high.astype(F32)).astype(BF16)


def dot(a, b, dims):
    return lax.dot_general(a, b, dims, preferred_element_type=F32)


def dot3(a_high, a_low, b_high, b_low, dims):
    return dot(a_high, b_high, dims) + dot(a_low, b_high, dims) + dot(a_high, b_low, dims)


def column(row):
    return jnp.broadcast_to(row, (LANES, row.shape[1])).T


def wide(block, width):
    return jnp.concatenate([block] * (width // LANES), axis=1)


def tie(x, after):
    return pl.pallas_call(
        lambda *refs: None,
        in_specs=[pl.BlockSpec(memory_space=pl.ANY)] + [pl.BlockSpec(memory_space=pltpu.HBM)] * len(after),
        out_specs=pl.BlockSpec(memory_space=pl.ANY),
        out_shape=jax.ShapeDtypeStruct(x.shape, x.dtype),
        input_output_aliases={0: 0},
    )(x, *after)


def total_kernel(n, *refs):
    value = None
    for ref in refs[:n]:
        for part in [ref[...]] if len(ref.shape) == 2 else [ref[k] for k in range(ref.shape[0])]:
            value = part if value is None else value + part
    refs[-2][...] = value
    refs[-1][...] = jnp.zeros_like(refs[-1])


def total(arrays, after):
    vmem = pl.BlockSpec(memory_space=pltpu.VMEM)
    return pl.pallas_call(
        functools.partial(total_kernel, len(arrays)),
        in_specs=[vmem] * len(arrays) + [pl.BlockSpec(memory_space=pltpu.HBM)] * len(after),
        out_specs=[vmem, vmem],
        out_shape=[jax.ShapeDtypeStruct(arrays[0].shape[-2:], F32), jax.ShapeDtypeStruct(TOKEN, F32)],
        compiler_params=pltpu.CompilerParams(vmem_limit_bytes=16 << 20),
    )(*arrays, *after)


def pack_weights(groups, w_in_ref, w_out_ref, to_ref):
    rows_in, rows_out = w_in_ref.shape[1], w_out_ref.shape[1]
    at = 0
    for e in (e for group in groups for e in group):
        for q in range(to_ref.shape[0]):
            to_ref[q, at : at + rows_in] = w_in_ref[e]
            to_ref[q, at + rows_in : at + rows_in + rows_out] = w_out_ref[e]
        at += rows_in + rows_out
    return at


def pack_kernel(in_bias, gain, shift, out_bias, task_gate, shared_gate, w_in_ref, w_out_ref, to_ref):
    rows_in, rows_out = w_in_ref.shape[1], w_out_ref.shape[1]
    at = pack_weights(GROUPS[:1], w_in_ref, w_out_ref, to_ref)
    n = SPEC + SHARED
    for q in range(to_ref.shape[0]):
        to_ref[q, at:] = jnp.zeros((to_ref.shape[1] - at, to_ref.shape[2]), F32)
        for k, bias in enumerate((in_bias, gain, shift, out_bias)):
            to_ref[q, at + k * EXPERTS : at + (k + 1) * EXPERTS, 0:rows_out] = bias[...]
        base = at + 4 * EXPERTS
        for t in range(TASKS):
            to_ref[q, base + t * n : base + (t + 1) * n, 0:rows_in] = task_gate[t]
        base += TASKS * n
        to_ref[q, base : base + EXPERTS, 0:rows_in] = shared_gate[...]


def pack(pairs, w_in, in_bias, gain, shift, w_out, out_bias, task_gate, shared_gate):
    rows = len(GROUPS[0]) * (w_in.shape[1] + w_out.shape[1]) + 4 * EXPERTS + GATES
    return pl.pallas_call(
        pack_kernel,
        out_shape=jax.ShapeDtypeStruct((pairs, rows, w_in.shape[2]), F32),
        compiler_params=pltpu.CompilerParams(vmem_limit_bytes=VMEM_BYTES),
    )(in_bias, gain, shift, out_bias, task_gate.transpose(0, 2, 1), shared_gate.T, w_in, w_out)


def prep_kernel(x_ref, c_ref, valid_ref, w_in_ref, w_out_ref, xh_ref, xl_ref, ct_ref, to_ref, done_ref):
    depth = x_ref.shape[1]

    @pl.when(pl.program_id(0) == 0)
    def _():
        pack_weights(GROUPS[1:], w_in_ref, w_out_ref, to_ref)
        done_ref[...] = jnp.zeros_like(done_ref)

    high, low = halves(x_ref[...].T)
    xh_ref[0:depth] = high
    xh_ref[depth:] = jnp.ones((xh_ref.shape[0] - depth, xh_ref.shape[1]), BF16)
    xl_ref[...] = low
    valid = valid_ref[...]
    for o in range(c_ref.shape[0]):
        ct_ref[o] = c_ref[o].T * valid


def prep(features, cotangent, valid, w_in, w_out, pairs):
    rows, depth = features.shape
    packed = sum(len(g) for g in GROUPS[1:]) * (w_in.shape[1] + w_out.shape[1])
    outs, _, units = cotangent.shape
    return pl.pallas_call(
        prep_kernel,
        grid=(rows // TILE,),
        in_specs=[
            pl.BlockSpec((TILE, depth), lambda i: (i, 0)),
            pl.BlockSpec((outs, TILE, units), lambda i: (0, i, 0)),
            pl.BlockSpec((1, TILE), lambda i: (0, i)),
            pl.BlockSpec(w_in.shape, lambda i: (0, 0, 0)),
            pl.BlockSpec(w_out.shape, lambda i: (0, 0, 0)),
        ],
        out_specs=[
            pl.BlockSpec((depth + STEP, TILE), lambda i: (0, i)),
            pl.BlockSpec((depth, TILE), lambda i: (0, i)),
            pl.BlockSpec((outs, units, TILE), lambda i: (0, 0, i)),
            pl.BlockSpec((pairs, packed, units), lambda i: (0, 0, 0)),
            pl.BlockSpec(TOKEN, lambda i: (0, 0)),
        ],
        out_shape=[
            jax.ShapeDtypeStruct((depth + STEP, rows), BF16),
            jax.ShapeDtypeStruct((depth, rows), BF16),
            jax.ShapeDtypeStruct((outs, units, rows), F32),
            jax.ShapeDtypeStruct((pairs, packed, units), F32),
            jax.ShapeDtypeStruct(TOKEN, F32),
        ],
        compiler_params=pltpu.CompilerParams(vmem_limit_bytes=VMEM_BYTES),
        cost_estimate=pl.CostEstimate(flops=0, bytes_accessed=32000000, transcendentals=0),
    )(features, cotangent, valid, w_in, w_out)


def softmax_rows(v):
    e = jnp.exp(v - jnp.max(v, axis=0, keepdims=True))
    return e / jnp.sum(e, axis=0, keepdims=True)


def expert_kernel(group, first, last, n_after, partial, *refs):
    used = sorted({o for e in group for o, _ in uses(e)})
    names = ["core", "own", "other", "small", "xh", "xl"]
    names += [f"c{o}" for o in used]
    names += ["gates"] if first else ["prob"]
    if last:
        names += [f"dp{k}" for k in range(len(GROUPS) - 1)]
    names += [f"in{o}" for o in partial]
    names += [f"after{k}" for k in range(n_after)]
    names += [f"{name}{l}" for name in ("dah", "dal") for l in range(len(group))]
    names += ["out"] if last else [f"out{o}" for o in used]
    names += ["wih", "wil"]
    names += ["keep", "send"] if last else ["grads"]
    if first:
        names += ["prob"]
    names += ["dl"] if last else ["dp"]
    names += ["done"]
    each = ["win_t", "win_t_low", "wp", "wp_low", "wp_t", "wp_t_low", "b_in", "b_out", "acc_w", "acc_g"]
    each += ["h", "u", "a", "xhat", "h2", "g", "ex", "xhh", "xhl", "dzh", "dzl"]
    names += [f"{name}{l}" for name in each for l in range(len(group))]
    if last:
        names += ["all_dp", "acc_gate"] + [f"mix{o}" for o in used]
    r = dict(zip(names, refs, strict=True))
    for name in (*each, "dah", "dal"):
        r[name] = [r[f"{name}{l}"] for l in range(len(group))]
    step = pl.program_id(0)
    count = len(group)
    units = r["acc_w"][0].shape[1]
    depth = r["xl"].shape[0]
    pairs = r["own"].shape[0]
    devices = 2 * pairs
    rows_in, rows_out = depth // devices, units // devices
    rows_all = rows_in + rows_out
    core = r["core"][0]
    tile = r["xl"].shape[1]
    chunks = [slice(k, k + STEP) for k in range(0, units, STEP)]

    @pl.when(step == 0)
    def _():
        for l, e in enumerate(group):
            base = l * rows_all
            for q in range(pairs):
                for src, at in ((r["own"], core), (r["other"], 1 - core)):
                    place = q * 2 + at
                    r["acc_w"][l][pl.ds(place * rows_in, rows_in)] = src[q, base : base + rows_in]
                    r["acc_g"][l][pl.ds(place * rows_out, rows_out)] = src[
                        q, base + rows_in : base + rows_all
                    ]
            w_in = r["acc_w"][l][0:depth]
            high, low = halves(w_in)
            r["wih"][l] = high
            r["wil"][l] = low
            high, low = halves((0.5 * w_in).T)
            r["win_t"][l][0:units] = high
            r["win_t_low"][l][0:units] = low
            w_out = r["acc_g"][l][0:units]
            b_in, gain, shift, b_out = (r["small"][k * EXPERTS + e : k * EXPERTS + e + 1] for k in range(4))
            scaled = w_out * wide(column(gain), units)
            high, low = halves(scaled)
            r["wp"][l][...] = high
            r["wp_low"][l][...] = low
            high, low = halves((0.5 * scaled).T)
            r["wp_t"][l][...] = high
            r["wp_t_low"][l][...] = low
            b_out = b_out + jnp.sum(w_out * wide(column(shift), units), axis=0, keepdims=True)
            r["b_in"][l][...] = column(0.5 * b_in)
            r["b_out"][l][...] = column(0.5 * b_out)
            r["xhh"][l][units:] = jnp.ones((STEP, tile), BF16)
        if first:
            high, low = halves(r["gates"][...])
            r["win_t"][0][units:] = high
            r["win_t_low"][0][units:] = low
        for l in range(count):
            r["acc_w"][l][...] = jnp.zeros_like(r["acc_w"][l])
            r["acc_g"][l][...] = jnp.zeros_like(r["acc_g"][l])
        r["done"][...] = jnp.zeros_like(r["done"])
        if last:
            r["acc_gate"][...] = jnp.zeros_like(r["acc_gate"])

    stats = {}

    spans = [slice(k, k + SPAN) for k in range(0, tile, SPAN)]
    zero = jnp.zeros((STEP, SPAN), F32)

    def project_in(l, s):
        top = units + (GATES if first and l == 0 else 0)
        r["h"][l][0:top, s] = dot3(
            r["win_t"][l][0:top], r["win_t_low"][l][0:top], r["xh"][0:depth, s], r["xl"][:, s], NN
        )

    def gate_weights(s):
        z = r["h"][0][units:, s]
        for lower, upper in ((0, 4), (4, 8), (8, 14)):
            r["prob"][lower:upper, s] = softmax_rows(z[lower:upper])
        r["prob"][14:16, s] = jnp.zeros((2, SPAN), F32)

    def normalise(l, s):
        total = zero
        for c in chunks:
            h = r["h"][l][c, s] + wide(r["b_in"][l][c], SPAN)
            u = 1.0 + jnp.tanh(h)
            a = h * u
            r["u"][l][c, s] = u
            r["a"][l][c, s] = a
            total = total + a
        mean = jnp.sum(total, axis=0, keepdims=True) * (1.0 / units)
        total = zero
        for c in chunks:
            d = r["a"][l][c, s] - mean
            total = total + d * d
        scale = lax.rsqrt(jnp.sum(total, axis=0, keepdims=True) * (1.0 / units) + EPSILON)
        stats[l, s.start] = scale
        for c in chunks:
            x = (r["a"][l][c, s] - mean) * scale
            r["xhat"][l][c, s] = x
            r["xhh"][l][c, s], r["xhl"][l][c, s] = halves(x)

    def project_out(l, s):
        r["h2"][l][:, s] = dot3(
            r["wp_t"][l][...], r["wp_t_low"][l][...], r["xhh"][l][0:units, s], r["xhl"][l][:, s], NN
        )

    def combine(l, s):
        taken = uses(group[l])
        prob = [0.5 * r["prob"][row : row + 1, s] for _, row in taken]
        sums = [zero for _ in taken]
        end = l == count - 1
        full = [[r["prob"][row : row + 1, s] for _, row in uses(e)] for e in group] if end else None
        for c in chunks:
            h = r["h2"][l][c, s] + wide(r["b_out"][l][c], SPAN)
            u = 1.0 + jnp.tanh(h)
            ex = h * u
            if not end:
                r["ex"][l][c, s] = ex
            slope = u + ex * (2.0 - u)
            d = None
            for k, (o, _) in enumerate(taken):
                cot = r[f"c{o}"][0, c, s]
                sums[k] = sums[k] + cot * ex
                term = prob[k] * cot
                d = term if d is None else d + term
                if end:
                    mix = full[l][k] * ex
                    for m in range(l):
                        mix = mix + full[m][k] * r["ex"][m][c, s]
                    if o in partial:
                        mix = mix + r[f"in{o}"][c, s]
                    if last:
                        r[f"mix{o}"][c, s] = mix
                    else:
                        r[f"out{o}"][c, s] = mix
            r["dzh"][l][c, s], r["dzl"][l][c, s] = halves(d * slope)
        for k, (_, row) in enumerate(taken):
            value = jnp.sum(sums[k], axis=0, keepdims=True)
            if last:
                r["all_dp"][row : row + 1, s] = value
            else:
                at = l * len(taken) + k
                r["dp"][at : at + 1, s] = value

    def back_out(l, s):
        r["g"][l][:, s] = dot3(
            r["wp"][l][...], r["wp_low"][l][...], r["dzh"][l][:, s], r["dzl"][l][:, s], NN
        )

    def grad_out(l):
        r["acc_g"][l][...] += dot(r["xhh"][l][...], r["dzh"][l][...], NT) + dot(
            r["xhh"][l][...], r["dzl"][l][...], NT
        )
        r["acc_g"][l][0:units] += dot(r["xhl"][l][...], r["dzh"][l][...], NT)

    def back_norm(l, s):
        total, along = zero, zero
        for c in chunks:
            g = r["g"][l][c, s]
            total = total + g
            along = along + g * r["xhat"][l][c, s]
        mean = jnp.sum(total, axis=0, keepdims=True) * (1.0 / units)
        along = jnp.sum(along, axis=0, keepdims=True) * (1.0 / units)
        scale = 0.5 * stats[l, s.start]
        for c in chunks:
            u, a = r["u"][l][c, s], r["a"][l][c, s]
            slope = (u + a * (2.0 - u)) * scale
            da = (r["g"][l][c, s] - mean - r["xhat"][l][c, s] * along) * slope
            r["dah"][l][c, s], r["dal"][l][c, s] = halves(da)

    def grad_in(l):
        high, low = r["dah"][l][...], r["dal"][l][...]
        r["acc_w"][l][...] += dot(r["xh"][...], high, NT) + dot(r["xh"][...], low, NT)
        r["acc_w"][l][0:depth] += dot(r["xl"][...], high, NT)

    chains = [(l, s) for l in range(count) for s in spans]
    for stage in ORDER:
        if isinstance(stage, tuple):
            name, k = stage
            if name == "go":
                grad_out(k)
            elif name == "gi":
                grad_in(k)
            else:
                at = {
                    "in": project_in, "norm": normalise, "out": project_out, "comb": combine, "back": back_out,
                    "bnorm": back_norm,
                }[name]
                at(*chains[k])
                if name == "in" and first and chains[k][0] == 0:
                    gate_weights(chains[k][1])

    if last:
        for o in used:
            r["out"][o] = r[f"mix{o}"][...].T
    if last:
        for k, g in enumerate(GROUPS[:-1]):
            at = 0
            for e in g:
                for _, row in uses(e):
                    r["all_dp"][row : row + 1] = r[f"dp{k}"][at : at + 1]
                    at += 1
        for lower, upper in ((0, 4), (4, 8), (8, 14)):
            p, d = r["prob"][lower:upper], r["all_dp"][lower:upper]
            r["dl"][lower:upper] = p * (d - jnp.sum(p * d, axis=0, keepdims=True))
        r["dl"][14:16] = jnp.zeros((2, tile), F32)
        high, low = halves(r["dl"][...])
        r["acc_gate"][:, 0:GATES] += (
            dot(r["xh"][0:depth], high, NT) + dot(r["xh"][0:depth], low, NT) + dot(r["xl"][...], high, NT)
        )

    @pl.when(step == pl.num_programs(0) - 1)
    def _():
        for l in range(count):
            base = l * (rows_all + 8)
            tail = jnp.concatenate([r["acc_g"][l][units : units + 1], r["acc_w"][l][depth : depth + 1]], 0)
            tail = jnp.concatenate([tail] * 4, 0)
            if last:
                places = [
                    (dst, q, q * 2 + at)
                    for q in range(pairs)
                    for dst, at in ((r["keep"], core), (r["send"], 1 - core))
                ]
            else:
                places = [(r["grads"], k, k) for k in range(devices)]
            for dst, q, place in places:
                dst[q, base : base + rows_in] = r["acc_w"][l][pl.ds(place * rows_in, rows_in)]
                dst[q, base + rows_in : base + rows_all] = r["acc_g"][l][pl.ds(place * rows_out, rows_out)]
                dst[q, base + rows_all : base + rows_all + 8] = tail
        if last:
            gate = r["acc_gate"][...].T[0:GATES]
            base = count * (rows_all + 8)
            for q in range(pairs):
                even = gate[:, 2 * q * rows_in : (2 * q + 1) * rows_in]
                odd = gate[:, (2 * q + 1) * rows_in : (2 * q + 2) * rows_in]
                for dst, at in ((r["keep"], core), (r["send"], 1 - core)):
                    dst[q, base:, 0:rows_in] = jnp.where(at == 0, even, odd)


def expert_call(group, core, own, other, small, xh, xl, ct, prob, gates, dps, last, after, skip, mixed):
    first = gates is not None
    pairs, _, units = own.shape
    depth, rows = xl.shape
    devices = 2 * pairs
    rows_in, rows_out = depth // devices, units // devices
    count = len(group)
    whole = lambda shape: pl.BlockSpec(shape, lambda i: (0,) * len(shape))
    along = lambda n: pl.BlockSpec((n, TILE), lambda i: (0, i))
    used = sorted({o for e in group for o, _ in uses(e)})
    ins = [core, own, other, small, xh, xl] + [ct] * len(used)
    held = own.shape[1] if first else count * (rows_in + rows_out)
    weights = pl.BlockSpec((pairs, held, units), lambda i: (0, skip, 0))
    in_specs = [
        pl.BlockSpec(memory_space=pltpu.SMEM),
        weights,
        weights,
        whole(small.shape),
        along(xh.shape[0]),
        along(depth),
    ]
    in_specs += [pl.BlockSpec((1, units, TILE), lambda i, o=o: (o, 0, i)) for o in used]
    if first:
        ins.append(gates)
        in_specs.append(whole(gates.shape))
    else:
        ins.append(prob)
        in_specs.append(along(GATES))
    if last:
        ins += dps
        in_specs += [along(8)] * len(dps)
    ins += [mixed[o] for o in sorted(mixed)]
    in_specs += [along(units)] * len(mixed)
    ins += after
    in_specs += [pl.BlockSpec(memory_space=pltpu.HBM)] * len(after)
    packed = count * (rows_in + rows_out + 8)
    shape = jax.ShapeDtypeStruct
    if last:
        mixes = [
            (pl.BlockSpec((len(used), TILE, units), lambda i: (0, i, 0)), shape((len(used), rows, units), F32))
        ]
    else:
        mixes = [(along(units), shape((units, rows), F32))] * len(used)
    outs = [
        *[(along(units), shape((units, rows), BF16))] * (2 * count),
        *mixes,
        (whole((count, depth, units)), shape((count, depth, units), BF16)),
        (whole((count, depth, units)), shape((count, depth, units), BF16)),
    ]
    if last:
        packed += GATES
        outs += [(whole((pairs, packed, units)), shape((pairs, packed, units), F32))] * 2
    else:
        outs.append((whole((devices, packed, units)), shape((devices, packed, units), F32)))
    if first:
        outs.append((along(GATES), shape((GATES, rows), F32)))
    if last:
        outs.append((along(GATES), shape((GATES, rows), F32)))
    else:
        outs.append((along(8), shape((8, rows), F32)))
    outs.append((whole(TOKEN), shape(TOKEN, F32)))
    top = units + (GATES if first else 0)
    kinds = [
        ((top, depth), BF16),
        ((top, depth), BF16),
        ((units, units), BF16),
        ((units, units), BF16),
        ((units, units), BF16),
        ((units, units), BF16),
        ((units, LANES), F32),
        ((units, LANES), F32),
        ((depth + STEP, units), F32),
        ((units + STEP, units), F32),
        ((top, TILE), F32),
        ((units, TILE), F32),
        ((units, TILE), F32),
        ((units, TILE), F32),
        ((units, TILE), F32),
        ((units, TILE), F32),
        ((units, TILE), F32),
        ((units + STEP, TILE), BF16),
        ((units, TILE), BF16),
        ((units, TILE), BF16),
        ((units, TILE), BF16),
    ]
    scratch = [pltpu.VMEM(*kind) for kind in kinds for _ in group]
    if last:
        scratch += [pltpu.VMEM((GATES, TILE), F32), pltpu.VMEM((depth, LANES), F32)]
        scratch += [pltpu.VMEM((units, TILE), F32)] * len(used)
    return pl.pallas_call(
        functools.partial(expert_kernel, group, first, last, len(after), tuple(sorted(mixed))),
        grid=(rows // TILE,),
        in_specs=in_specs,
        out_specs=[o[0] for o in outs],
        out_shape=[o[1] for o in outs],
        scratch_shapes=scratch,
        compiler_params=pltpu.CompilerParams(vmem_limit_bytes=VMEM_BYTES),
        cost_estimate=pl.CostEstimate(
            flops=20000000000 * count // 2, bytes_accessed=30000000, transcendentals=0
        ),
    )(*ins)


def final_kernel(steps, *refs):
    n = EXPERTS
    dahs, dals = refs[:n], refs[n : 2 * n]
    wihs, wils = refs[2 * n : 2 * n + len(GROUPS)], refs[2 * n + len(GROUPS) : 2 * n + 2 * len(GROUPS)]
    dl_ref, gates_ref = refs[2 * n + 2 * len(GROUPS) : 2 * n + 2 * len(GROUPS) + 2]
    gf_ref, done_ref, gate_ref = refs[-3:]
    done_ref[...] = jnp.zeros_like(done_ref)

    @pl.when(pl.program_id(0) == 0)
    def _():
        high, low = halves(gates_ref[...])
        gate_ref[0:GATES] = high
        gate_ref[GATES : 2 * GATES] = low
        gate_ref[2 * GATES :] = high

    high, low = halves(dl_ref[...])
    total = dot(gate_ref[...], jnp.concatenate([high, high, low], 0), TN)
    at = 0
    for k, group in enumerate(GROUPS):
        for l in range(len(group)):
            total = total + dot3(wihs[k][l], wils[k][l], dahs[at][...], dals[at][...], NN)
            at += 1
    gf_ref[...] = total.T


def final_call(dahs, dals, wihs, wils, dl, gates, part, parts, before, after):
    rows = dl.shape[1]
    _, depth, units = wihs[0].shape
    steps = rows // TILE // parts
    skip = part * steps
    whole = lambda a: pl.BlockSpec(a.shape, lambda i: (0,) * a.ndim)
    along = lambda a: pl.BlockSpec((a.shape[0], TILE), lambda i: (0, i + skip))
    ins = [*dahs, *dals, *wihs, *wils, dl, gates, *before, *after]
    n = 2 * EXPERTS + 2 * len(GROUPS) + 2
    return pl.pallas_call(
        functools.partial(final_kernel, steps),
        grid=(steps,),
        in_specs=[along(a) for a in (*dahs, *dals)]
        + [whole(a) for a in (*wihs, *wils)]
        + [along(dl), whole(gates)]
        + [pl.BlockSpec(memory_space=pltpu.HBM)] * (len(before) + len(after)),
        out_specs=[pl.BlockSpec((TILE, depth), lambda i: (i + skip, 0)), pl.BlockSpec(TOKEN, lambda i: (0, 0))],
        out_shape=[jax.ShapeDtypeStruct((rows, depth), F32), jax.ShapeDtypeStruct(TOKEN, F32)],
        scratch_shapes=[pltpu.VMEM((3 * GATES, depth), BF16)],
        input_output_aliases={n + k: k for k in range(len(before))},
        compiler_params=pltpu.CompilerParams(vmem_limit_bytes=VMEM_BYTES),
        cost_estimate=pl.CostEstimate(
            flops=15000000000 // parts, bytes_accessed=25000000 // parts, transcendentals=0
        ),
    )(*ins)


def finish_kernel(me_ref, *refs):
    n = len(GROUPS) + 1
    w_out_ref, gain_ref, shift_ref = refs[n : n + 3]
    g_in, g_in_bias, g_gain, g_shift, g_out, g_out_bias, g_task, g_shared = refs[n + 3 :]
    rows_in, rows_out, units = g_in.shape[1], g_out.shape[1], g_in.shape[2]
    me = me_ref[0]

    def own(row):
        value = row[:, 0:rows_out]
        for p in range(1, units // rows_out):
            value = jnp.where(me == p, row[:, p * rows_out : (p + 1) * rows_out], value)
        return value

    def as_row(col):
        return jnp.broadcast_to(col, (rows_out, LANES)).T[0:1]

    for k, group in enumerate(GROUPS):
        if k < len(GROUPS) - 1:
            add = lambda lower, upper, a=refs[k]: a[lower:upper]
        else:
            add = lambda lower, upper, a=refs[k], b=refs[k + 1]: a[lower:upper] + b[lower:upper]
        at = 0
        for e in group:
            g_in[e] = add(at, at + rows_in)
            at += rows_in
            raw = add(at, at + rows_out)
            at += rows_out
            tail = add(at, at + 8)
            at += 8
            total = tail[0:1]
            gain = wide(column(gain_ref[e : e + 1]), units)
            shift = wide(column(shift_ref[e : e + 1]), units)
            g_out[e] = gain * raw + shift * total
            w = w_out_ref[e]
            g_gain[e : e + 1] = as_row(jnp.sum(w * raw, axis=1, keepdims=True))
            g_shift[e : e + 1] = as_row(jnp.sum(w * total, axis=1, keepdims=True))
            g_in_bias[e : e + 1] = own(tail[1:2])
            g_out_bias[e : e + 1] = own(total)
    gate = add(at, at + GATES)[:, 0:rows_in]
    m = SPEC + SHARED
    for t in range(TASKS):
        g_task[t] = gate[t * m : (t + 1) * m]
    g_shared[...] = gate[TASKS * m : TASKS * m + EXPERTS]


def finish(me, totals, w_in, w_out, gain, shift):
    experts, rows_in, units = w_in.shape
    rows_out = w_out.shape[1]
    shape = lambda *s: jax.ShapeDtypeStruct(s, F32)
    vector = shape(experts, rows_out)
    outs = [
        shape(*w_in.shape),
        vector,
        vector,
        vector,
        shape(*w_out.shape),
        vector,
        shape(TASKS, SPEC + SHARED, rows_in),
        shape(EXPERTS, rows_in),
    ]
    vmem = pl.BlockSpec(memory_space=pltpu.VMEM)
    got = pl.pallas_call(
        finish_kernel,
        in_specs=[pl.BlockSpec(memory_space=pltpu.SMEM)] + [vmem] * (len(totals) + 3),
        out_specs=[vmem] * len(outs),
        out_shape=outs,
        compiler_params=pltpu.CompilerParams(vmem_limit_bytes=VMEM_BYTES),
    )(me, *totals, w_out, gain, shift)
    return (*got[:6], got[6].transpose(0, 2, 1), got[7].T)


def make(mesh):
    n_fsdp, n_dp = mesh.shape["fsdp"], mesh.shape["dp"]
    pairs = n_fsdp // 2
    across = [[q * 2 + c for q in range(pairs)] for c in range(2)]
    twin = [(i, i ^ 1) for i in range(n_fsdp)]

    def spread_out(x):
        return lax.all_to_all(x, "fsdp", 0, 0, axis_index_groups=across)

    def swap(x, bit):
        return lax.ppermute(x, "dp", [(i, i ^ bit) for i in range(n_dp)])

    def reduce_some(x, token, some, beside):
        for bit in some:
            x, token = total([x, swap(x, bit)], beside)
        return x, token

    bits = [1 << k for k in range(n_dp.bit_length() - 1)]

    def on_device(
        features, cotangent, counts, keep, w_in, in_bias, norm_gain, norm_bias, w_out, out_bias, task_gate, shared_gate
    ):
        rows = features.shape[0]
        depth = features.shape[1]
        experts, rows_in, units = w_in.shape
        rows_out = w_out.shape[1]
        valid = (lax.broadcasted_iota(jnp.int32, (1, rows), 1) < counts[0]) & (keep.reshape(1, rows) > 0)
        me = lax.axis_index("fsdp")
        core = (me % 2).astype(jnp.int32).reshape(1)
        xh, xl, ct, spread, done = prep(features, cotangent, valid.astype(F32), w_in, w_out, pairs)
        own0 = tie(
            spread_out(
                pack(pairs, w_in, in_bias, norm_gain, norm_bias, w_out, out_bias, task_gate, shared_gate)
            ),
            [done],
        )
        other0 = lax.ppermute(own0, "fsdp", twin)
        begin = len(GROUPS[0]) * (rows_in + rows_out)
        mine, theirs = own0[:, begin:], other0[:, begin:]
        both = jnp.where(core[0] == 0, jnp.stack([mine, theirs], 1), jnp.stack([theirs, mine], 1))
        both = both.reshape(n_fsdp, *both.shape[2:])
        n_bias = 4 * EXPERTS
        small = both[:, :n_bias, :rows_out].transpose(1, 0, 2).reshape(n_bias, units)
        gates = both[:, n_bias:, :rows_in].transpose(1, 0, 2).reshape(GATES, depth)

        def parts_of(got, group):
            n = len(group)
            m = 1 if group == GROUPS[-1] else len({o for e in group for o, _ in uses(e)})
            return got[:n], got[n : 2 * n], got[2 * n : 2 * n + m], got[2 * n + m :]

        got = expert_call(GROUPS[0], core, own0, other0, small, xh, xl, ct, None, gates, [], False, [], 0, {})
        dah0, dal0, mix0, (wih0, wil0, grads0, prob, dp0, done0) = parts_of(got, GROUPS[0])
        own1 = tie(spread_out(spread), [done0])
        other1 = lax.ppermute(own1, "fsdp", twin)
        got = expert_call(
            GROUPS[1], core, own1, other1, small, xh, xl, ct, prob, None, [], False, [], 0, {2: mix0[1]}
        )
        dah1, dal1, mix1, (wih1, wil1, grads1, dp1, done1) = parts_of(got, GROUPS[1])
        sum0, token0 = total([lax.all_to_all(grads0, "fsdp", 0, 0)], [done1])
        got = expert_call(
            GROUPS[2],
            core,
            own1,
            other1,
            small,
            xh,
            xl,
            ct,
            prob,
            None,
            [dp0, dp1],
            True,
            [token0],
            1,
            {0: mix0[0], 1: mix1[0], 2: mix1[1]},
        )
        dah2, dal2, (outputs,), (wih2, wil2, keep2, send2, dl, done2) = parts_of(got, GROUPS[2])
        sum1, token1 = total([lax.all_to_all(grads1, "fsdp", 0, 0)], [done2])
        sum0, token0 = reduce_some(sum0, token0, bits[:-1], [done2])
        kept = keep2 + lax.ppermute(tie(send2, [token0, token1]), "fsdp", twin)
        tail = (
            (*dah0, *dah1, *dah2),
            (*dal0, *dal1, *dal2),
            (wih0, wih1, wih2),
            (wil0, wil1, wil2),
            dl,
            gates,
        )
        part, done3 = final_call(*tail, 0, 2, [], [])
        sum2, token2 = total([spread_out(kept)], [done3])
        sum0, token0 = total([sum0, swap(sum0, bits[-1])], [done3])
        sum1, token1 = reduce_some(sum1, token1, bits[:-1], [done3])
        grad_features, done4 = final_call(*tail, 1, 2, [part], [token0, token1, token2])
        sum1, token1 = total([sum1, swap(sum1, bits[-1])], [done4])
        sum2, token2 = reduce_some(sum2, token2, bits[:-1], [done4, token1])
        pair2 = (sum2, swap(sum2, bits[-1]))
        rest = finish(me.astype(jnp.int32).reshape(1), (sum0, sum1, *pair2), w_in, w_out, norm_gain, norm_bias)
        return (outputs, grad_features, *rest)

    return on_device


def solution(mesh):
    placed = (
        P(("dp", "fsdp"), None),
        P(None, ("dp", "fsdp"), None),
        P(("dp", "fsdp")),
        P(("dp", "fsdp")),
        P(None, "fsdp", None),
        P(None, "fsdp"),
        P(None, "fsdp"),
        P(None, "fsdp"),
        P(None, "fsdp", None),
        P(None, "fsdp"),
        P(None, "fsdp", None),
        P("fsdp", None),
    )
    return jax.shard_map(
        make(mesh),
        mesh=mesh,
        in_specs=placed,
        out_specs=(
            P(None, ("dp", "fsdp"), None),
            P(("dp", "fsdp"), None),
            P(None, "fsdp", None),
            P(None, "fsdp"),
            P(None, "fsdp"),
            P(None, "fsdp"),
            P(None, "fsdp", None),
            P(None, "fsdp"),
            P(None, "fsdp", None),
            P("fsdp", None),
        ),
        check_vma=False,
    )
```

```python
import functools

import jax
import jax.numpy as jnp
from jax import lax
from jax.experimental import pallas as pl
from jax.experimental.pallas import tpu as pltpu
from jax.sharding import PartitionSpec as P

TASKS = 2
SPEC = 2
SHARED = 2
EXPERTS = 6
EPSILON = 1e-05
GROUPS = ((0, 1), (2, 3), (4, 5))
TILE = 512
STEP = 16
PARTS = 3
TOKEN = (8, 128)
SPAN = 256
ORDER = (('in', 0), ('in', 1), ('norm', 0), ('in', 2), ('norm', 1), ('in', 3), ('out', 0), ('norm', 2), ('out', 1), ('norm', 3), ('comb', 0), ('out', 2), ('comb', 1), ('out', 3), ('back', 0), ('comb', 2), ('back', 1), ('comb', 3), ('go', 0), ('bnorm', 0), ('back', 2), ('bnorm', 1), ('back', 3), ('gi', 0), ('bnorm', 2), ('go', 1), ('bnorm', 3), ('gi', 1))
LANES = 128
GATES = 16
F32 = jnp.float32
BF16 = jnp.bfloat16
VMEM_BYTES = 58 << 20

NN = (((1,), (0,)), ((), ()))
NT = (((1,), (1,)), ((), ()))
TN = (((0,), (0,)), ((), ()))


def uses(expert):
    if expert >= TASKS * SPEC:
        shared = expert - TASKS * SPEC
        first = [(t, t * (SPEC + SHARED) + SPEC + shared) for t in range(TASKS)]
    else:
        t = expert // SPEC
        first = [(t, t * (SPEC + SHARED) + expert % SPEC)]
    return first + [(TASKS, TASKS * (SPEC + SHARED) + expert)]


def halves(v):
    high = v.astype(BF16)
    return high, (v - high.astype(F32)).astype(BF16)


def dot(a, b, dims):
    return lax.dot_general(a, b, dims, preferred_element_type=F32)


def dot3(a_high, a_low, b_high, b_low, dims):
    return dot(a_high, b_high, dims) + dot(a_low, b_high, dims) + dot(a_high, b_low, dims)


def column(row):
    return jnp.broadcast_to(row, (LANES, row.shape[1])).T


def wide(block, width):
    return jnp.concatenate([block] * (width // LANES), axis=1)


def tie(x, after):
    return pl.pallas_call(
        lambda *refs: None,
        in_specs=[pl.BlockSpec(memory_space=pl.ANY)] + [pl.BlockSpec(memory_space=pltpu.HBM)] * len(after),
        out_specs=pl.BlockSpec(memory_space=pl.ANY),
        out_shape=jax.ShapeDtypeStruct(x.shape, x.dtype),
        input_output_aliases={0: 0},
    )(x, *after)


def total_kernel(n, *refs):
    value = None
    for ref in refs[:n]:
        for part in [ref[...]] if len(ref.shape) == 2 else [ref[k] for k in range(ref.shape[0])]:
            value = part if value is None else value + part
    refs[-2][...] = value
    refs[-1][...] = jnp.zeros_like(refs[-1])


def total(arrays, after):
    vmem = pl.BlockSpec(memory_space=pltpu.VMEM)
    return pl.pallas_call(
        functools.partial(total_kernel, len(arrays)),
        in_specs=[vmem] * len(arrays) + [pl.BlockSpec(memory_space=pltpu.HBM)] * len(after),
        out_specs=[vmem, vmem],
        out_shape=[jax.ShapeDtypeStruct(arrays[0].shape[-2:], F32), jax.ShapeDtypeStruct(TOKEN, F32)],
        compiler_params=pltpu.CompilerParams(vmem_limit_bytes=16 << 20),
    )(*arrays, *after)


def pack_weights(groups, w_in_ref, w_out_ref, to_ref):
    rows_in, rows_out = w_in_ref.shape[1], w_out_ref.shape[1]
    at = 0
    for e in (e for group in groups for e in group):
        for q in range(to_ref.shape[0]):
            to_ref[q, at : at + rows_in] = w_in_ref[e]
            to_ref[q, at + rows_in : at + rows_in + rows_out] = w_out_ref[e]
        at += rows_in + rows_out
    return at


def pack_kernel(in_bias, gain, shift, out_bias, task_gate, shared_gate, w_in_ref, w_out_ref, to_ref):
    rows_in, rows_out = w_in_ref.shape[1], w_out_ref.shape[1]
    at = pack_weights(GROUPS[:1], w_in_ref, w_out_ref, to_ref)
    n = SPEC + SHARED
    for q in range(to_ref.shape[0]):
        to_ref[q, at:] = jnp.zeros((to_ref.shape[1] - at, to_ref.shape[2]), F32)
        for k, bias in enumerate((in_bias, gain, shift, out_bias)):
            to_ref[q, at + k * EXPERTS : at + (k + 1) * EXPERTS, 0:rows_out] = bias[...]
        base = at + 4 * EXPERTS
        for t in range(TASKS):
            to_ref[q, base + t * n : base + (t + 1) * n, 0:rows_in] = task_gate[t]
        base += TASKS * n
        to_ref[q, base : base + EXPERTS, 0:rows_in] = shared_gate[...]


def pack(pairs, w_in, in_bias, gain, shift, w_out, out_bias, task_gate, shared_gate):
    rows = len(GROUPS[0]) * (w_in.shape[1] + w_out.shape[1]) + 4 * EXPERTS + GATES
    return pl.pallas_call(
        pack_kernel,
        out_shape=jax.ShapeDtypeStruct((pairs, rows, w_in.shape[2]), F32),
        compiler_params=pltpu.CompilerParams(vmem_limit_bytes=VMEM_BYTES),
    )(in_bias, gain, shift, out_bias, task_gate.transpose(0, 2, 1), shared_gate.T, w_in, w_out)


def prep_kernel(x_ref, c_ref, valid_ref, w_in_ref, w_out_ref, xh_ref, xl_ref, ct_ref, to_ref, done_ref):
    depth = x_ref.shape[1]

    @pl.when(pl.program_id(0) == 0)
    def _():
        pack_weights(GROUPS[1:], w_in_ref, w_out_ref, to_ref)
        done_ref[...] = jnp.zeros_like(done_ref)

    high, low = halves(x_ref[...].T)
    xh_ref[0:depth] = high
    xh_ref[depth:] = jnp.ones((xh_ref.shape[0] - depth, xh_ref.shape[1]), BF16)
    xl_ref[...] = low
    valid = valid_ref[...]
    for o in range(c_ref.shape[0]):
        ct_ref[o] = c_ref[o].T * valid


def prep(features, cotangent, valid, w_in, w_out, pairs):
    rows, depth = features.shape
    packed = sum(len(g) for g in GROUPS[1:]) * (w_in.shape[1] + w_out.shape[1])
    outs, _, units = cotangent.shape
    return pl.pallas_call(
        prep_kernel,
        grid=(rows // TILE,),
        in_specs=[
            pl.BlockSpec((TILE, depth), lambda i: (i, 0)),
            pl.BlockSpec((outs, TILE, units), lambda i: (0, i, 0)),
            pl.BlockSpec((1, TILE), lambda i: (0, i)),
            pl.BlockSpec(w_in.shape, lambda i: (0, 0, 0)),
            pl.BlockSpec(w_out.shape, lambda i: (0, 0, 0)),
        ],
        out_specs=[
            pl.BlockSpec((depth + STEP, TILE), lambda i: (0, i)),
            pl.BlockSpec((depth, TILE), lambda i: (0, i)),
            pl.BlockSpec((outs, units, TILE), lambda i: (0, 0, i)),
            pl.BlockSpec((pairs, packed, units), lambda i: (0, 0, 0)),
            pl.BlockSpec(TOKEN, lambda i: (0, 0)),
        ],
        out_shape=[
            jax.ShapeDtypeStruct((depth + STEP, rows), BF16),
            jax.ShapeDtypeStruct((depth, rows), BF16),
            jax.ShapeDtypeStruct((outs, units, rows), F32),
            jax.ShapeDtypeStruct((pairs, packed, units), F32),
            jax.ShapeDtypeStruct(TOKEN, F32),
        ],
        compiler_params=pltpu.CompilerParams(vmem_limit_bytes=VMEM_BYTES),
        cost_estimate=pl.CostEstimate(flops=0, bytes_accessed=32000000, transcendentals=0),
    )(features, cotangent, valid, w_in, w_out)


def softmax_rows(v):
    e = jnp.exp(v - jnp.max(v, axis=0, keepdims=True))
    return e / jnp.sum(e, axis=0, keepdims=True)


def expert_kernel(group, first, last, n_after, partial, *refs):
    used = sorted({o for e in group for o, _ in uses(e)})
    names = ["core", "own", "other", "small", "xh", "xl"]
    names += [f"c{o}" for o in used]
    names += ["gates"] if first else ["prob"]
    if last:
        names += [f"dp{k}" for k in range(len(GROUPS) - 1)]
    names += [f"in{o}" for o in partial]
    names += [f"after{k}" for k in range(n_after)]
    names += [f"{name}{l}" for name in ("dah", "dal") for l in range(len(group))]
    names += ["out"] if last else [f"out{o}" for o in used]
    names += ["wih", "wil"]
    names += ["keep", "send"] if last else ["grads"]
    if first:
        names += ["prob"]
    names += ["dl"] if last else ["dp"]
    names += ["done"]
    each = ["win_t", "win_t_low", "wp", "wp_low", "wp_t", "wp_t_low", "b_in", "b_out", "acc_w", "acc_g"]
    each += ["h", "u", "a", "xhat", "h2", "g", "ex", "xhh", "xhl", "dzh", "dzl"]
    names += [f"{name}{l}" for name in each for l in range(len(group))]
    if last:
        names += ["all_dp", "acc_gate"] + [f"mix{o}" for o in used]
    r = dict(zip(names, refs, strict=True))
    for name in (*each, "dah", "dal"):
        r[name] = [r[f"{name}{l}"] for l in range(len(group))]
    step = pl.program_id(0)
    count = len(group)
    units = r["acc_w"][0].shape[1]
    depth = r["xl"].shape[0]
    pairs = r["own"].shape[0]
    devices = 2 * pairs
    rows_in, rows_out = depth // devices, units // devices
    rows_all = rows_in + rows_out
    core = r["core"][0]
    tile = r["xl"].shape[1]
    chunks = [slice(k, k + STEP) for k in range(0, units, STEP)]

    @pl.when(step == 0)
    def _():
        for l, e in enumerate(group):
            base = l * rows_all
            for q in range(pairs):
                for src, at in ((r["own"], core), (r["other"], 1 - core)):
                    place = q * 2 + at
                    r["acc_w"][l][pl.ds(place * rows_in, rows_in)] = src[q, base : base + rows_in]
                    r["acc_g"][l][pl.ds(place * rows_out, rows_out)] = src[
                        q, base + rows_in : base + rows_all
                    ]
            w_in = r["acc_w"][l][0:depth]
            high, low = halves(w_in)
            r["wih"][l] = high
            r["wil"][l] = low
            high, low = halves((0.5 * w_in).T)
            r["win_t"][l][0:units] = high
            r["win_t_low"][l][0:units] = low
            w_out = r["acc_g"][l][0:units]
            b_in, gain, shift, b_out = (r["small"][k * EXPERTS + e : k * EXPERTS + e + 1] for k in range(4))
            scaled = w_out * wide(column(gain), units)
            high, low = halves(scaled)
            r["wp"][l][...] = high
            r["wp_low"][l][...] = low
            high, low = halves((0.5 * scaled).T)
            r["wp_t"][l][...] = high
            r["wp_t_low"][l][...] = low
            b_out = b_out + jnp.sum(w_out * wide(column(shift), units), axis=0, keepdims=True)
            r["b_in"][l][...] = column(0.5 * b_in)
            r["b_out"][l][...] = column(0.5 * b_out)
            r["xhh"][l][units:] = jnp.ones((STEP, tile), BF16)
        if first:
            high, low = halves(r["gates"][...])
            r["win_t"][0][units:] = high
            r["win_t_low"][0][units:] = low
        for l in range(count):
            r["acc_w"][l][...] = jnp.zeros_like(r["acc_w"][l])
            r["acc_g"][l][...] = jnp.zeros_like(r["acc_g"][l])
        r["done"][...] = jnp.zeros_like(r["done"])
        if last:
            r["acc_gate"][...] = jnp.zeros_like(r["acc_gate"])

    stats = {}

    spans = [slice(k, k + SPAN) for k in range(0, tile, SPAN)]
    zero = jnp.zeros((STEP, SPAN), F32)

    def project_in(l, s):
        top = units + (GATES if first and l == 0 else 0)
        r["h"][l][0:top, s] = dot3(
            r["win_t"][l][0:top], r["win_t_low"][l][0:top], r["xh"][0:depth, s], r["xl"][:, s], NN
        )

    def gate_weights(s):
        z = r["h"][0][units:, s]
        for lower, upper in ((0, 4), (4, 8), (8, 14)):
            r["prob"][lower:upper, s] = softmax_rows(z[lower:upper])
        r["prob"][14:16, s] = jnp.zeros((2, SPAN), F32)

    def normalise(l, s):
        total = zero
        for c in chunks:
            h = r["h"][l][c, s] + wide(r["b_in"][l][c], SPAN)
            u = 1.0 + jnp.tanh(h)
            a = h * u
            r["u"][l][c, s] = u
            r["a"][l][c, s] = a
            total = total + a
        mean = jnp.sum(total, axis=0, keepdims=True) * (1.0 / units)
        total = zero
        for c in chunks:
            d = r["a"][l][c, s] - mean
            total = total + d * d
        scale = lax.rsqrt(jnp.sum(total, axis=0, keepdims=True) * (1.0 / units) + EPSILON)
        stats[l, s.start] = scale
        for c in chunks:
            x = (r["a"][l][c, s] - mean) * scale
            r["xhat"][l][c, s] = x
            r["xhh"][l][c, s], r["xhl"][l][c, s] = halves(x)

    def project_out(l, s):
        r["h2"][l][:, s] = dot3(
            r["wp_t"][l][...], r["wp_t_low"][l][...], r["xhh"][l][0:units, s], r["xhl"][l][:, s], NN
        )

    def combine(l, s):
        taken = uses(group[l])
        prob = [0.5 * r["prob"][row : row + 1, s] for _, row in taken]
        sums = [zero for _ in taken]
        end = l == count - 1
        full = [[r["prob"][row : row + 1, s] for _, row in uses(e)] for e in group] if end else None
        for c in chunks:
            h = r["h2"][l][c, s] + wide(r["b_out"][l][c], SPAN)
            u = 1.0 + jnp.tanh(h)
            ex = h * u
            if not end:
                r["ex"][l][c, s] = ex
            slope = u + ex * (2.0 - u)
            d = None
            for k, (o, _) in enumerate(taken):
                cot = r[f"c{o}"][0, c, s]
                sums[k] = sums[k] + cot * ex
                term = prob[k] * cot
                d = term if d is None else d + term
                if end:
                    mix = full[l][k] * ex
                    for m in range(l):
                        mix = mix + full[m][k] * r["ex"][m][c, s]
                    if o in partial:
                        mix = mix + r[f"in{o}"][c, s]
                    if last:
                        r[f"mix{o}"][c, s] = mix
                    else:
                        r[f"out{o}"][c, s] = mix
            r["dzh"][l][c, s], r["dzl"][l][c, s] = halves(d * slope)
        for k, (_, row) in enumerate(taken):
            value = jnp.sum(sums[k], axis=0, keepdims=True)
            if last:
                r["all_dp"][row : row + 1, s] = value
            else:
                at = l * len(taken) + k
                r["dp"][at : at + 1, s] = value

    def back_out(l, s):
        r["g"][l][:, s] = dot3(
            r["wp"][l][...], r["wp_low"][l][...], r["dzh"][l][:, s], r["dzl"][l][:, s], NN
        )

    def grad_out(l):
        r["acc_g"][l][...] += dot(r["xhh"][l][...], r["dzh"][l][...], NT) + dot(
            r["xhh"][l][...], r["dzl"][l][...], NT
        )
        r["acc_g"][l][0:units] += dot(r["xhl"][l][...], r["dzh"][l][...], NT)

    def back_norm(l, s):
        total, along = zero, zero
        for c in chunks:
            g = r["g"][l][c, s]
            total = total + g
            along = along + g * r["xhat"][l][c, s]
        mean = jnp.sum(total, axis=0, keepdims=True) * (1.0 / units)
        along = jnp.sum(along, axis=0, keepdims=True) * (1.0 / units)
        scale = 0.5 * stats[l, s.start]
        for c in chunks:
            u, a = r["u"][l][c, s], r["a"][l][c, s]
            slope = (u + a * (2.0 - u)) * scale
            da = (r["g"][l][c, s] - mean - r["xhat"][l][c, s] * along) * slope
            r["dah"][l][c, s], r["dal"][l][c, s] = halves(da)

    def grad_in(l):
        high, low = r["dah"][l][...], r["dal"][l][...]
        r["acc_w"][l][...] += dot(r["xh"][...], high, NT) + dot(r["xh"][...], low, NT)
        r["acc_w"][l][0:depth] += dot(r["xl"][...], high, NT)

    chains = [(l, s) for l in range(count) for s in spans]
    for stage in ORDER:
        if isinstance(stage, tuple):
            name, k = stage
            if name == "go":
                grad_out(k)
            elif name == "gi":
                grad_in(k)
            else:
                at = {
                    "in": project_in, "norm": normalise, "out": project_out, "comb": combine, "back": back_out,
                    "bnorm": back_norm,
                }[name]
                at(*chains[k])
                if name == "in" and first and chains[k][0] == 0:
                    gate_weights(chains[k][1])

    if last:
        for o in used:
            r["out"][o] = r[f"mix{o}"][...].T
    if last:
        for k, g in enumerate(GROUPS[:-1]):
            at = 0
            for e in g:
                for _, row in uses(e):
                    r["all_dp"][row : row + 1] = r[f"dp{k}"][at : at + 1]
                    at += 1
        for lower, upper in ((0, 4), (4, 8), (8, 14)):
            p, d = r["prob"][lower:upper], r["all_dp"][lower:upper]
            r["dl"][lower:upper] = p * (d - jnp.sum(p * d, axis=0, keepdims=True))
        r["dl"][14:16] = jnp.zeros((2, tile), F32)
        high, low = halves(r["dl"][...])
        both = dot(r["xh"][0:depth], jnp.concatenate([high, low], 0), NT)
        r["acc_gate"][:, 0:GATES] += both[:, 0:GATES] + both[:, GATES:] + dot(r["xl"][...], high, NT)

    @pl.when(step == pl.num_programs(0) - 1)
    def _():
        for l in range(count):
            base = l * (rows_all + 8)
            tail = jnp.concatenate([r["acc_g"][l][units : units + 1], r["acc_w"][l][depth : depth + 1]], 0)
            tail = jnp.concatenate([tail] * 4, 0)
            if last:
                places = [
                    (dst, q, q * 2 + at)
                    for q in range(pairs)
                    for dst, at in ((r["keep"], core), (r["send"], 1 - core))
                ]
            else:
                places = [(r["grads"], k, k) for k in range(devices)]
            for dst, q, place in places:
                dst[q, base : base + rows_in] = r["acc_w"][l][pl.ds(place * rows_in, rows_in)]
                dst[q, base + rows_in : base + rows_all] = r["acc_g"][l][pl.ds(place * rows_out, rows_out)]
                dst[q, base + rows_all : base + rows_all + 8] = tail
        if last:
            gate = r["acc_gate"][...].T[0:GATES]
            base = count * (rows_all + 8)
            for q in range(pairs):
                even = gate[:, 2 * q * rows_in : (2 * q + 1) * rows_in]
                odd = gate[:, (2 * q + 1) * rows_in : (2 * q + 2) * rows_in]
                for dst, at in ((r["keep"], core), (r["send"], 1 - core)):
                    dst[q, base:, 0:rows_in] = jnp.where(at == 0, even, odd)


def expert_call(group, core, own, other, small, xh, xl, ct, prob, gates, dps, last, after, skip, mixed):
    first = gates is not None
    pairs, _, units = own.shape
    depth, rows = xl.shape
    devices = 2 * pairs
    rows_in, rows_out = depth // devices, units // devices
    count = len(group)
    whole = lambda shape: pl.BlockSpec(shape, lambda i: (0,) * len(shape))
    along = lambda n: pl.BlockSpec((n, TILE), lambda i: (0, i))
    used = sorted({o for e in group for o, _ in uses(e)})
    ins = [core, own, other, small, xh, xl] + [ct] * len(used)
    held = own.shape[1] if first else count * (rows_in + rows_out)
    weights = pl.BlockSpec((pairs, held, units), lambda i: (0, skip, 0))
    in_specs = [
        pl.BlockSpec(memory_space=pltpu.SMEM),
        weights,
        weights,
        whole(small.shape),
        along(xh.shape[0]),
        along(depth),
    ]
    in_specs += [pl.BlockSpec((1, units, TILE), lambda i, o=o: (o, 0, i)) for o in used]
    if first:
        ins.append(gates)
        in_specs.append(whole(gates.shape))
    else:
        ins.append(prob)
        in_specs.append(along(GATES))
    if last:
        ins += dps
        in_specs += [along(8)] * len(dps)
    ins += [mixed[o] for o in sorted(mixed)]
    in_specs += [along(units)] * len(mixed)
    ins += after
    in_specs += [pl.BlockSpec(memory_space=pltpu.HBM)] * len(after)
    packed = count * (rows_in + rows_out + 8)
    shape = jax.ShapeDtypeStruct
    if last:
        mixes = [
            (pl.BlockSpec((len(used), TILE, units), lambda i: (0, i, 0)), shape((len(used), rows, units), F32))
        ]
    else:
        mixes = [(along(units), shape((units, rows), F32))] * len(used)
    outs = [
        *[(along(units), shape((units, rows), BF16))] * (2 * count),
        *mixes,
        (whole((count, depth, units)), shape((count, depth, units), BF16)),
        (whole((count, depth, units)), shape((count, depth, units), BF16)),
    ]
    if last:
        packed += GATES
        outs += [(whole((pairs, packed, units)), shape((pairs, packed, units), F32))] * 2
    else:
        outs.append((whole((devices, packed, units)), shape((devices, packed, units), F32)))
    if first:
        outs.append((along(GATES), shape((GATES, rows), F32)))
    if last:
        outs.append((along(GATES), shape((GATES, rows), F32)))
    else:
        outs.append((along(8), shape((8, rows), F32)))
    outs.append((whole(TOKEN), shape(TOKEN, F32)))
    top = units + (GATES if first else 0)
    kinds = [
        ((top, depth), BF16),
        ((top, depth), BF16),
        ((units, units), BF16),
        ((units, units), BF16),
        ((units, units), BF16),
        ((units, units), BF16),
        ((units, LANES), F32),
        ((units, LANES), F32),
        ((depth + STEP, units), F32),
        ((units + STEP, units), F32),
        ((top, TILE), F32),
        ((units, TILE), F32),
        ((units, TILE), F32),
        ((units, TILE), F32),
        ((units, TILE), F32),
        ((units, TILE), F32),
        ((units, TILE), F32),
        ((units + STEP, TILE), BF16),
        ((units, TILE), BF16),
        ((units, TILE), BF16),
        ((units, TILE), BF16),
    ]
    scratch = [pltpu.VMEM(*kind) for kind in kinds for _ in group]
    if last:
        scratch += [pltpu.VMEM((GATES, TILE), F32), pltpu.VMEM((depth, LANES), F32)]
        scratch += [pltpu.VMEM((units, TILE), F32)] * len(used)
    return pl.pallas_call(
        functools.partial(expert_kernel, group, first, last, len(after), tuple(sorted(mixed))),
        grid=(rows // TILE,),
        in_specs=in_specs,
        out_specs=[o[0] for o in outs],
        out_shape=[o[1] for o in outs],
        scratch_shapes=scratch,
        compiler_params=pltpu.CompilerParams(vmem_limit_bytes=58 << 20),
        cost_estimate=pl.CostEstimate(
            flops=20000000000 * count // 2, bytes_accessed=30000000, transcendentals=0
        ),
    )(*ins)


def final_kernel(steps, *refs):
    n = EXPERTS
    dahs, dals = refs[:n], refs[n : 2 * n]
    wihs, wils = refs[2 * n : 2 * n + len(GROUPS)], refs[2 * n + len(GROUPS) : 2 * n + 2 * len(GROUPS)]
    dl_ref, gates_ref = refs[2 * n + 2 * len(GROUPS) : 2 * n + 2 * len(GROUPS) + 2]
    gf_ref, done_ref, gate_ref = refs[-3:]
    done_ref[...] = jnp.zeros_like(done_ref)

    @pl.when(pl.program_id(0) == 0)
    def _():
        high, low = halves(gates_ref[...])
        gate_ref[0:GATES] = high
        gate_ref[GATES : 2 * GATES] = low
        gate_ref[2 * GATES :] = high

    for k in range(0, TILE, SPAN):
        span = slice(k, k + SPAN)
        high, low = halves(dl_ref[:, span])
        value = dot(gate_ref[...], jnp.concatenate([high, high, low], 0), TN)
        at = 0
        for k, group in enumerate(GROUPS):
            for l in range(len(group)):
                value = value + dot3(wihs[k][l], wils[k][l], dahs[at][:, span], dals[at][:, span], NN)
                at += 1
        gf_ref[span] = value.T


def final_call(dahs, dals, wihs, wils, dl, gates, part, before, after):
    rows = dl.shape[1]
    _, depth, units = wihs[0].shape
    tiles = rows // TILE
    skip, end = (tiles * k // PARTS for k in (part, part + 1))
    steps, parts = end - skip, PARTS
    whole = lambda a: pl.BlockSpec(a.shape, lambda i: (0,) * a.ndim)
    along = lambda a: pl.BlockSpec((a.shape[0], TILE), lambda i: (0, i + skip))
    ins = [*dahs, *dals, *wihs, *wils, dl, gates, *before, *after]
    n = 2 * EXPERTS + 2 * len(GROUPS) + 2
    return pl.pallas_call(
        functools.partial(final_kernel, steps),
        grid=(steps,),
        in_specs=[along(a) for a in (*dahs, *dals)]
        + [whole(a) for a in (*wihs, *wils)]
        + [along(dl), whole(gates)]
        + [pl.BlockSpec(memory_space=pltpu.HBM)] * (len(before) + len(after)),
        out_specs=[pl.BlockSpec((TILE, depth), lambda i: (i + skip, 0)), pl.BlockSpec(TOKEN, lambda i: (0, 0))],
        out_shape=[jax.ShapeDtypeStruct((rows, depth), F32), jax.ShapeDtypeStruct(TOKEN, F32)],
        scratch_shapes=[pltpu.VMEM((3 * GATES, depth), BF16)],
        input_output_aliases={n + k: k for k in range(len(before))},
        compiler_params=pltpu.CompilerParams(vmem_limit_bytes=58 << 20),
        cost_estimate=pl.CostEstimate(
            flops=15000000000 // parts, bytes_accessed=25000000 // parts, transcendentals=0
        ),
    )(*ins)


def finish_kernel(me_ref, *refs):
    n = len(GROUPS) + 1
    w_out_ref, gain_ref, shift_ref = refs[n : n + 3]
    g_in, g_in_bias, g_gain, g_shift, g_out, g_out_bias, g_task, g_shared = refs[n + 3 :]
    rows_in, rows_out, units = g_in.shape[1], g_out.shape[1], g_in.shape[2]
    me = me_ref[0]

    def own(row):
        value = row[:, 0:rows_out]
        for p in range(1, units // rows_out):
            value = jnp.where(me == p, row[:, p * rows_out : (p + 1) * rows_out], value)
        return value

    def as_row(col):
        return jnp.broadcast_to(col, (rows_out, LANES)).T[0:1]

    for k, group in enumerate(GROUPS):
        if k < len(GROUPS) - 1:
            add = lambda lower, upper, a=refs[k]: a[lower:upper]
        else:
            add = lambda lower, upper, a=refs[k], b=refs[k + 1]: a[lower:upper] + b[lower:upper]
        at = 0
        for e in group:
            g_in[e] = add(at, at + rows_in)
            at += rows_in
            raw = add(at, at + rows_out)
            at += rows_out
            tail = add(at, at + 8)
            at += 8
            total = tail[0:1]
            gain = wide(column(gain_ref[e : e + 1]), units)
            shift = wide(column(shift_ref[e : e + 1]), units)
            g_out[e] = gain * raw + shift * total
            w = w_out_ref[e]
            g_gain[e : e + 1] = as_row(jnp.sum(w * raw, axis=1, keepdims=True))
            g_shift[e : e + 1] = as_row(jnp.sum(w * total, axis=1, keepdims=True))
            g_in_bias[e : e + 1] = own(tail[1:2])
            g_out_bias[e : e + 1] = own(total)
    gate = add(at, at + GATES)[:, 0:rows_in]
    m = SPEC + SHARED
    for t in range(TASKS):
        g_task[t] = gate[t * m : (t + 1) * m]
    g_shared[...] = gate[TASKS * m : TASKS * m + EXPERTS]


def finish(me, totals, w_in, w_out, gain, shift):
    experts, rows_in, units = w_in.shape
    rows_out = w_out.shape[1]
    shape = lambda *s: jax.ShapeDtypeStruct(s, F32)
    vector = shape(experts, rows_out)
    outs = [
        shape(*w_in.shape),
        vector,
        vector,
        vector,
        shape(*w_out.shape),
        vector,
        shape(TASKS, SPEC + SHARED, rows_in),
        shape(EXPERTS, rows_in),
    ]
    vmem = pl.BlockSpec(memory_space=pltpu.VMEM)
    got = pl.pallas_call(
        finish_kernel,
        in_specs=[pl.BlockSpec(memory_space=pltpu.SMEM)] + [vmem] * (len(totals) + 3),
        out_specs=[vmem] * len(outs),
        out_shape=outs,
        compiler_params=pltpu.CompilerParams(vmem_limit_bytes=16 << 20),
    )(me, *totals, w_out, gain, shift)
    return (*got[:6], got[6].transpose(0, 2, 1), got[7].T)


def make(mesh):
    n_fsdp, n_dp = mesh.shape["fsdp"], mesh.shape["dp"]
    pairs = n_fsdp // 2
    across = [[q * 2 + c for q in range(pairs)] for c in range(2)]
    twin = [(i, i ^ 1) for i in range(n_fsdp)]

    def spread_out(x):
        return lax.all_to_all(x, "fsdp", 0, 0, axis_index_groups=across)

    def swap(x, bit):
        return lax.ppermute(x, "dp", [(i, i ^ bit) for i in range(n_dp)])

    def reduce_some(x, token, some, beside):
        for bit in some:
            x, token = total([x, swap(x, bit)], beside)
        return x, token

    bits = [1 << k for k in range(n_dp.bit_length() - 1)]

    def on_device(
        features, cotangent, counts, keep, w_in, in_bias, norm_gain, norm_bias, w_out, out_bias, task_gate, shared_gate
    ):
        rows = features.shape[0]
        depth = features.shape[1]
        experts, rows_in, units = w_in.shape
        rows_out = w_out.shape[1]
        valid = (lax.broadcasted_iota(jnp.int32, (1, rows), 1) < counts[0]) & (keep.reshape(1, rows) > 0)
        me = lax.axis_index("fsdp")
        core = (me % 2).astype(jnp.int32).reshape(1)
        xh, xl, ct, spread, done = prep(features, cotangent, valid.astype(F32), w_in, w_out, pairs)
        own0 = tie(
            spread_out(
                pack(pairs, w_in, in_bias, norm_gain, norm_bias, w_out, out_bias, task_gate, shared_gate)
            ),
            [done],
        )
        other0 = lax.ppermute(own0, "fsdp", twin)
        begin = len(GROUPS[0]) * (rows_in + rows_out)
        mine, theirs = own0[:, begin:], other0[:, begin:]
        both = jnp.where(core[0] == 0, jnp.stack([mine, theirs], 1), jnp.stack([theirs, mine], 1))
        both = both.reshape(n_fsdp, *both.shape[2:])
        n_bias = 4 * EXPERTS
        small = both[:, :n_bias, :rows_out].transpose(1, 0, 2).reshape(n_bias, units)
        gates = both[:, n_bias:, :rows_in].transpose(1, 0, 2).reshape(GATES, depth)

        def parts_of(got, group):
            n = len(group)
            m = 1 if group == GROUPS[-1] else len({o for e in group for o, _ in uses(e)})
            return got[:n], got[n : 2 * n], got[2 * n : 2 * n + m], got[2 * n + m :]

        got = expert_call(GROUPS[0], core, own0, other0, small, xh, xl, ct, None, gates, [], False, [], 0, {})
        dah0, dal0, mix0, (wih0, wil0, grads0, prob, dp0, done0) = parts_of(got, GROUPS[0])
        own1 = tie(spread_out(spread), [done0])
        other1 = lax.ppermute(own1, "fsdp", twin)
        got = expert_call(
            GROUPS[1], core, own1, other1, small, xh, xl, ct, prob, None, [], False, [], 0, {2: mix0[1]}
        )
        dah1, dal1, mix1, (wih1, wil1, grads1, dp1, done1) = parts_of(got, GROUPS[1])
        sum0, token0 = total([lax.all_to_all(grads0, "fsdp", 0, 0)], [done1])
        got = expert_call(
            GROUPS[2],
            core,
            own1,
            other1,
            small,
            xh,
            xl,
            ct,
            prob,
            None,
            [dp0, dp1],
            True,
            [token0],
            1,
            {0: mix0[0], 1: mix1[0], 2: mix1[1]},
        )
        dah2, dal2, (outputs,), (wih2, wil2, keep2, send2, dl, done2) = parts_of(got, GROUPS[2])
        sum1, token1 = total([lax.all_to_all(grads1, "fsdp", 0, 0)], [done2])
        sum0, token0 = reduce_some(sum0, token0, bits[:-1], [done2])
        kept = keep2 + lax.ppermute(tie(send2, [token0, token1]), "fsdp", twin)
        tail = (
            (*dah0, *dah1, *dah2),
            (*dal0, *dal1, *dal2),
            (wih0, wih1, wih2),
            (wil0, wil1, wil2),
            dl,
            gates,
        )
        part, done3 = final_call(*tail, 0, [], [])
        sum2, token2 = total([spread_out(kept)], [done3])
        sum1, token1 = reduce_some(sum1, token1, bits[:-1], [done3])
        part, done4 = final_call(*tail, 1, [part], [token1, token2])
        sum0, token0 = total([sum0, swap(sum0, bits[-1])], [done4])
        sum2, token2 = reduce_some(sum2, token2, bits[:-1], [done4])
        grad_features, done5 = final_call(*tail, 2, [part], [token0, token2])
        sum1, token1 = total([sum1, swap(sum1, bits[-1])], [done5])
        pair2 = (sum2, swap(sum2, bits[-1]))
        rest = finish(me.astype(jnp.int32).reshape(1), (sum0, sum1, *pair2), w_in, w_out, norm_gain, norm_bias)
        return (outputs, grad_features, *rest)

    return on_device


def solution(mesh):
    placed = (
        P(("dp", "fsdp"), None),
        P(None, ("dp", "fsdp"), None),
        P(("dp", "fsdp")),
        P(("dp", "fsdp")),
        P(None, "fsdp", None),
        P(None, "fsdp"),
        P(None, "fsdp"),
        P(None, "fsdp"),
        P(None, "fsdp", None),
        P(None, "fsdp"),
        P(None, "fsdp", None),
        P("fsdp", None),
    )
    return jax.shard_map(
        make(mesh),
        mesh=mesh,
        in_specs=placed,
        out_specs=(
            P(None, ("dp", "fsdp"), None),
            P(("dp", "fsdp"), None),
            P(None, "fsdp", None),
            P(None, "fsdp"),
            P(None, "fsdp"),
            P(None, "fsdp"),
            P(None, "fsdp", None),
            P(None, "fsdp"),
            P(None, "fsdp", None),
            P("fsdp", None),
        ),
        check_vma=False,
    )
```

```python
import functools

import jax
import jax.numpy as jnp
from jax import lax
from jax.experimental import pallas as pl
from jax.experimental.pallas import tpu as pltpu
from jax.sharding import PartitionSpec as P

TASKS = 2
SPEC = 2
SHARED = 2
EXPERTS = 6
EPSILON = 1e-05
GROUPS = ((0, 1), (2, 3), (4, 5))
TILE = 512
STEP = 16
PARTS = 3
TOKEN = (8, 128)
SPAN = 256
ORDER = (('in', 0), ('in', 1), ('norm', 0), ('in', 2), ('norm', 1), ('in', 3), ('out', 0), ('norm', 2), ('out', 1), ('norm', 3), ('comb', 0), ('out', 2), ('comb', 1), ('out', 3), ('back', 0), ('comb', 2), ('back', 1), ('comb', 3), ('go', 0), ('bnorm', 0), ('back', 2), ('bnorm', 1), ('back', 3), ('gi', 0), ('bnorm', 2), ('go', 1), ('bnorm', 3), ('gi', 1))
LANES = 128
GATES = 16
F32 = jnp.float32
BF16 = jnp.bfloat16
VMEM_BYTES = 58 << 20

NN = (((1,), (0,)), ((), ()))
NT = (((1,), (1,)), ((), ()))
TN = (((0,), (0,)), ((), ()))


def uses(expert):
    if expert >= TASKS * SPEC:
        shared = expert - TASKS * SPEC
        first = [(t, t * (SPEC + SHARED) + SPEC + shared) for t in range(TASKS)]
    else:
        t = expert // SPEC
        first = [(t, t * (SPEC + SHARED) + expert % SPEC)]
    return first + [(TASKS, TASKS * (SPEC + SHARED) + expert)]


def halves(v):
    high = v.astype(BF16)
    return high, (v - high.astype(F32)).astype(BF16)


def dot(a, b, dims):
    return lax.dot_general(a, b, dims, preferred_element_type=F32)


def dot3(a_high, a_low, b_high, b_low, dims):
    return dot(a_high, b_high, dims) + dot(a_low, b_high, dims) + dot(a_high, b_low, dims)


def dot3_stacked(both, b_high, b_low):
    n = both.shape[0] // 2
    product = dot(both[...], b_high, NN)
    return product[0:n] + product[n:] + dot(both[0:n], b_low, NN)


def column(row):
    return jnp.broadcast_to(row, (LANES, row.shape[1])).T


def wide(block, width):
    return jnp.concatenate([block] * (width // LANES), axis=1)


def tie(x, after):
    return pl.pallas_call(
        lambda *refs: None,
        in_specs=[pl.BlockSpec(memory_space=pl.ANY)] + [pl.BlockSpec(memory_space=pltpu.HBM)] * len(after),
        out_specs=pl.BlockSpec(memory_space=pl.ANY),
        out_shape=jax.ShapeDtypeStruct(x.shape, x.dtype),
        input_output_aliases={0: 0},
    )(x, *after)


def total_kernel(n, *refs):
    value = None
    for ref in refs[:n]:
        for part in [ref[...]] if len(ref.shape) == 2 else [ref[k] for k in range(ref.shape[0])]:
            value = part if value is None else value + part
    refs[-2][...] = value
    refs[-1][...] = jnp.zeros_like(refs[-1])


def total(arrays, after):
    vmem = pl.BlockSpec(memory_space=pltpu.VMEM)
    return pl.pallas_call(
        functools.partial(total_kernel, len(arrays)),
        in_specs=[vmem] * len(arrays) + [pl.BlockSpec(memory_space=pltpu.HBM)] * len(after),
        out_specs=[vmem, vmem],
        out_shape=[jax.ShapeDtypeStruct(arrays[0].shape[-2:], F32), jax.ShapeDtypeStruct(TOKEN, F32)],
        compiler_params=pltpu.CompilerParams(vmem_limit_bytes=16 << 20),
    )(*arrays, *after)


def pack_weights(groups, w_in_ref, w_out_ref, to_ref):
    rows_in, rows_out = w_in_ref.shape[1], w_out_ref.shape[1]
    at = 0
    for e in (e for group in groups for e in group):
        for q in range(to_ref.shape[0]):
            to_ref[q, at : at + rows_in] = w_in_ref[e]
            to_ref[q, at + rows_in : at + rows_in + rows_out] = w_out_ref[e]
        at += rows_in + rows_out
    return at


def pack_kernel(in_bias, gain, shift, out_bias, task_gate, shared_gate, w_in_ref, w_out_ref, to_ref):
    rows_in, rows_out = w_in_ref.shape[1], w_out_ref.shape[1]
    at = pack_weights(GROUPS[:1], w_in_ref, w_out_ref, to_ref)
    n = SPEC + SHARED
    for q in range(to_ref.shape[0]):
        to_ref[q, at:] = jnp.zeros((to_ref.shape[1] - at, to_ref.shape[2]), F32)
        for k, bias in enumerate((in_bias, gain, shift, out_bias)):
            to_ref[q, at + k * EXPERTS : at + (k + 1) * EXPERTS, 0:rows_out] = bias[...]
        base = at + 4 * EXPERTS
        for t in range(TASKS):
            to_ref[q, base + t * n : base + (t + 1) * n, 0:rows_in] = task_gate[t]
        base += TASKS * n
        to_ref[q, base : base + EXPERTS, 0:rows_in] = shared_gate[...]


def pack(pairs, w_in, in_bias, gain, shift, w_out, out_bias, task_gate, shared_gate):
    rows = len(GROUPS[0]) * (w_in.shape[1] + w_out.shape[1]) + 4 * EXPERTS + GATES
    return pl.pallas_call(
        pack_kernel,
        out_shape=jax.ShapeDtypeStruct((pairs, rows, w_in.shape[2]), F32),
        compiler_params=pltpu.CompilerParams(vmem_limit_bytes=VMEM_BYTES),
    )(in_bias, gain, shift, out_bias, task_gate.transpose(0, 2, 1), shared_gate.T, w_in, w_out)


def prep_kernel(x_ref, c_ref, valid_ref, w_in_ref, w_out_ref, xh_ref, xl_ref, ct_ref, to_ref, done_ref):
    depth = x_ref.shape[1]

    @pl.when(pl.program_id(0) == 0)
    def _():
        pack_weights(GROUPS[1:], w_in_ref, w_out_ref, to_ref)
        done_ref[...] = jnp.zeros_like(done_ref)

    high, low = halves(x_ref[...].T)
    xh_ref[0:depth] = high
    xh_ref[depth:] = jnp.ones((xh_ref.shape[0] - depth, xh_ref.shape[1]), BF16)
    xl_ref[...] = low
    valid = valid_ref[...]
    for o in range(c_ref.shape[0]):
        ct_ref[o] = c_ref[o].T * valid


def prep(features, cotangent, valid, w_in, w_out, pairs):
    rows, depth = features.shape
    packed = sum(len(g) for g in GROUPS[1:]) * (w_in.shape[1] + w_out.shape[1])
    outs, _, units = cotangent.shape
    return pl.pallas_call(
        prep_kernel,
        grid=(rows // TILE,),
        in_specs=[
            pl.BlockSpec((TILE, depth), lambda i: (i, 0)),
            pl.BlockSpec((outs, TILE, units), lambda i: (0, i, 0)),
            pl.BlockSpec((1, TILE), lambda i: (0, i)),
            pl.BlockSpec(w_in.shape, lambda i: (0, 0, 0)),
            pl.BlockSpec(w_out.shape, lambda i: (0, 0, 0)),
        ],
        out_specs=[
            pl.BlockSpec((depth + STEP, TILE), lambda i: (0, i)),
            pl.BlockSpec((depth, TILE), lambda i: (0, i)),
            pl.BlockSpec((outs, units, TILE), lambda i: (0, 0, i)),
            pl.BlockSpec((pairs, packed, units), lambda i: (0, 0, 0)),
            pl.BlockSpec(TOKEN, lambda i: (0, 0)),
        ],
        out_shape=[
            jax.ShapeDtypeStruct((depth + STEP, rows), BF16),
            jax.ShapeDtypeStruct((depth, rows), BF16),
            jax.ShapeDtypeStruct((outs, units, rows), F32),
            jax.ShapeDtypeStruct((pairs, packed, units), F32),
            jax.ShapeDtypeStruct(TOKEN, F32),
        ],
        compiler_params=pltpu.CompilerParams(vmem_limit_bytes=VMEM_BYTES),
        cost_estimate=pl.CostEstimate(flops=0, bytes_accessed=32000000, transcendentals=0),
    )(features, cotangent, valid, w_in, w_out)


def softmax_rows(v):
    e = jnp.exp(v - jnp.max(v, axis=0, keepdims=True))
    return e / jnp.sum(e, axis=0, keepdims=True)


def expert_kernel(group, first, last, n_after, partial, *refs):
    used = sorted({o for e in group for o, _ in uses(e)})
    names = ["core", "own", "other"] + ([] if first else ["small"]) + ["xh", "xl"]
    names += [f"c{o}" for o in used]
    names += [] if first else ["prob"]
    if last:
        names += [f"dp{k}" for k in range(len(GROUPS) - 1)]
    names += [f"in{o}" for o in partial]
    names += [f"after{k}" for k in range(n_after)]
    names += [f"{name}{l}" for name in ("dah", "dal") for l in range(len(group))]
    names += ["out"] if last else [f"out{o}" for o in used]
    names += ["wih", "wil"]
    names += ["keep", "send"] if last else ["grads"]
    if first:
        names += ["prob", "small", "gates"]
    names += ["dl"] if last else ["dp"]
    names += ["done"]
    each = ["win_t", "wp", "wp_t", "b_in", "b_out", "acc_w", "acc_g"]
    each += ["h", "u", "a", "xhat", "h2", "g", "ex", "xhh", "xhl", "dzh", "dzl"]
    names += [f"{name}{l}" for name in each for l in range(len(group))]
    if last:
        names += ["all_dp", "acc_gate"] + [f"mix{o}" for o in used]
    r = dict(zip(names, refs, strict=True))
    for name in (*each, "dah", "dal"):
        r[name] = [r[f"{name}{l}"] for l in range(len(group))]
    step = pl.program_id(0)
    count = len(group)
    units = r["acc_w"][0].shape[1]
    depth = r["xl"].shape[0]
    pairs = r["own"].shape[0]
    devices = 2 * pairs
    rows_in, rows_out = depth // devices, units // devices
    rows_all = rows_in + rows_out
    core = r["core"][0]
    tile = r["xl"].shape[1]
    chunks = [slice(k, k + STEP) for k in range(0, units, STEP)]

    @pl.when(step == 0)
    def _():
        if first:
            begin = count * rows_all
            r["small"][...] = jnp.zeros_like(r["small"])
            r["gates"][...] = jnp.zeros_like(r["gates"])
            for q in range(pairs):
                block, offset = divmod(2 * q * rows_in, units)
                lanes = slice(block * units, (block + 1) * units)
                for src, at in ((r["own"], core), (r["other"], 1 - core)):
                    piece = src[q, begin : begin + 4 * EXPERTS]
                    r["small"][...] += pltpu.roll(piece, (2 * q + at) * rows_out, 1)
                    piece = src[q, begin + 4 * EXPERTS : begin + 4 * EXPERTS + GATES]
                    r["gates"][:, lanes] += pltpu.roll(piece, offset + at * rows_in, 1)
        for l, e in enumerate(group):
            base = l * rows_all
            for q in range(pairs):
                for src, at in ((r["own"], core), (r["other"], 1 - core)):
                    place = q * 2 + at
                    r["acc_w"][l][pl.ds(place * rows_in, rows_in)] = src[q, base : base + rows_in]
                    r["acc_g"][l][pl.ds(place * rows_out, rows_out)] = src[
                        q, base + rows_in : base + rows_all
                    ]
            w_in = r["acc_w"][l][0:depth]
            high, low = halves(w_in)
            r["wih"][l] = high
            r["wil"][l] = low
            high, low = halves((0.5 * w_in).T)
            top = r["win_t"][l].shape[0] // 2
            r["win_t"][l][0:units] = high
            r["win_t"][l][top : top + units] = low
            w_out = r["acc_g"][l][0:units]
            b_in, gain, shift, b_out = (r["small"][k * EXPERTS + e : k * EXPERTS + e + 1] for k in range(4))
            scaled = w_out * wide(column(gain), units)
            high, low = halves(scaled)
            r["wp"][l][0:units] = high
            r["wp"][l][units:] = low
            high, low = halves((0.5 * scaled).T)
            r["wp_t"][l][0:units] = high
            r["wp_t"][l][units:] = low
            b_out = b_out + jnp.sum(w_out * wide(column(shift), units), axis=0, keepdims=True)
            r["b_in"][l][...] = column(0.5 * b_in)
            r["b_out"][l][...] = column(0.5 * b_out)
            r["xhh"][l][units:] = jnp.ones((STEP, tile), BF16)
        if first:
            high, low = halves(r["gates"][...])
            top = r["win_t"][0].shape[0] // 2
            r["win_t"][0][units:top] = high
            r["win_t"][0][top + units :] = low
            for l in range(1, count):
                r["win_t"][l][units:top] = high
                r["win_t"][l][top + units :] = low
        for l in range(count):
            r["acc_w"][l][...] = jnp.zeros_like(r["acc_w"][l])
            r["acc_g"][l][...] = jnp.zeros_like(r["acc_g"][l])
        r["done"][...] = jnp.zeros_like(r["done"])
        if last:
            r["acc_gate"][...] = jnp.zeros_like(r["acc_gate"])

    stats = {}

    spans = [slice(k, k + SPAN) for k in range(0, tile, SPAN)]
    zero = jnp.zeros((STEP, SPAN), F32)

    def project_in(l, s):
        r["h"][l][:, s] = dot3_stacked(r["win_t"][l], r["xh"][0:depth, s], r["xl"][:, s])

    def gate_weights(s):
        z = r["h"][0][units:, s]
        for lower, upper in ((0, 4), (4, 8), (8, 14)):
            r["prob"][lower:upper, s] = softmax_rows(z[lower:upper])
        r["prob"][14:16, s] = jnp.zeros((2, SPAN), F32)

    def normalise(l, s):
        total = zero
        for c in chunks:
            h = r["h"][l][c, s] + wide(r["b_in"][l][c], SPAN)
            u = 1.0 + jnp.tanh(h)
            a = h * u
            r["u"][l][c, s] = u
            r["a"][l][c, s] = a
            total = total + a
        mean = jnp.sum(total, axis=0, keepdims=True) * (1.0 / units)
        total = zero
        for c in chunks:
            d = r["a"][l][c, s] - mean
            total = total + d * d
        scale = lax.rsqrt(jnp.sum(total, axis=0, keepdims=True) * (1.0 / units) + EPSILON)
        stats[l, s.start] = scale
        for c in chunks:
            x = (r["a"][l][c, s] - mean) * scale
            r["xhat"][l][c, s] = x
            r["xhh"][l][c, s], r["xhl"][l][c, s] = halves(x)

    def project_out(l, s):
        r["h2"][l][:, s] = dot3_stacked(r["wp_t"][l], r["xhh"][l][0:units, s], r["xhl"][l][:, s])

    def combine(l, s):
        taken = uses(group[l])
        prob = [0.5 * r["prob"][row : row + 1, s] for _, row in taken]
        sums = [zero for _ in taken]
        end = l == count - 1
        full = [[r["prob"][row : row + 1, s] for _, row in uses(e)] for e in group] if end else None
        for c in chunks:
            h = r["h2"][l][c, s] + wide(r["b_out"][l][c], SPAN)
            u = 1.0 + jnp.tanh(h)
            ex = h * u
            if not end:
                r["ex"][l][c, s] = ex
            slope = u + ex * (2.0 - u)
            d = None
            for k, (o, _) in enumerate(taken):
                cot = r[f"c{o}"][0, c, s]
                sums[k] = sums[k] + cot * ex
                term = prob[k] * cot
                d = term if d is None else d + term
                if end:
                    mix = full[l][k] * ex
                    for m in range(l):
                        mix = mix + full[m][k] * r["ex"][m][c, s]
                    if o in partial:
                        mix = mix + r[f"in{o}"][c, s]
                    if last:
                        r[f"mix{o}"][c, s] = mix
                    else:
                        r[f"out{o}"][c, s] = mix
            r["dzh"][l][c, s], r["dzl"][l][c, s] = halves(d * slope)
        for k, (_, row) in enumerate(taken):
            value = jnp.sum(sums[k], axis=0, keepdims=True)
            if last:
                r["all_dp"][row : row + 1, s] = value
            else:
                at = l * len(taken) + k
                r["dp"][at : at + 1, s] = value

    def back_out(l, s):
        r["g"][l][:, s] = dot3_stacked(r["wp"][l], r["dzh"][l][:, s], r["dzl"][l][:, s])

    def grad_out(l):
        r["acc_g"][l][...] += dot(r["xhh"][l][...], r["dzh"][l][...], NT) + dot(
            r["xhh"][l][...], r["dzl"][l][...], NT
        )
        r["acc_g"][l][0:units] += dot(r["xhl"][l][...], r["dzh"][l][...], NT)

    def back_norm(l, s):
        total, along = zero, zero
        for c in chunks:
            g = r["g"][l][c, s]
            total = total + g
            along = along + g * r["xhat"][l][c, s]
        mean = jnp.sum(total, axis=0, keepdims=True) * (1.0 / units)
        along = jnp.sum(along, axis=0, keepdims=True) * (1.0 / units)
        scale = 0.5 * stats[l, s.start]
        for c in chunks:
            u, a = r["u"][l][c, s], r["a"][l][c, s]
            slope = (u + a * (2.0 - u)) * scale
            da = (r["g"][l][c, s] - mean - r["xhat"][l][c, s] * along) * slope
            r["dah"][l][c, s], r["dal"][l][c, s] = halves(da)

    def grad_in(l):
        high, low = r["dah"][l][...], r["dal"][l][...]
        r["acc_w"][l][...] += dot(r["xh"][...], high, NT) + dot(r["xh"][...], low, NT)
        r["acc_w"][l][0:depth] += dot(r["xl"][...], high, NT)

    chains = [(l, s) for l in range(count) for s in spans]
    for stage in ORDER:
        if isinstance(stage, tuple):
            name, k = stage
            if name == "go":
                grad_out(k)
            elif name == "gi":
                grad_in(k)
            else:
                at = {
                    "in": project_in, "norm": normalise, "out": project_out, "comb": combine, "back": back_out,
                    "bnorm": back_norm,
                }[name]
                at(*chains[k])
                if name == "in" and first and chains[k][0] == 0:
                    gate_weights(chains[k][1])

    if last:
        for o in used:
            r["out"][o] = r[f"mix{o}"][...].T
    if last:
        for k, g in enumerate(GROUPS[:-1]):
            at = 0
            for e in g:
                for _, row in uses(e):
                    r["all_dp"][row : row + 1] = r[f"dp{k}"][at : at + 1]
                    at += 1
        for lower, upper in ((0, 4), (4, 8), (8, 14)):
            p, d = r["prob"][lower:upper], r["all_dp"][lower:upper]
            r["dl"][lower:upper] = p * (d - jnp.sum(p * d, axis=0, keepdims=True))
        r["dl"][14:16] = jnp.zeros((2, tile), F32)
        high, low = halves(r["dl"][...])
        both = dot(r["xh"][0:depth], jnp.concatenate([high, low], 0), NT)
        r["acc_gate"][:, 0:GATES] += both[:, 0:GATES] + both[:, GATES:] + dot(r["xl"][...], high, NT)

    @pl.when(step == pl.num_programs(0) - 1)
    def _():
        for l in range(count):
            base = l * (rows_all + 8)
            tail = jnp.concatenate([r["acc_g"][l][units : units + 1], r["acc_w"][l][depth : depth + 1]], 0)
            tail = jnp.concatenate([tail] * 4, 0)
            if last:
                places = [
                    (dst, q, q * 2 + at)
                    for q in range(pairs)
                    for dst, at in ((r["keep"], core), (r["send"], 1 - core))
                ]
            else:
                places = [(r["grads"], k, k) for k in range(devices)]
            for dst, q, place in places:
                dst[q, base : base + rows_in] = r["acc_w"][l][pl.ds(place * rows_in, rows_in)]
                dst[q, base + rows_in : base + rows_all] = r["acc_g"][l][pl.ds(place * rows_out, rows_out)]
                dst[q, base + rows_all : base + rows_all + 8] = tail
        if last:
            gate = r["acc_gate"][...].T[0:GATES]
            base = count * (rows_all + 8)
            for q in range(pairs):
                even = gate[:, 2 * q * rows_in : (2 * q + 1) * rows_in]
                odd = gate[:, (2 * q + 1) * rows_in : (2 * q + 2) * rows_in]
                for dst, at in ((r["keep"], core), (r["send"], 1 - core)):
                    dst[q, base:, 0:rows_in] = jnp.where(at == 0, even, odd)


def expert_call(group, core, own, other, small, xh, xl, ct, prob, dps, last, after, skip, mixed):
    first = small is None
    pairs, _, units = own.shape
    depth, rows = xl.shape
    devices = 2 * pairs
    rows_in, rows_out = depth // devices, units // devices
    count = len(group)
    whole = lambda shape: pl.BlockSpec(shape, lambda i: (0,) * len(shape))
    along = lambda n: pl.BlockSpec((n, TILE), lambda i: (0, i))
    used = sorted({o for e in group for o, _ in uses(e)})
    ins = [core, own, other] + ([] if first else [small]) + [xh, xl] + [ct] * len(used)
    held = own.shape[1] if first else count * (rows_in + rows_out)
    weights = pl.BlockSpec((pairs, held, units), lambda i: (0, skip, 0))
    in_specs = [
        pl.BlockSpec(memory_space=pltpu.SMEM),
        weights,
        weights,
        *([] if first else [whole((4 * EXPERTS, units))]),
        along(xh.shape[0]),
        along(depth),
    ]
    in_specs += [pl.BlockSpec((1, units, TILE), lambda i, o=o: (o, 0, i)) for o in used]
    if not first:
        ins.append(prob)
        in_specs.append(along(GATES))
    if last:
        ins += dps
        in_specs += [along(8)] * len(dps)
    ins += [mixed[o] for o in sorted(mixed)]
    in_specs += [along(units)] * len(mixed)
    ins += after
    in_specs += [pl.BlockSpec(memory_space=pltpu.HBM)] * len(after)
    packed = count * (rows_in + rows_out + 8)
    shape = jax.ShapeDtypeStruct
    if last:
        mixes = [
            (pl.BlockSpec((len(used), TILE, units), lambda i: (0, i, 0)), shape((len(used), rows, units), F32))
        ]
    else:
        mixes = [(along(units), shape((units, rows), F32))] * len(used)
    outs = [
        *[(along(units), shape((units, rows), BF16))] * (2 * count),
        *mixes,
        (whole((count, depth, units)), shape((count, depth, units), BF16)),
        (whole((count, depth, units)), shape((count, depth, units), BF16)),
    ]
    if last:
        packed += GATES
        outs += [(whole((pairs, packed, units)), shape((pairs, packed, units), F32))] * 2
    else:
        outs.append((whole((devices, packed, units)), shape((devices, packed, units), F32)))
    if first:
        outs.append((along(GATES), shape((GATES, rows), F32)))
        outs += [
            (whole((n, lanes)), shape((n, lanes), F32)) for n, lanes in ((4 * EXPERTS, units), (GATES, depth))
        ]
    if last:
        outs.append((along(GATES), shape((GATES, rows), F32)))
    else:
        outs.append((along(8), shape((8, rows), F32)))
    outs.append((whole(TOKEN), shape(TOKEN, F32)))
    top = units + (GATES if first else 0)
    kinds = [
        ((2 * top, depth), BF16),
        ((2 * units, units), BF16),
        ((2 * units, units), BF16),
        ((units, LANES), F32),
        ((units, LANES), F32),
        ((depth + STEP, units), F32),
        ((units + STEP, units), F32),
        ((top, TILE), F32),
        ((units, TILE), F32),
        ((units, TILE), F32),
        ((units, TILE), F32),
        ((units, TILE), F32),
        ((units, TILE), F32),
        ((units, TILE), F32),
        ((units + STEP, TILE), BF16),
        ((units, TILE), BF16),
        ((units, TILE), BF16),
        ((units, TILE), BF16),
    ]
    scratch = [pltpu.VMEM(*kind) for kind in kinds for _ in group]
    if last:
        scratch += [pltpu.VMEM((GATES, TILE), F32), pltpu.VMEM((depth, LANES), F32)]
        scratch += [pltpu.VMEM((units, TILE), F32)] * len(used)
    return pl.pallas_call(
        functools.partial(expert_kernel, group, first, last, len(after), tuple(sorted(mixed))),
        grid=(rows // TILE,),
        in_specs=in_specs,
        out_specs=[o[0] for o in outs],
        out_shape=[o[1] for o in outs],
        scratch_shapes=scratch,
        compiler_params=pltpu.CompilerParams(vmem_limit_bytes=58 << 20),
        cost_estimate=pl.CostEstimate(
            flops=20000000000 * count // 2, bytes_accessed=30000000, transcendentals=0
        ),
    )(*ins)


def final_kernel(steps, *refs):
    n = EXPERTS
    dahs, dals = refs[:n], refs[n : 2 * n]
    wihs, wils = refs[2 * n : 2 * n + len(GROUPS)], refs[2 * n + len(GROUPS) : 2 * n + 2 * len(GROUPS)]
    dl_ref, gates_ref = refs[2 * n + 2 * len(GROUPS) : 2 * n + 2 * len(GROUPS) + 2]
    gf_ref, done_ref, gate_ref = refs[-3:]
    done_ref[...] = jnp.zeros_like(done_ref)

    @pl.when(pl.program_id(0) == 0)
    def _():
        high, low = halves(gates_ref[...])
        gate_ref[0:GATES] = high
        gate_ref[GATES : 2 * GATES] = low
        gate_ref[2 * GATES :] = high

    for k in range(0, TILE, SPAN):
        span = slice(k, k + SPAN)
        high, low = halves(dl_ref[:, span])
        value = dot(gate_ref[...], jnp.concatenate([high, high, low], 0), TN)
        at = 0
        for k, group in enumerate(GROUPS):
            for l in range(len(group)):
                value = value + dot3(wihs[k][l], wils[k][l], dahs[at][:, span], dals[at][:, span], NN)
                at += 1
        gf_ref[span] = value.T


def final_call(dahs, dals, wihs, wils, dl, gates, part, before, after):
    rows = dl.shape[1]
    _, depth, units = wihs[0].shape
    tiles = rows // TILE
    skip, end = (tiles * k // PARTS for k in (part, part + 1))
    steps, parts = end - skip, PARTS
    whole = lambda a: pl.BlockSpec(a.shape, lambda i: (0,) * a.ndim)
    along = lambda a: pl.BlockSpec((a.shape[0], TILE), lambda i: (0, i + skip))
    ins = [*dahs, *dals, *wihs, *wils, dl, gates, *before, *after]
    n = 2 * EXPERTS + 2 * len(GROUPS) + 2
    return pl.pallas_call(
        functools.partial(final_kernel, steps),
        grid=(steps,),
        in_specs=[along(a) for a in (*dahs, *dals)]
        + [whole(a) for a in (*wihs, *wils)]
        + [along(dl), whole(gates)]
        + [pl.BlockSpec(memory_space=pltpu.HBM)] * (len(before) + len(after)),
        out_specs=[pl.BlockSpec((TILE, depth), lambda i: (i + skip, 0)), pl.BlockSpec(TOKEN, lambda i: (0, 0))],
        out_shape=[jax.ShapeDtypeStruct((rows, depth), F32), jax.ShapeDtypeStruct(TOKEN, F32)],
        scratch_shapes=[pltpu.VMEM((3 * GATES, depth), BF16)],
        input_output_aliases={n + k: k for k in range(len(before))},
        compiler_params=pltpu.CompilerParams(vmem_limit_bytes=58 << 20),
        cost_estimate=pl.CostEstimate(
            flops=15000000000 // parts, bytes_accessed=25000000 // parts, transcendentals=0
        ),
    )(*ins)


def finish_kernel(me_ref, *refs):
    n = len(GROUPS) + 1
    w_out_ref, gain_ref, shift_ref = refs[n : n + 3]
    g_in, g_in_bias, g_gain, g_shift, g_out, g_out_bias, g_task, g_shared = refs[n + 3 :]
    rows_in, rows_out, units = g_in.shape[1], g_out.shape[1], g_in.shape[2]
    me = me_ref[0]

    def own(row):
        value = row[:, 0:rows_out]
        for p in range(1, units // rows_out):
            value = jnp.where(me == p, row[:, p * rows_out : (p + 1) * rows_out], value)
        return value

    def as_row(col):
        return jnp.broadcast_to(col, (rows_out, LANES)).T[0:1]

    for k, group in enumerate(GROUPS):
        if k < len(GROUPS) - 1:
            add = lambda lower, upper, a=refs[k]: a[lower:upper]
        else:
            add = lambda lower, upper, a=refs[k], b=refs[k + 1]: a[lower:upper] + b[lower:upper]
        at = 0
        for e in group:
            g_in[e] = add(at, at + rows_in)
            at += rows_in
            raw = add(at, at + rows_out)
            at += rows_out
            tail = add(at, at + 8)
            at += 8
            total = tail[0:1]
            gain = wide(column(gain_ref[e : e + 1]), units)
            shift = wide(column(shift_ref[e : e + 1]), units)
            g_out[e] = gain * raw + shift * total
            w = w_out_ref[e]
            g_gain[e : e + 1] = as_row(jnp.sum(w * raw, axis=1, keepdims=True))
            g_shift[e : e + 1] = as_row(jnp.sum(w * total, axis=1, keepdims=True))
            g_in_bias[e : e + 1] = own(tail[1:2])
            g_out_bias[e : e + 1] = own(total)
    gate = add(at, at + GATES)[:, 0:rows_in]
    m = SPEC + SHARED
    for t in range(TASKS):
        g_task[t] = gate[t * m : (t + 1) * m]
    g_shared[...] = gate[TASKS * m : TASKS * m + EXPERTS]


def finish(me, totals, w_in, w_out, gain, shift):
    experts, rows_in, units = w_in.shape
    rows_out = w_out.shape[1]
    shape = lambda *s: jax.ShapeDtypeStruct(s, F32)
    vector = shape(experts, rows_out)
    outs = [
        shape(*w_in.shape),
        vector,
        vector,
        vector,
        shape(*w_out.shape),
        vector,
        shape(TASKS, SPEC + SHARED, rows_in),
        shape(EXPERTS, rows_in),
    ]
    vmem = pl.BlockSpec(memory_space=pltpu.VMEM)
    got = pl.pallas_call(
        finish_kernel,
        in_specs=[pl.BlockSpec(memory_space=pltpu.SMEM)] + [vmem] * (len(totals) + 3),
        out_specs=[vmem] * len(outs),
        out_shape=outs,
        compiler_params=pltpu.CompilerParams(vmem_limit_bytes=16 << 20),
    )(me, *totals, w_out, gain, shift)
    return (*got[:6], got[6].transpose(0, 2, 1), got[7].T)


def make(mesh):
    n_fsdp, n_dp = mesh.shape["fsdp"], mesh.shape["dp"]
    pairs = n_fsdp // 2
    across = [[q * 2 + c for q in range(pairs)] for c in range(2)]
    twin = [(i, i ^ 1) for i in range(n_fsdp)]

    def spread_out(x):
        return lax.all_to_all(x, "fsdp", 0, 0, axis_index_groups=across)

    def swap(x, bit):
        return lax.ppermute(x, "dp", [(i, i ^ bit) for i in range(n_dp)])

    def reduce_some(x, token, some, beside):
        for bit in some:
            x, token = total([x, swap(x, bit)], beside)
        return x, token

    bits = [1 << k for k in range(n_dp.bit_length() - 1)]

    def on_device(
        features, cotangent, counts, keep, w_in, in_bias, norm_gain, norm_bias, w_out, out_bias, task_gate, shared_gate
    ):
        rows = features.shape[0]
        depth = features.shape[1]
        experts, rows_in, units = w_in.shape
        rows_out = w_out.shape[1]
        valid = (lax.broadcasted_iota(jnp.int32, (1, rows), 1) < counts[0]) & (keep.reshape(1, rows) > 0)
        me = lax.axis_index("fsdp")
        core = (me % 2).astype(jnp.int32).reshape(1)
        xh, xl, ct, spread, done = prep(features, cotangent, valid.astype(F32), w_in, w_out, pairs)
        own0 = tie(
            spread_out(
                pack(pairs, w_in, in_bias, norm_gain, norm_bias, w_out, out_bias, task_gate, shared_gate)
            ),
            [done],
        )
        other0 = lax.ppermute(own0, "fsdp", twin)
        def parts_of(got, group):
            n = len(group)
            m = 1 if group == GROUPS[-1] else len({o for e in group for o, _ in uses(e)})
            return got[:n], got[n : 2 * n], got[2 * n : 2 * n + m], got[2 * n + m :]

        got = expert_call(GROUPS[0], core, own0, other0, None, xh, xl, ct, None, [], False, [], 0, {})
        dah0, dal0, mix0, (wih0, wil0, grads0, prob, small, gates, dp0, done0) = parts_of(got, GROUPS[0])
        own1 = tie(spread_out(spread), [done0])
        other1 = lax.ppermute(own1, "fsdp", twin)
        got = expert_call(
            GROUPS[1], core, own1, other1, small, xh, xl, ct, prob, [], False, [], 0, {2: mix0[1]}
        )
        dah1, dal1, mix1, (wih1, wil1, grads1, dp1, done1) = parts_of(got, GROUPS[1])
        sum0, token0 = total([lax.all_to_all(grads0, "fsdp", 0, 0)], [done1])
        got = expert_call(
            GROUPS[2],
            core,
            own1,
            other1,
            small,
            xh,
            xl,
            ct,
            prob,
            [dp0, dp1],
            True,
            [token0],
            1,
            {0: mix0[0], 1: mix1[0], 2: mix1[1]},
        )
        dah2, dal2, (outputs,), (wih2, wil2, keep2, send2, dl, done2) = parts_of(got, GROUPS[2])
        sum1, token1 = total([lax.all_to_all(grads1, "fsdp", 0, 0)], [done2])
        sum0, token0 = reduce_some(sum0, token0, bits[:-1], [done2])
        kept = keep2 + lax.ppermute(tie(send2, [token0, token1]), "fsdp", twin)
        tail = (
            (*dah0, *dah1, *dah2),
            (*dal0, *dal1, *dal2),
            (wih0, wih1, wih2),
            (wil0, wil1, wil2),
            dl,
            gates,
        )
        part, done3 = final_call(*tail, 0, [], [])
        sum2, token2 = total([spread_out(kept)], [done3])
        sum1, token1 = reduce_some(sum1, token1, bits[:-1], [done3])
        part, done4 = final_call(*tail, 1, [part], [token1, token2])
        sum0, token0 = total([sum0, swap(sum0, bits[-1])], [done4])
        sum2, token2 = reduce_some(sum2, token2, bits[:-1], [done4])
        grad_features, done5 = final_call(*tail, 2, [part], [token0, token2])
        sum1, token1 = total([sum1, swap(sum1, bits[-1])], [done5])
        pair2 = (sum2, swap(sum2, bits[-1]))
        rest = finish(me.astype(jnp.int32).reshape(1), (sum0, sum1, *pair2), w_in, w_out, norm_gain, norm_bias)
        return (outputs, grad_features, *rest)

    return on_device


def solution(mesh):
    placed = (
        P(("dp", "fsdp"), None),
        P(None, ("dp", "fsdp"), None),
        P(("dp", "fsdp")),
        P(("dp", "fsdp")),
        P(None, "fsdp", None),
        P(None, "fsdp"),
        P(None, "fsdp"),
        P(None, "fsdp"),
        P(None, "fsdp", None),
        P(None, "fsdp"),
        P(None, "fsdp", None),
        P("fsdp", None),
    )
    return jax.shard_map(
        make(mesh),
        mesh=mesh,
        in_specs=placed,
        out_specs=(
            P(None, ("dp", "fsdp"), None),
            P(("dp", "fsdp"), None),
            P(None, "fsdp", None),
            P(None, "fsdp"),
            P(None, "fsdp"),
            P(None, "fsdp"),
            P(None, "fsdp", None),
            P(None, "fsdp"),
            P(None, "fsdp", None),
            P("fsdp", None),
        ),
        check_vma=False,
    )
```

```python
import functools

import jax
import jax.numpy as jnp
from jax import lax
from jax.experimental import pallas as pl
from jax.experimental.pallas import tpu as pltpu
from jax.sharding import PartitionSpec as P

TASKS = 2
SPEC = 2
SHARED = 2
EXPERTS = 6
EPSILON = 1e-05
GROUPS = ((0, 1), (2, 3), (4, 5))
TILE = 512
STEP = 16
PARTS = 3
TOKEN = (8, 128)
SPAN = 256
ORDER = (('in', 0), ('in', 1), ('norm', 0), ('in', 2), ('norm', 1), ('in', 3), ('out', 0), ('norm', 2), ('out', 1), ('norm', 3), ('comb', 0), ('out', 2), ('comb', 1), ('out', 3), ('back', 0), ('comb', 2), ('back', 1), ('comb', 3), ('go', 0), ('bnorm', 0), ('back', 2), ('bnorm', 1), ('back', 3), ('gi', 0), ('bnorm', 2), ('go', 1), ('bnorm', 3), ('gi', 1))
LANES = 128
GATES = 16
F32 = jnp.float32
BF16 = jnp.bfloat16
VMEM_BYTES = 58 << 20

NN = (((1,), (0,)), ((), ()))
NT = (((1,), (1,)), ((), ()))
TN = (((0,), (0,)), ((), ()))


def uses(expert):
    if expert >= TASKS * SPEC:
        shared = expert - TASKS * SPEC
        first = [(t, t * (SPEC + SHARED) + SPEC + shared) for t in range(TASKS)]
    else:
        t = expert // SPEC
        first = [(t, t * (SPEC + SHARED) + expert % SPEC)]
    return first + [(TASKS, TASKS * (SPEC + SHARED) + expert)]


def halves(v):
    high = v.astype(BF16)
    return high, (v - high.astype(F32)).astype(BF16)


def dot(a, b, dims):
    return lax.dot_general(a, b, dims, preferred_element_type=F32)


def dot3(a_high, a_low, b_high, b_low, dims):
    return dot(a_high, b_high, dims) + dot(a_low, b_high, dims) + dot(a_high, b_low, dims)


def dot3_stacked(both, b_high, b_low):
    n = both.shape[0] // 2
    product = dot(both[...], b_high, NN)
    return product[0:n] + product[n:] + dot(both[0:n], b_low, NN)


def column(row):
    return jnp.broadcast_to(row, (LANES, row.shape[1])).T


def wide(block, width):
    return jnp.concatenate([block] * (width // LANES), axis=1)


def tie(x, after):
    return pl.pallas_call(
        lambda *refs: None,
        in_specs=[pl.BlockSpec(memory_space=pl.ANY)] + [pl.BlockSpec(memory_space=pltpu.HBM)] * len(after),
        out_specs=pl.BlockSpec(memory_space=pl.ANY),
        out_shape=jax.ShapeDtypeStruct(x.shape, x.dtype),
        input_output_aliases={0: 0},
    )(x, *after)


def total_kernel(n, *refs):
    value = None
    for ref in refs[:n]:
        for part in [ref[...]] if len(ref.shape) == 2 else [ref[k] for k in range(ref.shape[0])]:
            value = part if value is None else value + part
    refs[-2][...] = value
    refs[-1][...] = jnp.zeros_like(refs[-1])


def total(arrays, after):
    vmem = pl.BlockSpec(memory_space=pltpu.VMEM)
    return pl.pallas_call(
        functools.partial(total_kernel, len(arrays)),
        in_specs=[vmem] * len(arrays) + [pl.BlockSpec(memory_space=pltpu.HBM)] * len(after),
        out_specs=[vmem, vmem],
        out_shape=[jax.ShapeDtypeStruct(arrays[0].shape[-2:], F32), jax.ShapeDtypeStruct(TOKEN, F32)],
        compiler_params=pltpu.CompilerParams(vmem_limit_bytes=16 << 20),
    )(*arrays, *after)


def used_by(group):
    return sorted({o for e in group for o, _ in uses(e)})


def pack_weights(groups, w_in_ref, w_out_ref, to_ref):
    rows_in, rows_out = w_in_ref.shape[1], w_out_ref.shape[1]
    at = 0
    for e in (e for group in groups for e in group):
        for q in range(to_ref.shape[0]):
            to_ref[q, at : at + rows_in] = w_in_ref[e]
            to_ref[q, at + rows_in : at + rows_in + rows_out] = w_out_ref[e]
        at += rows_in + rows_out
    return at


def pack_kernel(in_bias, gain, shift, out_bias, task_gate, shared_gate, w_in_ref, w_out_ref, to_ref):
    rows_in, rows_out = w_in_ref.shape[1], w_out_ref.shape[1]
    at = pack_weights(GROUPS[:1], w_in_ref, w_out_ref, to_ref)
    n = SPEC + SHARED
    for q in range(to_ref.shape[0]):
        to_ref[q, at:] = jnp.zeros((to_ref.shape[1] - at, to_ref.shape[2]), F32)
        for k, bias in enumerate((in_bias, gain, shift, out_bias)):
            to_ref[q, at + k * EXPERTS : at + (k + 1) * EXPERTS, 0:rows_out] = bias[...]
        base = at + 4 * EXPERTS
        for t in range(TASKS):
            to_ref[q, base + t * n : base + (t + 1) * n, 0:rows_in] = task_gate[t]
        base += TASKS * n
        to_ref[q, base : base + EXPERTS, 0:rows_in] = shared_gate[...]


def pack(pairs, w_in, in_bias, gain, shift, w_out, out_bias, task_gate, shared_gate):
    rows = len(GROUPS[0]) * (w_in.shape[1] + w_out.shape[1]) + 4 * EXPERTS + GATES
    return pl.pallas_call(
        pack_kernel,
        out_shape=jax.ShapeDtypeStruct((pairs, rows, w_in.shape[2]), F32),
        compiler_params=pltpu.CompilerParams(vmem_limit_bytes=VMEM_BYTES),
    )(in_bias, gain, shift, out_bias, task_gate.transpose(0, 2, 1), shared_gate.T, w_in, w_out)


def prep_kernel(x_ref, c_refs, valid_ref, w_in_ref, w_out_ref, xh_ref, xl_ref, ct_ref, to_ref, done_ref):
    depth = x_ref.shape[1]

    @pl.when(pl.program_id(0) == 0)
    def _():
        pack_weights(GROUPS[1:], w_in_ref, w_out_ref, to_ref)
        done_ref[...] = jnp.zeros_like(done_ref)

    high, low = halves(x_ref[...].T)
    xh_ref[0:depth] = high
    xh_ref[depth:] = jnp.ones((xh_ref.shape[0] - depth, xh_ref.shape[1]), BF16)
    xl_ref[...] = low
    valid = valid_ref[...]
    for k, c_ref in enumerate(c_refs):
        ct_ref[k] = c_ref[0].T * valid


def prep(features, cotangent, valid, w_in, w_out, pairs):
    rows, depth = features.shape
    packed = sum(len(g) for g in GROUPS[1:]) * (w_in.shape[1] + w_out.shape[1])
    units = cotangent.shape[2]
    used = used_by(GROUPS[0])
    outs = len(used)
    return pl.pallas_call(
        prep_kernel,
        grid=(rows // TILE,),
        in_specs=[
            pl.BlockSpec((TILE, depth), lambda i: (i, 0)),
            [pl.BlockSpec((1, TILE, units), lambda i, o=o: (o, i, 0)) for o in used],
            pl.BlockSpec((1, TILE), lambda i: (0, i)),
            pl.BlockSpec(w_in.shape, lambda i: (0, 0, 0)),
            pl.BlockSpec(w_out.shape, lambda i: (0, 0, 0)),
        ],
        out_specs=[
            pl.BlockSpec((depth + STEP, TILE), lambda i: (0, i)),
            pl.BlockSpec((depth, TILE), lambda i: (0, i)),
            pl.BlockSpec((outs, units, TILE), lambda i: (0, 0, i)),
            pl.BlockSpec((pairs, packed, units), lambda i: (0, 0, 0)),
            pl.BlockSpec(TOKEN, lambda i: (0, 0)),
        ],
        out_shape=[
            jax.ShapeDtypeStruct((depth + STEP, rows), BF16),
            jax.ShapeDtypeStruct((depth, rows), BF16),
            jax.ShapeDtypeStruct((outs, units, rows), F32),
            jax.ShapeDtypeStruct((pairs, packed, units), F32),
            jax.ShapeDtypeStruct(TOKEN, F32),
        ],
        compiler_params=pltpu.CompilerParams(vmem_limit_bytes=VMEM_BYTES),
        cost_estimate=pl.CostEstimate(flops=0, bytes_accessed=26000000, transcendentals=0),
    )(features, [cotangent] * outs, valid, w_in, w_out)


def softmax_rows(v):
    e = jnp.exp(v - jnp.max(v, axis=0, keepdims=True))
    return e / jnp.sum(e, axis=0, keepdims=True)


def expert_kernel(group, first, last, n_after, partial, fresh, *refs):
    used = used_by(group)
    names = ["core", "own", "other"] + ([] if first else ["small"]) + ["xh", "xl"]
    names += [f"c{o}" for o in used if o not in fresh]
    names += (["valid"] + [f"cot{o}" for o in fresh]) if fresh else []
    names += [] if first else ["prob"]
    if last:
        names += [f"dp{k}" for k in range(len(GROUPS) - 1)]
    names += [f"in{o}" for o in partial]
    names += [f"after{k}" for k in range(n_after)]
    names += [f"{name}{l}" for name in ("dah", "dal") for l in range(len(group))]
    names += ["out"] if last else [f"out{o}" for o in used]
    names += ["wih", "wil"]
    names += ["keep", "send"] if last else ["grads"]
    if first:
        names += ["prob", "small", "gates"]
    names += ["dl"] if last else ["dp"]
    names += ["done"] + [f"c{o}" for o in fresh]
    each = ["win_t", "wp", "wp_t", "b_in", "b_out", "acc_w", "acc_g"]
    each += ["h", "u", "a", "xhat", "h2", "g", "ex", "xhh", "xhl", "dzh", "dzl"]
    names += [f"{name}{l}" for name in each for l in range(len(group))]
    if last:
        names += ["all_dp", "acc_gate"] + [f"mix{o}" for o in used]
    r = dict(zip(names, refs, strict=True))
    for name in (*each, "dah", "dal"):
        r[name] = [r[f"{name}{l}"] for l in range(len(group))]
    step = pl.program_id(0)
    count = len(group)
    units = r["acc_w"][0].shape[1]
    depth = r["xl"].shape[0]
    pairs = r["own"].shape[0]
    devices = 2 * pairs
    rows_in, rows_out = depth // devices, units // devices
    rows_all = rows_in + rows_out
    core = r["core"][0]
    tile = r["xl"].shape[1]
    chunks = [slice(k, k + STEP) for k in range(0, units, STEP)]

    @pl.when(step == 0)
    def _():
        if first:
            begin = count * rows_all
            r["small"][...] = jnp.zeros_like(r["small"])
            r["gates"][...] = jnp.zeros_like(r["gates"])
            for q in range(pairs):
                block, offset = divmod(2 * q * rows_in, units)
                lanes = slice(block * units, (block + 1) * units)
                for src, at in ((r["own"], core), (r["other"], 1 - core)):
                    piece = src[q, begin : begin + 4 * EXPERTS]
                    r["small"][...] += pltpu.roll(piece, (2 * q + at) * rows_out, 1)
                    piece = src[q, begin + 4 * EXPERTS : begin + 4 * EXPERTS + GATES]
                    r["gates"][:, lanes] += pltpu.roll(piece, offset + at * rows_in, 1)
        for l, e in enumerate(group):
            base = l * rows_all
            for q in range(pairs):
                for src, at in ((r["own"], core), (r["other"], 1 - core)):
                    place = q * 2 + at
                    r["acc_w"][l][pl.ds(place * rows_in, rows_in)] = src[q, base : base + rows_in]
                    r["acc_g"][l][pl.ds(place * rows_out, rows_out)] = src[
                        q, base + rows_in : base + rows_all
                    ]
            w_in = r["acc_w"][l][0:depth]
            high, low = halves(w_in)
            r["wih"][l] = high
            r["wil"][l] = low
            high, low = halves((0.5 * w_in).T)
            top = r["win_t"][l].shape[0] // 2
            r["win_t"][l][0:units] = high
            r["win_t"][l][top : top + units] = low
            w_out = r["acc_g"][l][0:units]
            b_in, gain, shift, b_out = (r["small"][k * EXPERTS + e : k * EXPERTS + e + 1] for k in range(4))
            scaled = w_out * wide(column(gain), units)
            high, low = halves(scaled)
            r["wp"][l][0:units] = high
            r["wp"][l][units:] = low
            high, low = halves((0.5 * scaled).T)
            r["wp_t"][l][0:units] = high
            r["wp_t"][l][units:] = low
            b_out = b_out + jnp.sum(w_out * wide(column(shift), units), axis=0, keepdims=True)
            r["b_in"][l][...] = column(0.5 * b_in)
            r["b_out"][l][...] = column(0.5 * b_out)
            r["xhh"][l][units:] = jnp.ones((STEP, tile), BF16)
        if first:
            high, low = halves(r["gates"][...])
            top = r["win_t"][0].shape[0] // 2
            r["win_t"][0][units:top] = high
            r["win_t"][0][top + units :] = low
            for l in range(1, count):
                r["win_t"][l][units:top] = high
                r["win_t"][l][top + units :] = low
        for l in range(count):
            r["acc_w"][l][...] = jnp.zeros_like(r["acc_w"][l])
            r["acc_g"][l][...] = jnp.zeros_like(r["acc_g"][l])
        r["done"][...] = jnp.zeros_like(r["done"])
        if last:
            r["acc_gate"][...] = jnp.zeros_like(r["acc_gate"])

    stats = {}

    spans = [slice(k, k + SPAN) for k in range(0, tile, SPAN)]
    zero = jnp.zeros((STEP, SPAN), F32)

    def project_in(l, s):
        r["h"][l][:, s] = dot3_stacked(r["win_t"][l], r["xh"][0:depth, s], r["xl"][:, s])

    def gate_weights(s):
        z = r["h"][0][units:, s]
        for lower, upper in ((0, 4), (4, 8), (8, 14)):
            r["prob"][lower:upper, s] = softmax_rows(z[lower:upper])
        r["prob"][14:16, s] = jnp.zeros((2, SPAN), F32)

    def normalise(l, s):
        total = zero
        for c in chunks:
            h = r["h"][l][c, s] + wide(r["b_in"][l][c], SPAN)
            u = 1.0 + jnp.tanh(h)
            a = h * u
            r["u"][l][c, s] = u
            r["a"][l][c, s] = a
            total = total + a
        mean = jnp.sum(total, axis=0, keepdims=True) * (1.0 / units)
        total = zero
        for c in chunks:
            d = r["a"][l][c, s] - mean
            total = total + d * d
        scale = lax.rsqrt(jnp.sum(total, axis=0, keepdims=True) * (1.0 / units) + EPSILON)
        stats[l, s.start] = scale
        for c in chunks:
            x = (r["a"][l][c, s] - mean) * scale
            r["xhat"][l][c, s] = x
            r["xhh"][l][c, s], r["xhl"][l][c, s] = halves(x)

    def project_out(l, s):
        r["h2"][l][:, s] = dot3_stacked(r["wp_t"][l], r["xhh"][l][0:units, s], r["xhl"][l][:, s])

    def combine(l, s):
        taken = uses(group[l])
        prob = [0.5 * r["prob"][row : row + 1, s] for _, row in taken]
        sums = [zero for _ in taken]
        end = l == count - 1
        full = [[r["prob"][row : row + 1, s] for _, row in uses(e)] for e in group] if end else None
        for c in chunks:
            h = r["h2"][l][c, s] + wide(r["b_out"][l][c], SPAN)
            u = 1.0 + jnp.tanh(h)
            ex = h * u
            if not end:
                r["ex"][l][c, s] = ex
            slope = u + ex * (2.0 - u)
            d = None
            for k, (o, _) in enumerate(taken):
                cot = r[f"c{o}"][0, c, s]
                sums[k] = sums[k] + cot * ex
                term = prob[k] * cot
                d = term if d is None else d + term
                if end:
                    mix = full[l][k] * ex
                    for m in range(l):
                        mix = mix + full[m][k] * r["ex"][m][c, s]
                    if o in partial:
                        mix = mix + r[f"in{o}"][c, s]
                    if last:
                        r[f"mix{o}"][c, s] = mix
                    else:
                        r[f"out{o}"][c, s] = mix
            r["dzh"][l][c, s], r["dzl"][l][c, s] = halves(d * slope)
        for k, (_, row) in enumerate(taken):
            value = jnp.sum(sums[k], axis=0, keepdims=True)
            if last:
                r["all_dp"][row : row + 1, s] = value
            else:
                at = l * len(taken) + k
                r["dp"][at : at + 1, s] = value

    def back_out(l, s):
        r["g"][l][:, s] = dot3_stacked(r["wp"][l], r["dzh"][l][:, s], r["dzl"][l][:, s])

    def grad_out(l):
        r["acc_g"][l][...] += dot(r["xhh"][l][...], r["dzh"][l][...], NT) + dot(
            r["xhh"][l][...], r["dzl"][l][...], NT
        )
        r["acc_g"][l][0:units] += dot(r["xhl"][l][...], r["dzh"][l][...], NT)

    def back_norm(l, s):
        total, along = zero, zero
        for c in chunks:
            g = r["g"][l][c, s]
            total = total + g
            along = along + g * r["xhat"][l][c, s]
        mean = jnp.sum(total, axis=0, keepdims=True) * (1.0 / units)
        along = jnp.sum(along, axis=0, keepdims=True) * (1.0 / units)
        scale = 0.5 * stats[l, s.start]
        for c in chunks:
            u, a = r["u"][l][c, s], r["a"][l][c, s]
            slope = (u + a * (2.0 - u)) * scale
            da = (r["g"][l][c, s] - mean - r["xhat"][l][c, s] * along) * slope
            r["dah"][l][c, s], r["dal"][l][c, s] = halves(da)

    def grad_in(l):
        high, low = r["dah"][l][...], r["dal"][l][...]
        r["acc_w"][l][...] += dot(r["xh"][...], high, NT) + dot(r["xh"][...], low, NT)
        r["acc_w"][l][0:depth] += dot(r["xl"][...], high, NT)

    chains = [(l, s) for l in range(count) for s in spans]
    for o in fresh:
        r[f"c{o}"][0] = r[f"cot{o}"][0].T * r["valid"][...]
    for stage in ORDER:
        if isinstance(stage, tuple):
            name, k = stage
            if name == "go":
                grad_out(k)
            elif name == "gi":
                grad_in(k)
            else:
                at = {
                    "in": project_in, "norm": normalise, "out": project_out, "comb": combine, "back": back_out,
                    "bnorm": back_norm,
                }[name]
                at(*chains[k])
                if name == "in" and first and chains[k][0] == 0:
                    gate_weights(chains[k][1])

    if last:
        for o in used:
            r["out"][o] = r[f"mix{o}"][...].T
    if last:
        for k, g in enumerate(GROUPS[:-1]):
            at = 0
            for e in g:
                for _, row in uses(e):
                    r["all_dp"][row : row + 1] = r[f"dp{k}"][at : at + 1]
                    at += 1
        for lower, upper in ((0, 4), (4, 8), (8, 14)):
            p, d = r["prob"][lower:upper], r["all_dp"][lower:upper]
            r["dl"][lower:upper] = p * (d - jnp.sum(p * d, axis=0, keepdims=True))
        r["dl"][14:16] = jnp.zeros((2, tile), F32)
        high, low = halves(r["dl"][...])
        both = dot(jnp.concatenate([high, low], 0), r["xh"][0:depth], NT)
        r["acc_gate"][...] += both[0:GATES] + both[GATES:] + dot(high, r["xl"][...], NT)

    @pl.when(step == pl.num_programs(0) - 1)
    def _():
        for l in range(count):
            base = l * (rows_all + 8)
            tail = jnp.concatenate([r["acc_g"][l][units : units + 1], r["acc_w"][l][depth : depth + 1]], 0)
            tail = jnp.concatenate([tail] * 4, 0)
            if last:
                places = [
                    (dst, q, q * 2 + at)
                    for q in range(pairs)
                    for dst, at in ((r["keep"], core), (r["send"], 1 - core))
                ]
            else:
                places = [(r["grads"], k, k) for k in range(devices)]
            for dst, q, place in places:
                dst[q, base : base + rows_in] = r["acc_w"][l][pl.ds(place * rows_in, rows_in)]
                dst[q, base + rows_in : base + rows_all] = r["acc_g"][l][pl.ds(place * rows_out, rows_out)]
                dst[q, base + rows_all : base + rows_all + 8] = tail
        if last:
            gate = r["acc_gate"][...]
            base = count * (rows_all + 8)
            for q in range(pairs):
                even = gate[:, 2 * q * rows_in : (2 * q + 1) * rows_in]
                odd = gate[:, (2 * q + 1) * rows_in : (2 * q + 2) * rows_in]
                for dst, at in ((r["keep"], core), (r["send"], 1 - core)):
                    dst[q, base:, 0:rows_in] = jnp.where(at == 0, even, odd)


def expert_call(group, core, own, other, small, xh, xl, cts, valid, cotangent, prob, dps, last, after, skip, mixed):
    first = small is None
    pairs, _, units = own.shape
    depth, rows = xl.shape
    devices = 2 * pairs
    rows_in, rows_out = depth // devices, units // devices
    count = len(group)
    whole = lambda shape: pl.BlockSpec(shape, lambda i: (0,) * len(shape))
    along = lambda n: pl.BlockSpec((n, TILE), lambda i: (0, i))
    used = used_by(group)
    old, fresh = [o for o in used if o in cts], tuple(o for o in used if o not in cts)
    ins = [core, own, other] + ([] if first else [small]) + [xh, xl] + [cts[o][0] for o in old]
    held = own.shape[1] if first else count * (rows_in + rows_out)
    weights = pl.BlockSpec((pairs, held, units), lambda i: (0, skip, 0))
    in_specs = [
        pl.BlockSpec(memory_space=pltpu.SMEM),
        weights,
        weights,
        *([] if first else [whole((4 * EXPERTS, units))]),
        along(xh.shape[0]),
        along(depth),
    ]
    in_specs += [pl.BlockSpec((1, units, TILE), lambda i, k=cts[o][1]: (k, 0, i)) for o in old]
    if fresh:
        ins += [valid] + [cotangent] * len(fresh)
        in_specs.append(along(1))
        in_specs += [pl.BlockSpec((1, TILE, units), lambda i, o=o: (o, i, 0)) for o in fresh]
    if not first:
        ins.append(prob)
        in_specs.append(along(GATES))
    if last:
        ins += dps
        in_specs += [along(8)] * len(dps)
    ins += [mixed[o] for o in sorted(mixed)]
    in_specs += [along(units)] * len(mixed)
    ins += after
    in_specs += [pl.BlockSpec(memory_space=pltpu.HBM)] * len(after)
    packed = count * (rows_in + rows_out + 8)
    shape = jax.ShapeDtypeStruct
    if last:
        mixes = [
            (pl.BlockSpec((len(used), TILE, units), lambda i: (0, i, 0)), shape((len(used), rows, units), F32))
        ]
    else:
        mixes = [(along(units), shape((units, rows), F32))] * len(used)
    outs = [
        *[(along(units), shape((units, rows), BF16))] * (2 * count),
        *mixes,
        (whole((count, depth, units)), shape((count, depth, units), BF16)),
        (whole((count, depth, units)), shape((count, depth, units), BF16)),
    ]
    if last:
        packed += GATES
        outs += [(whole((pairs, packed, units)), shape((pairs, packed, units), F32))] * 2
    else:
        outs.append((whole((devices, packed, units)), shape((devices, packed, units), F32)))
    if first:
        outs.append((along(GATES), shape((GATES, rows), F32)))
        outs += [
            (whole((n, lanes)), shape((n, lanes), F32)) for n, lanes in ((4 * EXPERTS, units), (GATES, depth))
        ]
    if last:
        outs.append((along(GATES), shape((GATES, rows), F32)))
    else:
        outs.append((along(8), shape((8, rows), F32)))
    outs.append((whole(TOKEN), shape(TOKEN, F32)))
    outs += [
        (pl.BlockSpec((1, units, TILE), lambda i: (0, 0, i)), shape((1, units, rows), F32)) for _ in fresh
    ]
    top = units + (GATES if first else 0)
    kinds = [
        ((2 * top, depth), BF16),
        ((2 * units, units), BF16),
        ((2 * units, units), BF16),
        ((units, LANES), F32),
        ((units, LANES), F32),
        ((depth + STEP, units), F32),
        ((units + STEP, units), F32),
        ((top, TILE), F32),
        ((units, TILE), F32),
        ((units, TILE), F32),
        ((units, TILE), F32),
        ((units, TILE), F32),
        ((units, TILE), F32),
        ((units, TILE), F32),
        ((units + STEP, TILE), BF16),
        ((units, TILE), BF16),
        ((units, TILE), BF16),
        ((units, TILE), BF16),
    ]
    scratch = [pltpu.VMEM(*kind) for kind in kinds for _ in group]
    if last:
        scratch += [pltpu.VMEM((GATES, TILE), F32), pltpu.VMEM((GATES, depth), F32)]
        scratch += [pltpu.VMEM((units, TILE), F32)] * len(used)
    return pl.pallas_call(
        functools.partial(expert_kernel, group, first, last, len(after), tuple(sorted(mixed)), fresh),
        grid=(rows // TILE,),
        in_specs=in_specs,
        out_specs=[o[0] for o in outs],
        out_shape=[o[1] for o in outs],
        scratch_shapes=scratch,
        compiler_params=pltpu.CompilerParams(vmem_limit_bytes=58 << 20),
        cost_estimate=pl.CostEstimate(
            flops=20000000000 * count // 2, bytes_accessed=30000000, transcendentals=0
        ),
    )(*ins)


def final_kernel(steps, *refs):
    n = EXPERTS
    dahs, dals = refs[:n], refs[n : 2 * n]
    wihs, wils = refs[2 * n : 2 * n + len(GROUPS)], refs[2 * n + len(GROUPS) : 2 * n + 2 * len(GROUPS)]
    dl_ref, gates_ref = refs[2 * n + 2 * len(GROUPS) : 2 * n + 2 * len(GROUPS) + 2]
    gf_ref, done_ref, gate_ref = refs[-3:]
    done_ref[...] = jnp.zeros_like(done_ref)

    @pl.when(pl.program_id(0) == 0)
    def _():
        high, low = halves(gates_ref[...])
        gate_ref[0:GATES] = high
        gate_ref[GATES : 2 * GATES] = low
        gate_ref[2 * GATES :] = high

    for k in range(0, TILE, SPAN):
        span = slice(k, k + SPAN)
        high, low = halves(dl_ref[:, span])
        value = dot(gate_ref[...], jnp.concatenate([high, high, low], 0), TN)
        at = 0
        for k, group in enumerate(GROUPS):
            for l in range(len(group)):
                value = value + dot3(wihs[k][l], wils[k][l], dahs[at][:, span], dals[at][:, span], NN)
                at += 1
        gf_ref[span] = value.T


def final_call(dahs, dals, wihs, wils, dl, gates, part, before, after):
    rows = dl.shape[1]
    _, depth, units = wihs[0].shape
    tiles = rows // TILE
    skip, end = (tiles * k // PARTS for k in (part, part + 1))
    steps, parts = end - skip, PARTS
    whole = lambda a: pl.BlockSpec(a.shape, lambda i: (0,) * a.ndim)
    along = lambda a: pl.BlockSpec((a.shape[0], TILE), lambda i: (0, i + skip))
    ins = [*dahs, *dals, *wihs, *wils, dl, gates, *before, *after]
    n = 2 * EXPERTS + 2 * len(GROUPS) + 2
    return pl.pallas_call(
        functools.partial(final_kernel, steps),
        grid=(steps,),
        in_specs=[along(a) for a in (*dahs, *dals)]
        + [whole(a) for a in (*wihs, *wils)]
        + [along(dl), whole(gates)]
        + [pl.BlockSpec(memory_space=pltpu.HBM)] * (len(before) + len(after)),
        out_specs=[pl.BlockSpec((TILE, depth), lambda i: (i + skip, 0)), pl.BlockSpec(TOKEN, lambda i: (0, 0))],
        out_shape=[jax.ShapeDtypeStruct((rows, depth), F32), jax.ShapeDtypeStruct(TOKEN, F32)],
        scratch_shapes=[pltpu.VMEM((3 * GATES, depth), BF16)],
        input_output_aliases={n + k: k for k in range(len(before))},
        compiler_params=pltpu.CompilerParams(vmem_limit_bytes=58 << 20),
        cost_estimate=pl.CostEstimate(
            flops=15000000000 // parts, bytes_accessed=25000000 // parts, transcendentals=0
        ),
    )(*ins)


def finish_kernel(me_ref, *refs):
    n = len(GROUPS) + 1
    w_out_ref, gain_ref, shift_ref = refs[n : n + 3]
    g_in, g_in_bias, g_gain, g_shift, g_out, g_out_bias, g_task, g_shared = refs[n + 3 :]
    rows_in, rows_out, units = g_in.shape[1], g_out.shape[1], g_in.shape[2]
    me = me_ref[0]

    def own(row):
        value = row[:, 0:rows_out]
        for p in range(1, units // rows_out):
            value = jnp.where(me == p, row[:, p * rows_out : (p + 1) * rows_out], value)
        return value

    def as_row(col):
        return jnp.broadcast_to(col, (rows_out, LANES)).T[0:1]

    for k, group in enumerate(GROUPS):
        if k < len(GROUPS) - 1:
            add = lambda lower, upper, a=refs[k]: a[lower:upper]
        else:
            add = lambda lower, upper, a=refs[k], b=refs[k + 1]: a[lower:upper] + b[lower:upper]
        at = 0
        for e in group:
            g_in[e] = add(at, at + rows_in)
            at += rows_in
            raw = add(at, at + rows_out)
            at += rows_out
            tail = add(at, at + 8)
            at += 8
            total = tail[0:1]
            gain = wide(column(gain_ref[e : e + 1]), units)
            shift = wide(column(shift_ref[e : e + 1]), units)
            g_out[e] = gain * raw + shift * total
            w = w_out_ref[e]
            g_gain[e : e + 1] = as_row(jnp.sum(w * raw, axis=1, keepdims=True))
            g_shift[e : e + 1] = as_row(jnp.sum(w * total, axis=1, keepdims=True))
            g_in_bias[e : e + 1] = own(tail[1:2])
            g_out_bias[e : e + 1] = own(total)
    gate = add(at, at + GATES)[:, 0:rows_in]
    m = SPEC + SHARED
    for t in range(TASKS):
        g_task[t] = gate[t * m : (t + 1) * m]
    g_shared[...] = gate[TASKS * m : TASKS * m + EXPERTS]


def finish(me, totals, w_in, w_out, gain, shift):
    experts, rows_in, units = w_in.shape
    rows_out = w_out.shape[1]
    shape = lambda *s: jax.ShapeDtypeStruct(s, F32)
    vector = shape(experts, rows_out)
    outs = [
        shape(*w_in.shape),
        vector,
        vector,
        vector,
        shape(*w_out.shape),
        vector,
        shape(TASKS, SPEC + SHARED, rows_in),
        shape(EXPERTS, rows_in),
    ]
    vmem = pl.BlockSpec(memory_space=pltpu.VMEM)
    got = pl.pallas_call(
        finish_kernel,
        in_specs=[pl.BlockSpec(memory_space=pltpu.SMEM)] + [vmem] * (len(totals) + 3),
        out_specs=[vmem] * len(outs),
        out_shape=outs,
        compiler_params=pltpu.CompilerParams(vmem_limit_bytes=16 << 20),
    )(me, *totals, w_out, gain, shift)
    return (*got[:6], got[6].transpose(0, 2, 1), got[7].T)


def make(mesh):
    n_fsdp, n_dp = mesh.shape["fsdp"], mesh.shape["dp"]
    pairs = n_fsdp // 2
    across = [[q * 2 + c for q in range(pairs)] for c in range(2)]
    twin = [(i, i ^ 1) for i in range(n_fsdp)]

    def spread_out(x):
        return lax.all_to_all(x, "fsdp", 0, 0, axis_index_groups=across)

    def swap(x, bit):
        return lax.ppermute(x, "dp", [(i, i ^ bit) for i in range(n_dp)])

    def reduce_some(x, token, some, beside):
        for bit in some:
            x, token = total([x, swap(x, bit)], beside)
        return x, token

    bits = [1 << k for k in range(n_dp.bit_length() - 1)]

    def on_device(
        features, cotangent, counts, keep, w_in, in_bias, norm_gain, norm_bias, w_out, out_bias, task_gate, shared_gate
    ):
        rows = features.shape[0]
        depth = features.shape[1]
        experts, rows_in, units = w_in.shape
        rows_out = w_out.shape[1]
        valid = (lax.broadcasted_iota(jnp.int32, (1, rows), 1) < counts[0]) & (keep.reshape(1, rows) > 0)
        me = lax.axis_index("fsdp")
        core = (me % 2).astype(jnp.int32).reshape(1)
        valid = valid.astype(F32)
        xh, xl, ct, spread, done = prep(features, cotangent, valid, w_in, w_out, pairs)
        own0 = tie(
            spread_out(
                pack(pairs, w_in, in_bias, norm_gain, norm_bias, w_out, out_bias, task_gate, shared_gate)
            ),
            [done],
        )
        other0 = lax.ppermute(own0, "fsdp", twin)
        cts = {o: (ct, k) for k, o in enumerate(used_by(GROUPS[0]))}

        def parts_of(got, group):
            n = len(group)
            m = 1 if group == GROUPS[-1] else len({o for e in group for o, _ in uses(e)})
            return got[:n], got[n : 2 * n], got[2 * n : 2 * n + m], got[2 * n + m :]

        got = expert_call(GROUPS[0], core, own0, other0, None, xh, xl, cts, valid, cotangent, None, [], False, [], 0, {})
        dah0, dal0, mix0, (wih0, wil0, grads0, prob, small, gates, dp0, done0) = parts_of(got, GROUPS[0])
        own1 = tie(spread_out(spread), [done0])
        other1 = lax.ppermute(own1, "fsdp", twin)
        got = expert_call(
            GROUPS[1], core, own1, other1, small, xh, xl, cts, valid, cotangent, prob, [], False, [], 0, {2: mix0[1]}
        )
        dah1, dal1, mix1, (wih1, wil1, grads1, dp1, done1, *fresh) = parts_of(got, GROUPS[1])
        cts.update(zip([o for o in used_by(GROUPS[1]) if o not in cts], [(c, 0) for c in fresh]))
        sum0, token0 = total([lax.all_to_all(grads0, "fsdp", 0, 0)], [done1])
        got = expert_call(
            GROUPS[2],
            core,
            own1,
            other1,
            small,
            xh,
            xl,
            cts,
            valid,
            cotangent,
            prob,
            [dp0, dp1],
            True,
            [token0],
            1,
            {0: mix0[0], 1: mix1[0], 2: mix1[1]},
        )
        dah2, dal2, (outputs,), (wih2, wil2, keep2, send2, dl, done2) = parts_of(got, GROUPS[2])
        sum1, token1 = total([lax.all_to_all(grads1, "fsdp", 0, 0)], [done2])
        sum0, token0 = reduce_some(sum0, token0, bits[:-1], [done2])
        kept = keep2 + lax.ppermute(tie(send2, [token0, token1]), "fsdp", twin)
        tail = (
            (*dah0, *dah1, *dah2),
            (*dal0, *dal1, *dal2),
            (wih0, wih1, wih2),
            (wil0, wil1, wil2),
            dl,
            gates,
        )
        part, done3 = final_call(*tail, 0, [], [])
        sum2, token2 = total([spread_out(kept)], [done3])
        sum1, token1 = reduce_some(sum1, token1, bits[:-1], [done3])
        part, done4 = final_call(*tail, 1, [part], [token1, token2])
        sum0, token0 = total([sum0, swap(sum0, bits[-1])], [done4])
        sum2, token2 = reduce_some(sum2, token2, bits[:-1], [done4])
        grad_features, done5 = final_call(*tail, 2, [part], [token0, token2])
        sum1, token1 = total([sum1, swap(sum1, bits[-1])], [done5])
        pair2 = (sum2, swap(sum2, bits[-1]))
        rest = finish(me.astype(jnp.int32).reshape(1), (sum0, sum1, *pair2), w_in, w_out, norm_gain, norm_bias)
        return (outputs, grad_features, *rest)

    return on_device


def solution(mesh):
    placed = (
        P(("dp", "fsdp"), None),
        P(None, ("dp", "fsdp"), None),
        P(("dp", "fsdp")),
        P(("dp", "fsdp")),
        P(None, "fsdp", None),
        P(None, "fsdp"),
        P(None, "fsdp"),
        P(None, "fsdp"),
        P(None, "fsdp", None),
        P(None, "fsdp"),
        P(None, "fsdp", None),
        P("fsdp", None),
    )
    return jax.shard_map(
        make(mesh),
        mesh=mesh,
        in_specs=placed,
        out_specs=(
            P(None, ("dp", "fsdp"), None),
            P(("dp", "fsdp"), None),
            P(None, "fsdp", None),
            P(None, "fsdp"),
            P(None, "fsdp"),
            P(None, "fsdp"),
            P(None, "fsdp", None),
            P(None, "fsdp"),
            P(None, "fsdp", None),
            P("fsdp", None),
        ),
        check_vma=False,
    )
```

```python
import functools

import jax
import jax.numpy as jnp
from jax import lax
from jax.experimental import pallas as pl
from jax.experimental.pallas import tpu as pltpu
from jax.sharding import PartitionSpec as P

TASKS = 2
SPEC = 2
SHARED = 2
EXPERTS = 6
EPSILON = 1e-05
GROUPS = ((0, 1), (2, 3), (4, 5))
TILE = 512
STEP = 16
PARTS = 3
TOKEN = (8, 128)
SPAN = 256
ORDER = (('in', 0), ('in', 1), ('norm', 0), ('in', 2), ('norm', 1), ('in', 3), ('out', 0), ('norm', 2), ('out', 1), ('norm', 3), ('comb', 0), ('out', 2), ('comb', 1), ('out', 3), ('back', 0), ('comb', 2), ('back', 1), ('comb', 3), ('go', 0), ('bnorm', 0), ('back', 2), ('bnorm', 1), ('back', 3), ('gi', 0), ('bnorm', 2), ('go', 1), ('bnorm', 3), ('gi', 1))
LANES = 128
GATES = 16
F32 = jnp.float32
BF16 = jnp.bfloat16
VMEM_BYTES = 58 << 20

NN = (((1,), (0,)), ((), ()))
NT = (((1,), (1,)), ((), ()))
TN = (((0,), (0,)), ((), ()))


def uses(expert):
    if expert >= TASKS * SPEC:
        shared = expert - TASKS * SPEC
        first = [(t, t * (SPEC + SHARED) + SPEC + shared) for t in range(TASKS)]
    else:
        t = expert // SPEC
        first = [(t, t * (SPEC + SHARED) + expert % SPEC)]
    return first + [(TASKS, TASKS * (SPEC + SHARED) + expert)]


def halves(v):
    high = v.astype(BF16)
    return high, (v - high.astype(F32)).astype(BF16)


def dot(a, b, dims):
    return lax.dot_general(a, b, dims, preferred_element_type=F32)


def dot3(a_high, a_low, b_high, b_low, dims):
    return dot(a_high, b_high, dims) + dot(a_low, b_high, dims) + dot(a_high, b_low, dims)


def dot3_stacked(both, b_high, b_low):
    n = both.shape[0] // 2
    product = dot(both[...], b_high, NN)
    return product[0:n] + product[n:] + dot(both[0:n], b_low, NN)


def column(row):
    return jnp.broadcast_to(row, (LANES, row.shape[1])).T


def wide(block, width):
    return jnp.concatenate([block] * (width // LANES), axis=1)


def pinned(tokens):
    return [pltpu.with_memory_space_constraint(token, pltpu.HBM) for token in tokens]


def tie(x, after):
    return pl.pallas_call(
        lambda *refs: None,
        in_specs=[pl.BlockSpec(memory_space=pl.ANY)] + [pl.BlockSpec(memory_space=pltpu.HBM)] * len(after),
        out_specs=pl.BlockSpec(memory_space=pl.ANY),
        out_shape=jax.ShapeDtypeStruct(x.shape, x.dtype),
        input_output_aliases={0: 0},
    )(x, *pinned(after))


def total_kernel(n, *refs):
    value = None
    for ref in refs[:n]:
        for part in [ref[...]] if len(ref.shape) == 2 else [ref[k] for k in range(ref.shape[0])]:
            value = part if value is None else value + part
    refs[-2][...] = value


def total(arrays, after):
    vmem = pl.BlockSpec(memory_space=pltpu.VMEM)
    return pl.pallas_call(
        functools.partial(total_kernel, len(arrays)),
        in_specs=[vmem] * len(arrays) + [pl.BlockSpec(memory_space=pltpu.HBM)] * len(after),
        out_specs=[vmem, pl.BlockSpec(memory_space=pltpu.HBM)],
        out_shape=[jax.ShapeDtypeStruct(arrays[0].shape[-2:], F32), pltpu.HBM(TOKEN, F32)],
        compiler_params=pltpu.CompilerParams(vmem_limit_bytes=16 << 20),
    )(*arrays, *pinned(after))


def used_by(group):
    return sorted({o for e in group for o, _ in uses(e)})


def pack_weights(groups, w_in_ref, w_out_ref, to_ref):
    rows_in, rows_out = w_in_ref.shape[1], w_out_ref.shape[1]
    at = 0
    for e in (e for group in groups for e in group):
        for q in range(to_ref.shape[0]):
            to_ref[q, at : at + rows_in] = w_in_ref[e]
            to_ref[q, at + rows_in : at + rows_in + rows_out] = w_out_ref[e]
        at += rows_in + rows_out
    return at


def pack_kernel(in_bias, gain, shift, out_bias, task_gate, shared_gate, w_in_ref, w_out_ref, to_ref):
    rows_in, rows_out = w_in_ref.shape[1], w_out_ref.shape[1]
    at = pack_weights(GROUPS[:1], w_in_ref, w_out_ref, to_ref)
    n = SPEC + SHARED
    for q in range(to_ref.shape[0]):
        to_ref[q, at:] = jnp.zeros((to_ref.shape[1] - at, to_ref.shape[2]), F32)
        for k, bias in enumerate((in_bias, gain, shift, out_bias)):
            to_ref[q, at + k * EXPERTS : at + (k + 1) * EXPERTS, 0:rows_out] = bias[...]
        base = at + 4 * EXPERTS
        for t in range(TASKS):
            to_ref[q, base + t * n : base + (t + 1) * n, 0:rows_in] = task_gate[t]
        base += TASKS * n
        to_ref[q, base : base + EXPERTS, 0:rows_in] = shared_gate[...]


def pack(pairs, w_in, in_bias, gain, shift, w_out, out_bias, task_gate, shared_gate):
    rows = len(GROUPS[0]) * (w_in.shape[1] + w_out.shape[1]) + 4 * EXPERTS + GATES
    return pl.pallas_call(
        pack_kernel,
        out_shape=jax.ShapeDtypeStruct((pairs, rows, w_in.shape[2]), F32),
        compiler_params=pltpu.CompilerParams(vmem_limit_bytes=VMEM_BYTES),
    )(in_bias, gain, shift, out_bias, task_gate.transpose(0, 2, 1), shared_gate.T, w_in, w_out)


def prep_kernel(x_ref, c_refs, valid_ref, w_in_ref, w_out_ref, xh_ref, xl_ref, ct_ref, to_ref, done_ref):
    depth = x_ref.shape[1]

    @pl.when(pl.program_id(0) == 0)
    def _():
        pack_weights(GROUPS[1:], w_in_ref, w_out_ref, to_ref)
        done_ref[...] = jnp.zeros_like(done_ref)

    high, low = halves(x_ref[...].T)
    xh_ref[0:depth] = high
    xh_ref[depth:] = jnp.ones((xh_ref.shape[0] - depth, xh_ref.shape[1]), BF16)
    xl_ref[...] = low
    valid = valid_ref[...]
    for k, c_ref in enumerate(c_refs):
        ct_ref[k] = c_ref[0].T * valid


def prep(features, cotangent, valid, w_in, w_out, pairs):
    rows, depth = features.shape
    packed = sum(len(g) for g in GROUPS[1:]) * (w_in.shape[1] + w_out.shape[1])
    units = cotangent.shape[2]
    used = used_by(GROUPS[0])
    outs = len(used)
    return pl.pallas_call(
        prep_kernel,
        grid=(rows // TILE,),
        in_specs=[
            pl.BlockSpec((TILE, depth), lambda i: (i, 0)),
            [pl.BlockSpec((1, TILE, units), lambda i, o=o: (o, i, 0)) for o in used],
            pl.BlockSpec((1, TILE), lambda i: (0, i)),
            pl.BlockSpec(w_in.shape, lambda i: (0, 0, 0)),
            pl.BlockSpec(w_out.shape, lambda i: (0, 0, 0)),
        ],
        out_specs=[
            pl.BlockSpec((depth + STEP, TILE), lambda i: (0, i)),
            pl.BlockSpec((depth, TILE), lambda i: (0, i)),
            pl.BlockSpec((outs, units, TILE), lambda i: (0, 0, i)),
            pl.BlockSpec((pairs, packed, units), lambda i: (0, 0, 0)),
            pl.BlockSpec(TOKEN, lambda i: (0, 0)),
        ],
        out_shape=[
            jax.ShapeDtypeStruct((depth + STEP, rows), BF16),
            jax.ShapeDtypeStruct((depth, rows), BF16),
            jax.ShapeDtypeStruct((outs, units, rows), F32),
            jax.ShapeDtypeStruct((pairs, packed, units), F32),
            jax.ShapeDtypeStruct(TOKEN, F32),
        ],
        compiler_params=pltpu.CompilerParams(vmem_limit_bytes=VMEM_BYTES),
        cost_estimate=pl.CostEstimate(flops=0, bytes_accessed=26000000, transcendentals=0),
    )(features, [cotangent] * outs, valid, w_in, w_out)


def softmax_rows(v):
    e = jnp.exp(v - jnp.max(v, axis=0, keepdims=True))
    return e / jnp.sum(e, axis=0, keepdims=True)


def expert_kernel(group, first, last, n_after, partial, fresh, *refs):
    used = used_by(group)
    names = ["core", "own", "other"] + ([] if first else ["small"]) + ["xh", "xl"]
    names += [f"c{o}" for o in used if o not in fresh]
    names += (["valid"] + [f"cot{o}" for o in fresh]) if fresh else []
    names += [] if first else ["prob"]
    if last:
        names += [f"dp{k}" for k in range(len(GROUPS) - 1)]
    names += [f"in{o}" for o in partial]
    names += [f"after{k}" for k in range(n_after)]
    names += [f"{name}{l}" for name in ("dah", "dal") for l in range(len(group))]
    names += ["out"] if last else [f"out{o}" for o in used]
    names += ["wih", "wil"]
    names += ["keep", "send"] if last else ["grads"]
    if first:
        names += ["prob", "small", "gates"]
    names += ["dl"] if last else ["dp"]
    names += ["done"] + [f"c{o}" for o in fresh]
    each = ["win_t", "wp", "wp_t", "b_in", "b_out", "acc_w", "acc_g"]
    each += ["h", "u", "a", "xhat", "h2", "g", "ex", "xhh", "xhl", "dzh", "dzl"]
    names += [f"{name}{l}" for name in each for l in range(len(group))]
    if last:
        names += ["all_dp", "acc_gate"] + [f"mix{o}" for o in used]
    r = dict(zip(names, refs, strict=True))
    for name in (*each, "dah", "dal"):
        r[name] = [r[f"{name}{l}"] for l in range(len(group))]
    step = pl.program_id(0)
    count = len(group)
    units = r["acc_w"][0].shape[1]
    depth = r["xl"].shape[0]
    pairs = r["own"].shape[0]
    devices = 2 * pairs
    rows_in, rows_out = depth // devices, units // devices
    rows_all = rows_in + rows_out
    core = r["core"][0]
    tile = r["xl"].shape[1]
    chunks = [slice(k, k + STEP) for k in range(0, units, STEP)]

    @pl.when(step == 0)
    def _():
        if first:
            begin = count * rows_all
            r["small"][...] = jnp.zeros_like(r["small"])
            r["gates"][...] = jnp.zeros_like(r["gates"])
            for q in range(pairs):
                block, offset = divmod(2 * q * rows_in, units)
                lanes = slice(block * units, (block + 1) * units)
                for src, at in ((r["own"], core), (r["other"], 1 - core)):
                    piece = src[q, begin : begin + 4 * EXPERTS]
                    r["small"][...] += pltpu.roll(piece, (2 * q + at) * rows_out, 1)
                    piece = src[q, begin + 4 * EXPERTS : begin + 4 * EXPERTS + GATES]
                    r["gates"][:, lanes] += pltpu.roll(piece, offset + at * rows_in, 1)
        for l, e in enumerate(group):
            base = l * rows_all
            for q in range(pairs):
                for src, at in ((r["own"], core), (r["other"], 1 - core)):
                    place = q * 2 + at
                    r["acc_w"][l][pl.ds(place * rows_in, rows_in)] = src[q, base : base + rows_in]
                    r["acc_g"][l][pl.ds(place * rows_out, rows_out)] = src[
                        q, base + rows_in : base + rows_all
                    ]
            w_in = r["acc_w"][l][0:depth]
            high, low = halves(w_in)
            r["wih"][l] = high
            r["wil"][l] = low
            high, low = halves((0.5 * w_in).T)
            top = r["win_t"][l].shape[0] // 2
            r["win_t"][l][0:units] = high
            r["win_t"][l][top : top + units] = low
            w_out = r["acc_g"][l][0:units]
            b_in, gain, shift, b_out = (r["small"][k * EXPERTS + e : k * EXPERTS + e + 1] for k in range(4))
            scaled = w_out * wide(column(gain), units)
            high, low = halves(scaled)
            r["wp"][l][0:units] = high
            r["wp"][l][units:] = low
            high, low = halves((0.5 * scaled).T)
            r["wp_t"][l][0:units] = high
            r["wp_t"][l][units:] = low
            b_out = b_out + jnp.sum(w_out * wide(column(shift), units), axis=0, keepdims=True)
            r["b_in"][l][...] = column(0.5 * b_in)
            r["b_out"][l][...] = column(0.5 * b_out)
            r["xhh"][l][units:] = jnp.ones((STEP, tile), BF16)
        if first:
            high, low = halves(r["gates"][...])
            top = r["win_t"][0].shape[0] // 2
            r["win_t"][0][units:top] = high
            r["win_t"][0][top + units :] = low
            for l in range(1, count):
                r["win_t"][l][units:top] = high
                r["win_t"][l][top + units :] = low
        for l in range(count):
            r["acc_w"][l][...] = jnp.zeros_like(r["acc_w"][l])
            r["acc_g"][l][...] = jnp.zeros_like(r["acc_g"][l])
        r["done"][...] = jnp.zeros_like(r["done"])
        if last:
            r["acc_gate"][...] = jnp.zeros_like(r["acc_gate"])

    stats = {}

    spans = [slice(k, k + SPAN) for k in range(0, tile, SPAN)]
    zero = jnp.zeros((STEP, SPAN), F32)

    def project_in(l, s):
        r["h"][l][:, s] = dot3_stacked(r["win_t"][l], r["xh"][0:depth, s], r["xl"][:, s])

    def gate_weights(s):
        z = r["h"][0][units:, s]
        for lower, upper in ((0, 4), (4, 8), (8, 14)):
            r["prob"][lower:upper, s] = softmax_rows(z[lower:upper])
        r["prob"][14:16, s] = jnp.zeros((2, SPAN), F32)

    def normalise(l, s):
        total = zero
        for c in chunks:
            h = r["h"][l][c, s] + wide(r["b_in"][l][c], SPAN)
            u = 1.0 + jnp.tanh(h)
            a = h * u
            r["u"][l][c, s] = u
            r["a"][l][c, s] = a
            total = total + a
        mean = jnp.sum(total, axis=0, keepdims=True) * (1.0 / units)
        total = zero
        for c in chunks:
            d = r["a"][l][c, s] - mean
            total = total + d * d
        scale = lax.rsqrt(jnp.sum(total, axis=0, keepdims=True) * (1.0 / units) + EPSILON)
        stats[l, s.start] = scale
        for c in chunks:
            x = (r["a"][l][c, s] - mean) * scale
            r["xhat"][l][c, s] = x
            r["xhh"][l][c, s], r["xhl"][l][c, s] = halves(x)

    def project_out(l, s):
        r["h2"][l][:, s] = dot3_stacked(r["wp_t"][l], r["xhh"][l][0:units, s], r["xhl"][l][:, s])

    def combine(l, s):
        taken = uses(group[l])
        prob = [0.5 * r["prob"][row : row + 1, s] for _, row in taken]
        sums = [zero for _ in taken]
        end = l == count - 1
        full = [[r["prob"][row : row + 1, s] for _, row in uses(e)] for e in group] if end else None
        for c in chunks:
            h = r["h2"][l][c, s] + wide(r["b_out"][l][c], SPAN)
            u = 1.0 + jnp.tanh(h)
            ex = h * u
            if not end:
                r["ex"][l][c, s] = ex
            slope = u + ex * (2.0 - u)
            d = None
            for k, (o, _) in enumerate(taken):
                cot = r[f"c{o}"][0, c, s]
                sums[k] = sums[k] + cot * ex
                term = prob[k] * cot
                d = term if d is None else d + term
                if end:
                    mix = full[l][k] * ex
                    for m in range(l):
                        mix = mix + full[m][k] * r["ex"][m][c, s]
                    if o in partial:
                        mix = mix + r[f"in{o}"][c, s]
                    if last:
                        r[f"mix{o}"][c, s] = mix
                    else:
                        r[f"out{o}"][c, s] = mix
            r["dzh"][l][c, s], r["dzl"][l][c, s] = halves(d * slope)
        for k, (_, row) in enumerate(taken):
            value = jnp.sum(sums[k], axis=0, keepdims=True)
            if last:
                r["all_dp"][row : row + 1, s] = value
            else:
                at = l * len(taken) + k
                r["dp"][at : at + 1, s] = value

    def back_out(l, s):
        r["g"][l][:, s] = dot3_stacked(r["wp"][l], r["dzh"][l][:, s], r["dzl"][l][:, s])

    def grad_out(l):
        r["acc_g"][l][...] += dot(r["xhh"][l][...], r["dzh"][l][...], NT) + dot(
            r["xhh"][l][...], r["dzl"][l][...], NT
        )
        r["acc_g"][l][0:units] += dot(r["xhl"][l][...], r["dzh"][l][...], NT)

    def back_norm(l, s):
        total, along = zero, zero
        for c in chunks:
            g = r["g"][l][c, s]
            total = total + g
            along = along + g * r["xhat"][l][c, s]
        mean = jnp.sum(total, axis=0, keepdims=True) * (1.0 / units)
        along = jnp.sum(along, axis=0, keepdims=True) * (1.0 / units)
        scale = 0.5 * stats[l, s.start]
        for c in chunks:
            u, a = r["u"][l][c, s], r["a"][l][c, s]
            slope = (u + a * (2.0 - u)) * scale
            da = (r["g"][l][c, s] - mean - r["xhat"][l][c, s] * along) * slope
            r["dah"][l][c, s], r["dal"][l][c, s] = halves(da)

    def grad_in(l):
        high, low = r["dah"][l][...], r["dal"][l][...]
        r["acc_w"][l][...] += dot(r["xh"][...], high, NT) + dot(r["xh"][...], low, NT)
        r["acc_w"][l][0:depth] += dot(r["xl"][...], high, NT)

    chains = [(l, s) for l in range(count) for s in spans]
    for o in fresh:
        r[f"c{o}"][0] = r[f"cot{o}"][0].T * r["valid"][...]
    for stage in ORDER:
        if isinstance(stage, tuple):
            name, k = stage
            if name == "go":
                grad_out(k)
            elif name == "gi":
                grad_in(k)
            else:
                at = {
                    "in": project_in, "norm": normalise, "out": project_out, "comb": combine, "back": back_out,
                    "bnorm": back_norm,
                }[name]
                at(*chains[k])
                if name == "in" and first and chains[k][0] == 0:
                    gate_weights(chains[k][1])

    if last:
        for o in used:
            r["out"][o] = r[f"mix{o}"][...].T
    if last:
        for k, g in enumerate(GROUPS[:-1]):
            at = 0
            for e in g:
                for _, row in uses(e):
                    r["all_dp"][row : row + 1] = r[f"dp{k}"][at : at + 1]
                    at += 1
        for lower, upper in ((0, 4), (4, 8), (8, 14)):
            p, d = r["prob"][lower:upper], r["all_dp"][lower:upper]
            r["dl"][lower:upper] = p * (d - jnp.sum(p * d, axis=0, keepdims=True))
        r["dl"][14:16] = jnp.zeros((2, tile), F32)
        high, low = halves(r["dl"][...])
        both = dot(jnp.concatenate([high, low], 0), r["xh"][0:depth], NT)
        r["acc_gate"][...] += both[0:GATES] + both[GATES:] + dot(high, r["xl"][...], NT)

    @pl.when(step == pl.num_programs(0) - 1)
    def _():
        for l in range(count):
            base = l * (rows_all + 8)
            tail = jnp.concatenate([r["acc_g"][l][units : units + 1], r["acc_w"][l][depth : depth + 1]], 0)
            tail = jnp.concatenate([tail] * 4, 0)
            if last:
                places = [
                    (dst, q, q * 2 + at)
                    for q in range(pairs)
                    for dst, at in ((r["keep"], core), (r["send"], 1 - core))
                ]
            else:
                places = [(r["grads"], k, k) for k in range(devices)]
            for dst, q, place in places:
                dst[q, base : base + rows_in] = r["acc_w"][l][pl.ds(place * rows_in, rows_in)]
                dst[q, base + rows_in : base + rows_all] = r["acc_g"][l][pl.ds(place * rows_out, rows_out)]
                dst[q, base + rows_all : base + rows_all + 8] = tail
        if last:
            gate = r["acc_gate"][...]
            base = count * (rows_all + 8)
            for q in range(pairs):
                even = gate[:, 2 * q * rows_in : (2 * q + 1) * rows_in]
                odd = gate[:, (2 * q + 1) * rows_in : (2 * q + 2) * rows_in]
                for dst, at in ((r["keep"], core), (r["send"], 1 - core)):
                    dst[q, base:, 0:rows_in] = jnp.where(at == 0, even, odd)


def expert_call(group, core, own, other, small, xh, xl, cts, valid, cotangent, prob, dps, last, after, skip, mixed):
    first = small is None
    pairs, _, units = own.shape
    depth, rows = xl.shape
    devices = 2 * pairs
    rows_in, rows_out = depth // devices, units // devices
    count = len(group)
    whole = lambda shape: pl.BlockSpec(shape, lambda i: (0,) * len(shape))
    along = lambda n: pl.BlockSpec((n, TILE), lambda i: (0, i))
    used = used_by(group)
    old, fresh = [o for o in used if o in cts], tuple(o for o in used if o not in cts)
    ins = [core, own, other] + ([] if first else [small]) + [xh, xl] + [cts[o][0] for o in old]
    held = own.shape[1] if first else count * (rows_in + rows_out)
    weights = pl.BlockSpec((pairs, held, units), lambda i: (0, skip, 0))
    in_specs = [
        pl.BlockSpec(memory_space=pltpu.SMEM),
        weights,
        weights,
        *([] if first else [whole((4 * EXPERTS, units))]),
        along(xh.shape[0]),
        along(depth),
    ]
    in_specs += [pl.BlockSpec((1, units, TILE), lambda i, k=cts[o][1]: (k, 0, i)) for o in old]
    if fresh:
        ins += [valid] + [cotangent] * len(fresh)
        in_specs.append(along(1))
        in_specs += [pl.BlockSpec((1, TILE, units), lambda i, o=o: (o, i, 0)) for o in fresh]
    if not first:
        ins.append(prob)
        in_specs.append(along(GATES))
    if last:
        ins += dps
        in_specs += [along(8)] * len(dps)
    ins += [mixed[o] for o in sorted(mixed)]
    in_specs += [along(units)] * len(mixed)
    ins += pinned(after)
    in_specs += [pl.BlockSpec(memory_space=pltpu.HBM)] * len(after)
    packed = count * (rows_in + rows_out + 8)
    shape = jax.ShapeDtypeStruct
    if last:
        mixes = [
            (pl.BlockSpec((len(used), TILE, units), lambda i: (0, i, 0)), shape((len(used), rows, units), F32))
        ]
    else:
        mixes = [(along(units), shape((units, rows), F32))] * len(used)
    outs = [
        *[(along(units), shape((units, rows), BF16))] * (2 * count),
        *mixes,
        (whole((count, depth, units)), shape((count, depth, units), BF16)),
        (whole((count, depth, units)), shape((count, depth, units), BF16)),
    ]
    if last:
        packed += GATES
        outs += [(whole((pairs, packed, units)), shape((pairs, packed, units), F32))] * 2
    else:
        outs.append((whole((devices, packed, units)), shape((devices, packed, units), F32)))
    if first:
        outs.append((along(GATES), shape((GATES, rows), F32)))
        outs += [
            (whole((n, lanes)), shape((n, lanes), F32)) for n, lanes in ((4 * EXPERTS, units), (GATES, depth))
        ]
    if last:
        outs.append((along(GATES), shape((GATES, rows), F32)))
    else:
        outs.append((along(8), shape((8, rows), F32)))
    outs.append((whole(TOKEN), shape(TOKEN, F32)))
    outs += [
        (pl.BlockSpec((1, units, TILE), lambda i: (0, 0, i)), shape((1, units, rows), F32)) for _ in fresh
    ]
    top = units + (GATES if first else 0)
    kinds = [
        ((2 * top, depth), BF16),
        ((2 * units, units), BF16),
        ((2 * units, units), BF16),
        ((units, LANES), F32),
        ((units, LANES), F32),
        ((depth + STEP, units), F32),
        ((units + STEP, units), F32),
        ((top, TILE), F32),
        ((units, TILE), F32),
        ((units, TILE), F32),
        ((units, TILE), F32),
        ((units, TILE), F32),
        ((units, TILE), F32),
        ((units, TILE), F32),
        ((units + STEP, TILE), BF16),
        ((units, TILE), BF16),
        ((units, TILE), BF16),
        ((units, TILE), BF16),
    ]
    scratch = [pltpu.VMEM(*kind) for kind in kinds for _ in group]
    if last:
        scratch += [pltpu.VMEM((GATES, TILE), F32), pltpu.VMEM((GATES, depth), F32)]
        scratch += [pltpu.VMEM((units, TILE), F32)] * len(used)
    return pl.pallas_call(
        functools.partial(expert_kernel, group, first, last, len(after), tuple(sorted(mixed)), fresh),
        grid=(rows // TILE,),
        in_specs=in_specs,
        out_specs=[o[0] for o in outs],
        out_shape=[o[1] for o in outs],
        scratch_shapes=scratch,
        compiler_params=pltpu.CompilerParams(vmem_limit_bytes=58 << 20),
        cost_estimate=pl.CostEstimate(
            flops=20000000000 * count // 2, bytes_accessed=30000000, transcendentals=0
        ),
    )(*ins)


def final_kernel(steps, *refs):
    n = EXPERTS
    dahs, dals = refs[:n], refs[n : 2 * n]
    wihs, wils = refs[2 * n : 2 * n + len(GROUPS)], refs[2 * n + len(GROUPS) : 2 * n + 2 * len(GROUPS)]
    dl_ref, gates_ref = refs[2 * n + 2 * len(GROUPS) : 2 * n + 2 * len(GROUPS) + 2]
    gf_ref, done_ref, gate_ref = refs[-3:]
    done_ref[...] = jnp.zeros_like(done_ref)

    @pl.when(pl.program_id(0) == 0)
    def _():
        high, low = halves(gates_ref[...])
        gate_ref[0:GATES] = high
        gate_ref[GATES : 2 * GATES] = low
        gate_ref[2 * GATES :] = high

    for k in range(0, TILE, SPAN):
        span = slice(k, k + SPAN)
        high, low = halves(dl_ref[:, span])
        value = dot(gate_ref[...], jnp.concatenate([high, high, low], 0), TN)
        at = 0
        for k, group in enumerate(GROUPS):
            for l in range(len(group)):
                value = value + dot3(wihs[k][l], wils[k][l], dahs[at][:, span], dals[at][:, span], NN)
                at += 1
        gf_ref[span] = value.T


def final_call(dahs, dals, wihs, wils, dl, gates, part, before, after):
    rows = dl.shape[1]
    _, depth, units = wihs[0].shape
    tiles = rows // TILE
    skip, end = (tiles * k // PARTS for k in (part, part + 1))
    steps, parts = end - skip, PARTS
    whole = lambda a: pl.BlockSpec(a.shape, lambda i: (0,) * a.ndim)
    along = lambda a: pl.BlockSpec((a.shape[0], TILE), lambda i: (0, i + skip))
    ins = [*dahs, *dals, *wihs, *wils, dl, gates, *before, *pinned(after)]
    n = 2 * EXPERTS + 2 * len(GROUPS) + 2
    return pl.pallas_call(
        functools.partial(final_kernel, steps),
        grid=(steps,),
        in_specs=[along(a) for a in (*dahs, *dals)]
        + [whole(a) for a in (*wihs, *wils)]
        + [along(dl), whole(gates)]
        + [pl.BlockSpec(memory_space=pltpu.HBM)] * (len(before) + len(after)),
        out_specs=[pl.BlockSpec((TILE, depth), lambda i: (i + skip, 0)), pl.BlockSpec(TOKEN, lambda i: (0, 0))],
        out_shape=[jax.ShapeDtypeStruct((rows, depth), F32), jax.ShapeDtypeStruct(TOKEN, F32)],
        scratch_shapes=[pltpu.VMEM((3 * GATES, depth), BF16)],
        input_output_aliases={n + k: k for k in range(len(before))},
        compiler_params=pltpu.CompilerParams(vmem_limit_bytes=58 << 20),
        cost_estimate=pl.CostEstimate(
            flops=15000000000 // parts, bytes_accessed=25000000 // parts, transcendentals=0
        ),
    )(*ins)


def finish_kernel(me_ref, *refs):
    n = len(GROUPS) + 1
    w_out_ref, gain_ref, shift_ref = refs[n : n + 3]
    g_in, g_in_bias, g_gain, g_shift, g_out, g_out_bias, g_task, g_shared = refs[n + 3 :]
    rows_in, rows_out, units = g_in.shape[1], g_out.shape[1], g_in.shape[2]
    me = me_ref[0]

    def own(row):
        value = row[:, 0:rows_out]
        for p in range(1, units // rows_out):
            value = jnp.where(me == p, row[:, p * rows_out : (p + 1) * rows_out], value)
        return value

    def as_row(col):
        return jnp.broadcast_to(col, (rows_out, LANES)).T[0:1]

    for k, group in enumerate(GROUPS):
        if k < len(GROUPS) - 1:
            add = lambda lower, upper, a=refs[k]: a[lower:upper]
        else:
            add = lambda lower, upper, a=refs[k], b=refs[k + 1]: a[lower:upper] + b[lower:upper]
        at = 0
        for e in group:
            g_in[e] = add(at, at + rows_in)
            at += rows_in
            raw = add(at, at + rows_out)
            at += rows_out
            tail = add(at, at + 8)
            at += 8
            total = tail[0:1]
            gain = wide(column(gain_ref[e : e + 1]), units)
            shift = wide(column(shift_ref[e : e + 1]), units)
            g_out[e] = gain * raw + shift * total
            w = w_out_ref[e]
            g_gain[e : e + 1] = as_row(jnp.sum(w * raw, axis=1, keepdims=True))
            g_shift[e : e + 1] = as_row(jnp.sum(w * total, axis=1, keepdims=True))
            g_in_bias[e : e + 1] = own(tail[1:2])
            g_out_bias[e : e + 1] = own(total)
    gate = add(at, at + GATES)[:, 0:rows_in]
    m = SPEC + SHARED
    for t in range(TASKS):
        g_task[t] = gate[t * m : (t + 1) * m]
    g_shared[...] = gate[TASKS * m : TASKS * m + EXPERTS]


def finish(me, totals, w_in, w_out, gain, shift):
    experts, rows_in, units = w_in.shape
    rows_out = w_out.shape[1]
    shape = lambda *s: jax.ShapeDtypeStruct(s, F32)
    vector = shape(experts, rows_out)
    outs = [
        shape(*w_in.shape),
        vector,
        vector,
        vector,
        shape(*w_out.shape),
        vector,
        shape(TASKS, SPEC + SHARED, rows_in),
        shape(EXPERTS, rows_in),
    ]
    vmem = pl.BlockSpec(memory_space=pltpu.VMEM)
    got = pl.pallas_call(
        finish_kernel,
        in_specs=[pl.BlockSpec(memory_space=pltpu.SMEM)] + [vmem] * (len(totals) + 3),
        out_specs=[vmem] * len(outs),
        out_shape=outs,
        compiler_params=pltpu.CompilerParams(vmem_limit_bytes=16 << 20),
    )(me, *totals, w_out, gain, shift)
    return (*got[:6], got[6].transpose(0, 2, 1), got[7].T)


def make(mesh):
    n_fsdp, n_dp = mesh.shape["fsdp"], mesh.shape["dp"]
    pairs = n_fsdp // 2
    across = [[q * 2 + c for q in range(pairs)] for c in range(2)]
    twin = [(i, i ^ 1) for i in range(n_fsdp)]

    def spread_out(x):
        return lax.all_to_all(x, "fsdp", 0, 0, axis_index_groups=across)

    def swap(x, bit):
        return lax.ppermute(x, "dp", [(i, i ^ bit) for i in range(n_dp)])

    def reduce_some(x, token, some, beside):
        for bit in some:
            x, token = total([x, swap(x, bit)], beside)
        return x, token

    bits = [1 << k for k in range(n_dp.bit_length() - 1)]

    def on_device(
        features, cotangent, counts, keep, w_in, in_bias, norm_gain, norm_bias, w_out, out_bias, task_gate, shared_gate
    ):
        rows = features.shape[0]
        depth = features.shape[1]
        experts, rows_in, units = w_in.shape
        rows_out = w_out.shape[1]
        valid = (lax.broadcasted_iota(jnp.int32, (1, rows), 1) < counts[0]) & (keep.reshape(1, rows) > 0)
        me = lax.axis_index("fsdp")
        core = (me % 2).astype(jnp.int32).reshape(1)
        valid = valid.astype(F32)
        xh, xl, ct, spread, done = prep(features, cotangent, valid, w_in, w_out, pairs)
        own0 = tie(
            spread_out(
                pack(pairs, w_in, in_bias, norm_gain, norm_bias, w_out, out_bias, task_gate, shared_gate)
            ),
            [done],
        )
        other0 = lax.ppermute(own0, "fsdp", twin)
        cts = {o: (ct, k) for k, o in enumerate(used_by(GROUPS[0]))}

        def parts_of(got, group):
            n = len(group)
            m = 1 if group == GROUPS[-1] else len({o for e in group for o, _ in uses(e)})
            return got[:n], got[n : 2 * n], got[2 * n : 2 * n + m], got[2 * n + m :]

        got = expert_call(GROUPS[0], core, own0, other0, None, xh, xl, cts, valid, cotangent, None, [], False, [], 0, {})
        dah0, dal0, mix0, (wih0, wil0, grads0, prob, small, gates, dp0, done0) = parts_of(got, GROUPS[0])
        own1 = tie(spread_out(spread), [done0])
        other1 = lax.ppermute(own1, "fsdp", twin)
        got = expert_call(
            GROUPS[1], core, own1, other1, small, xh, xl, cts, valid, cotangent, prob, [], False, [], 0, {2: mix0[1]}
        )
        dah1, dal1, mix1, (wih1, wil1, grads1, dp1, done1, *fresh) = parts_of(got, GROUPS[1])
        cts.update(zip([o for o in used_by(GROUPS[1]) if o not in cts], [(c, 0) for c in fresh]))
        sum0, token0 = total([lax.all_to_all(grads0, "fsdp", 0, 0)], [done1])
        got = expert_call(
            GROUPS[2],
            core,
            own1,
            other1,
            small,
            xh,
            xl,
            cts,
            valid,
            cotangent,
            prob,
            [dp0, dp1],
            True,
            [token0],
            1,
            {0: mix0[0], 1: mix1[0], 2: mix1[1]},
        )
        dah2, dal2, (outputs,), (wih2, wil2, keep2, send2, dl, done2) = parts_of(got, GROUPS[2])
        sum1, token1 = total([lax.all_to_all(grads1, "fsdp", 0, 0)], [done2])
        sum0, token0 = reduce_some(sum0, token0, bits[:-1], [done2])
        kept = keep2 + lax.ppermute(tie(send2, [token0, token1]), "fsdp", twin)
        tail = (
            (*dah0, *dah1, *dah2),
            (*dal0, *dal1, *dal2),
            (wih0, wih1, wih2),
            (wil0, wil1, wil2),
            dl,
            gates,
        )
        part, done3 = final_call(*tail, 0, [], [])
        sum2, token2 = total([spread_out(kept)], [done3])
        sum1, token1 = reduce_some(sum1, token1, bits[:-1], [done3])
        part, done4 = final_call(*tail, 1, [part], [token1, token2])
        sum0, token0 = total([sum0, swap(sum0, bits[-1])], [done4])
        sum2, token2 = reduce_some(sum2, token2, bits[:-1], [done4])
        grad_features, done5 = final_call(*tail, 2, [part], [token0, token2])
        sum1, token1 = total([sum1, swap(sum1, bits[-1])], [done5])
        pair2 = (sum2, swap(sum2, bits[-1]))
        rest = finish(me.astype(jnp.int32).reshape(1), (sum0, sum1, *pair2), w_in, w_out, norm_gain, norm_bias)
        return (outputs, grad_features, *rest)

    return on_device


def solution(mesh):
    placed = (
        P(("dp", "fsdp"), None),
        P(None, ("dp", "fsdp"), None),
        P(("dp", "fsdp")),
        P(("dp", "fsdp")),
        P(None, "fsdp", None),
        P(None, "fsdp"),
        P(None, "fsdp"),
        P(None, "fsdp"),
        P(None, "fsdp", None),
        P(None, "fsdp"),
        P(None, "fsdp", None),
        P("fsdp", None),
    )
    return jax.shard_map(
        make(mesh),
        mesh=mesh,
        in_specs=placed,
        out_specs=(
            P(None, ("dp", "fsdp"), None),
            P(("dp", "fsdp"), None),
            P(None, "fsdp", None),
            P(None, "fsdp"),
            P(None, "fsdp"),
            P(None, "fsdp"),
            P(None, "fsdp", None),
            P(None, "fsdp"),
            P(None, "fsdp", None),
            P("fsdp", None),
        ),
        check_vma=False,
    )
```

```python
import functools

import jax
import jax.numpy as jnp
from jax import lax
from jax.experimental import pallas as pl
from jax.experimental.pallas import tpu as pltpu
from jax.sharding import PartitionSpec as P

TASKS = 2
SPEC = 2
SHARED = 2
EXPERTS = 6
EPSILON = 1e-05
GROUPS = ((0, 1), (2, 3), (4, 5))
TILE = 512
STEP = 16
PARTS = 3
TOKEN = (8, 128)
SPAN = 256
ORDER = (('in', 0), ('in', 1), ('norm', 0), ('in', 2), ('norm', 1), ('in', 3), ('out', 0), ('norm', 2), ('out', 1), ('norm', 3), ('comb', 0), ('out', 2), ('comb', 1), ('out', 3), ('back', 0), ('comb', 2), ('back', 1), ('comb', 3), ('go', 0), ('bnorm', 0), ('back', 2), ('bnorm', 1), ('back', 3), ('gi', 0), ('bnorm', 2), ('go', 1), ('bnorm', 3), ('gi', 1))
LANES = 128
GATES = 16
F32 = jnp.float32
BF16 = jnp.bfloat16
VMEM_BYTES = 58 << 20

NN = (((1,), (0,)), ((), ()))
NT = (((1,), (1,)), ((), ()))
TN = (((0,), (0,)), ((), ()))


def uses(expert):
    if expert >= TASKS * SPEC:
        shared = expert - TASKS * SPEC
        first = [(t, t * (SPEC + SHARED) + SPEC + shared) for t in range(TASKS)]
    else:
        t = expert // SPEC
        first = [(t, t * (SPEC + SHARED) + expert % SPEC)]
    return first + [(TASKS, TASKS * (SPEC + SHARED) + expert)]


def halves(v):
    high = v.astype(BF16)
    return high, (v - high.astype(F32)).astype(BF16)


def dot(a, b, dims):
    return lax.dot_general(a, b, dims, preferred_element_type=F32)


def dot3(a_high, a_low, b_high, b_low, dims):
    return dot(a_high, b_high, dims) + dot(a_low, b_high, dims) + dot(a_high, b_low, dims)


def dot3_stacked(both, b_high, b_low):
    n = both.shape[0] // 2
    product = dot(both[...], b_high, NN)
    return product[0:n] + product[n:] + dot(both[0:n], b_low, NN)


def column(row):
    return jnp.broadcast_to(row, (LANES, row.shape[1])).T


def wide(block, width):
    return jnp.concatenate([block] * (width // LANES), axis=1)


def pinned(tokens):
    return [pltpu.with_memory_space_constraint(token, pltpu.HBM) for token in tokens]


def tie(x, after):
    return pl.pallas_call(
        lambda *refs: None,
        in_specs=[pl.BlockSpec(memory_space=pl.ANY)] + [pl.BlockSpec(memory_space=pltpu.HBM)] * len(after),
        out_specs=pl.BlockSpec(memory_space=pl.ANY),
        out_shape=jax.ShapeDtypeStruct(x.shape, x.dtype),
        input_output_aliases={0: 0},
    )(x, *pinned(after))


def total_kernel(n, *refs):
    value = None
    for ref in refs[:n]:
        for part in [ref[...]] if len(ref.shape) == 2 else [ref[k] for k in range(ref.shape[0])]:
            value = part if value is None else value + part
    refs[-2][...] = value


def total(arrays, after):
    vmem = pl.BlockSpec(memory_space=pltpu.VMEM)
    return pl.pallas_call(
        functools.partial(total_kernel, len(arrays)),
        in_specs=[vmem] * len(arrays) + [pl.BlockSpec(memory_space=pltpu.HBM)] * len(after),
        out_specs=[vmem, pl.BlockSpec(memory_space=pltpu.HBM)],
        out_shape=[jax.ShapeDtypeStruct(arrays[0].shape[-2:], F32), pltpu.HBM(TOKEN, F32)],
        compiler_params=pltpu.CompilerParams(vmem_limit_bytes=16 << 20),
    )(*arrays, *pinned(after))


def used_by(group):
    return sorted({o for e in group for o, _ in uses(e)})


def pack_weights(groups, w_in_ref, w_out_ref, to_ref):
    rows_in, rows_out = w_in_ref.shape[1], w_out_ref.shape[1]
    at = 0
    for e in (e for group in groups for e in group):
        for q in range(to_ref.shape[0]):
            to_ref[q, at : at + rows_in] = w_in_ref[e]
            to_ref[q, at + rows_in : at + rows_in + rows_out] = w_out_ref[e]
        at += rows_in + rows_out
    return at


def pack_kernel(in_bias, gain, shift, out_bias, task_gate, shared_gate, w_in_ref, w_out_ref, to_ref):
    rows_in, rows_out = w_in_ref.shape[1], w_out_ref.shape[1]
    at = pack_weights(GROUPS[:1], w_in_ref, w_out_ref, to_ref)
    n = SPEC + SHARED
    for q in range(to_ref.shape[0]):
        to_ref[q, at:] = jnp.zeros((to_ref.shape[1] - at, to_ref.shape[2]), F32)
        for k, bias in enumerate((in_bias, gain, shift, out_bias)):
            to_ref[q, at + k * EXPERTS : at + (k + 1) * EXPERTS, 0:rows_out] = bias[...]
        base = at + 4 * EXPERTS
        for t in range(TASKS):
            to_ref[q, base + t * n : base + (t + 1) * n, 0:rows_in] = task_gate[t]
        base += TASKS * n
        to_ref[q, base : base + EXPERTS, 0:rows_in] = shared_gate[...]


def pack(pairs, w_in, in_bias, gain, shift, w_out, out_bias, task_gate, shared_gate):
    rows = len(GROUPS[0]) * (w_in.shape[1] + w_out.shape[1]) + 4 * EXPERTS + GATES
    return pl.pallas_call(
        pack_kernel,
        out_shape=jax.ShapeDtypeStruct((pairs, rows, w_in.shape[2]), F32),
        compiler_params=pltpu.CompilerParams(vmem_limit_bytes=VMEM_BYTES),
    )(in_bias, gain, shift, out_bias, task_gate.transpose(0, 2, 1), shared_gate.T, w_in, w_out)


def prep_kernel(x_ref, c_refs, valid_ref, w_in_ref, w_out_ref, xh_ref, xl_ref, ct_ref, to_ref, done_ref):
    depth = x_ref.shape[1]

    @pl.when(pl.program_id(0) == 0)
    def _():
        pack_weights(GROUPS[1:], w_in_ref, w_out_ref, to_ref)
        done_ref[...] = jnp.zeros_like(done_ref)

    high, low = halves(x_ref[...].T)
    xh_ref[0:depth] = high
    xh_ref[depth:] = jnp.ones((xh_ref.shape[0] - depth, xh_ref.shape[1]), BF16)
    xl_ref[...] = low
    valid = valid_ref[...]
    for k, c_ref in enumerate(c_refs):
        ct_ref[k] = c_ref[0].T * valid


def prep(features, cotangent, valid, w_in, w_out, pairs):
    rows, depth = features.shape
    packed = sum(len(g) for g in GROUPS[1:]) * (w_in.shape[1] + w_out.shape[1])
    units = cotangent.shape[2]
    used = used_by(GROUPS[0])
    outs = len(used)
    return pl.pallas_call(
        prep_kernel,
        grid=(rows // TILE,),
        in_specs=[
            pl.BlockSpec((TILE, depth), lambda i: (i, 0)),
            [pl.BlockSpec((1, TILE, units), lambda i, o=o: (o, i, 0)) for o in used],
            pl.BlockSpec((1, TILE), lambda i: (0, i)),
            pl.BlockSpec(w_in.shape, lambda i: (0, 0, 0)),
            pl.BlockSpec(w_out.shape, lambda i: (0, 0, 0)),
        ],
        out_specs=[
            pl.BlockSpec((depth + STEP, TILE), lambda i: (0, i)),
            pl.BlockSpec((depth, TILE), lambda i: (0, i)),
            pl.BlockSpec((outs, units, TILE), lambda i: (0, 0, i)),
            pl.BlockSpec((pairs, packed, units), lambda i: (0, 0, 0)),
            pl.BlockSpec(TOKEN, lambda i: (0, 0)),
        ],
        out_shape=[
            jax.ShapeDtypeStruct((depth + STEP, rows), BF16),
            jax.ShapeDtypeStruct((depth, rows), BF16),
            jax.ShapeDtypeStruct((outs, units, rows), F32),
            jax.ShapeDtypeStruct((pairs, packed, units), F32),
            jax.ShapeDtypeStruct(TOKEN, F32),
        ],
        compiler_params=pltpu.CompilerParams(vmem_limit_bytes=VMEM_BYTES),
        cost_estimate=pl.CostEstimate(flops=0, bytes_accessed=26000000, transcendentals=0),
    )(features, [cotangent] * outs, valid, w_in, w_out)


def softmax_rows(v):
    e = jnp.exp(v - jnp.max(v, axis=0, keepdims=True))
    return e / jnp.sum(e, axis=0, keepdims=True)


def expert_kernel(group, first, last, n_after, partial, fresh, *refs):
    used = used_by(group)
    names = ["core", "own", "other"] + ([] if first else ["small"]) + ["xh", "xl"]
    names += [f"c{o}" for o in used if o not in fresh]
    names += (["valid"] + [f"cot{o}" for o in fresh]) if fresh else []
    names += [] if first else ["prob"]
    if last:
        names += [f"dp{k}" for k in range(len(GROUPS) - 1)]
    names += [f"in{o}" for o in partial]
    names += [f"after{k}" for k in range(n_after)]
    names += [f"{name}{l}" for name in ("dah", "dal") for l in range(len(group))]
    names += ["out"] if last else [f"out{o}" for o in used]
    names += ["wih", "wil"]
    names += ["keep", "send"] if last else ["grads"]
    if first:
        names += ["prob", "small", "gates"]
    names += ["dl"] if last else ["dp"]
    names += ["done"] + [f"c{o}" for o in fresh]
    each = ["win_t", "wp", "wp_t", "b_in", "b_out", "acc_w", "acc_g"]
    each += ["h", "u", "a", "xhat", "h2", "g", "ex", "xhh", "xhl", "dzh", "dzl"]
    names += [f"{name}{l}" for name in each for l in range(len(group))]
    if last:
        names += ["all_dp", "acc_gate"] + [f"mix{o}" for o in used]
    r = dict(zip(names, refs, strict=True))
    for name in (*each, "dah", "dal"):
        r[name] = [r[f"{name}{l}"] for l in range(len(group))]
    step = pl.program_id(0)
    count = len(group)
    units = r["acc_w"][0].shape[1]
    depth = r["xl"].shape[0]
    pairs = r["own"].shape[0]
    devices = 2 * pairs
    rows_in, rows_out = depth // devices, units // devices
    rows_all = rows_in + rows_out
    core = r["core"][0]
    tile = r["xl"].shape[1]
    chunks = [slice(k, k + STEP) for k in range(0, units, STEP)]

    @pl.when(step == 0)
    def _():
        if first:
            begin = count * rows_all
            r["small"][...] = jnp.zeros_like(r["small"])
            r["gates"][...] = jnp.zeros_like(r["gates"])
            for q in range(pairs):
                block, offset = divmod(2 * q * rows_in, units)
                lanes = slice(block * units, (block + 1) * units)
                for src, at in ((r["own"], core), (r["other"], 1 - core)):
                    piece = src[q, begin : begin + 4 * EXPERTS]
                    r["small"][...] += pltpu.roll(piece, (2 * q + at) * rows_out, 1)
                    piece = src[q, begin + 4 * EXPERTS : begin + 4 * EXPERTS + GATES]
                    r["gates"][:, lanes] += pltpu.roll(piece, offset + at * rows_in, 1)
        for l, e in enumerate(group):
            base = l * rows_all
            for q in range(pairs):
                for src, at in ((r["own"], core), (r["other"], 1 - core)):
                    place = q * 2 + at
                    r["acc_w"][l][pl.ds(place * rows_in, rows_in)] = src[q, base : base + rows_in]
                    r["acc_g"][l][pl.ds(place * rows_out, rows_out)] = src[
                        q, base + rows_in : base + rows_all
                    ]
            w_in = r["acc_w"][l][0:depth]
            high, low = halves(w_in)
            r["wih"][l] = high
            r["wil"][l] = low
            high, low = halves((0.5 * w_in).T)
            top = r["win_t"][l].shape[0] // 2
            r["win_t"][l][0:units] = high
            r["win_t"][l][top : top + units] = low
            w_out = r["acc_g"][l][0:units]
            b_in, gain, shift, b_out = (r["small"][k * EXPERTS + e : k * EXPERTS + e + 1] for k in range(4))
            scaled = w_out * wide(column(gain), units)
            high, low = halves(scaled)
            r["wp"][l][0:units] = high
            r["wp"][l][units:] = low
            high, low = halves((0.5 * scaled).T)
            r["wp_t"][l][0:units] = high
            r["wp_t"][l][units:] = low
            b_out = b_out + jnp.sum(w_out * wide(column(shift), units), axis=0, keepdims=True)
            r["b_in"][l][...] = column(0.5 * b_in)
            r["b_out"][l][...] = column(0.5 * b_out)
            r["xhh"][l][units:] = jnp.ones((STEP, tile), BF16)
        if first:
            high, low = halves(r["gates"][...])
            top = r["win_t"][0].shape[0] // 2
            r["win_t"][0][units:top] = high
            r["win_t"][0][top + units :] = low
            for l in range(1, count):
                r["win_t"][l][units:top] = high
                r["win_t"][l][top + units :] = low
        for l in range(count):
            r["acc_w"][l][...] = jnp.zeros_like(r["acc_w"][l])
            r["acc_g"][l][...] = jnp.zeros_like(r["acc_g"][l])
        r["done"][...] = jnp.zeros_like(r["done"])
        if last:
            r["acc_gate"][...] = jnp.zeros_like(r["acc_gate"])

    stats = {}

    spans = [slice(k, k + SPAN) for k in range(0, tile, SPAN)]
    zero = jnp.zeros((STEP, SPAN), F32)

    def project_in(l, s):
        r["h"][l][:, s] = dot3_stacked(r["win_t"][l], r["xh"][0:depth, s], r["xl"][:, s])

    def gate_weights(s):
        z = r["h"][0][units:, s]
        for lower, upper in ((0, 4), (4, 8), (8, 14)):
            r["prob"][lower:upper, s] = softmax_rows(z[lower:upper])
        r["prob"][14:16, s] = jnp.zeros((2, SPAN), F32)

    def normalise(l, s):
        total = zero
        for c in chunks:
            h = r["h"][l][c, s] + wide(r["b_in"][l][c], SPAN)
            u = 1.0 + jnp.tanh(h)
            a = h * u
            r["u"][l][c, s] = u
            r["a"][l][c, s] = a
            total = total + a
        mean = jnp.sum(total, axis=0, keepdims=True) * (1.0 / units)
        total = zero
        for c in chunks:
            d = r["a"][l][c, s] - mean
            total = total + d * d
        scale = lax.rsqrt(jnp.sum(total, axis=0, keepdims=True) * (1.0 / units) + EPSILON)
        stats[l, s.start] = scale
        for c in chunks:
            x = (r["a"][l][c, s] - mean) * scale
            r["xhat"][l][c, s] = x
            r["xhh"][l][c, s], r["xhl"][l][c, s] = halves(x)

    def project_out(l, s):
        r["h2"][l][:, s] = dot3_stacked(r["wp_t"][l], r["xhh"][l][0:units, s], r["xhl"][l][:, s])

    def combine(l, s):
        taken = uses(group[l])
        prob = [0.5 * r["prob"][row : row + 1, s] for _, row in taken]
        sums = [zero for _ in taken]
        end = l == count - 1
        full = [[r["prob"][row : row + 1, s] for _, row in uses(e)] for e in group] if end else None
        for c in chunks:
            h = r["h2"][l][c, s] + wide(r["b_out"][l][c], SPAN)
            u = 1.0 + jnp.tanh(h)
            ex = h * u
            if not end:
                r["ex"][l][c, s] = ex
            slope = u + ex * (2.0 - u)
            d = None
            for k, (o, _) in enumerate(taken):
                cot = r[f"c{o}"][0, c, s]
                sums[k] = sums[k] + cot * ex
                term = prob[k] * cot
                d = term if d is None else d + term
                if end:
                    mix = full[l][k] * ex
                    for m in range(l):
                        mix = mix + full[m][k] * r["ex"][m][c, s]
                    if o in partial:
                        mix = mix + r[f"in{o}"][c, s]
                    if last:
                        r[f"mix{o}"][c, s] = mix
                    else:
                        r[f"out{o}"][c, s] = mix
            r["dzh"][l][c, s], r["dzl"][l][c, s] = halves(d * slope)
        for k, (_, row) in enumerate(taken):
            value = jnp.sum(sums[k], axis=0, keepdims=True)
            if last:
                r["all_dp"][row : row + 1, s] = value
            else:
                at = l * len(taken) + k
                r["dp"][at : at + 1, s] = value

    def back_out(l, s):
        r["g"][l][:, s] = dot3_stacked(r["wp"][l], r["dzh"][l][:, s], r["dzl"][l][:, s])

    def grad_out(l):
        r["acc_g"][l][...] += dot(r["xhh"][l][...], r["dzh"][l][...], NT) + dot(
            r["xhh"][l][...], r["dzl"][l][...], NT
        )
        r["acc_g"][l][0:units] += dot(r["xhl"][l][...], r["dzh"][l][...], NT)

    def back_norm(l, s):
        total, along = zero, zero
        for c in chunks:
            g = r["g"][l][c, s]
            total = total + g
            along = along + g * r["xhat"][l][c, s]
        mean = jnp.sum(total, axis=0, keepdims=True) * (1.0 / units)
        along = jnp.sum(along, axis=0, keepdims=True) * (1.0 / units)
        scale = 0.5 * stats[l, s.start]
        for c in chunks:
            u, a = r["u"][l][c, s], r["a"][l][c, s]
            slope = (u + a * (2.0 - u)) * scale
            da = (r["g"][l][c, s] - mean - r["xhat"][l][c, s] * along) * slope
            r["dah"][l][c, s], r["dal"][l][c, s] = halves(da)

    def grad_in(l):
        high, low = r["dah"][l][...], r["dal"][l][...]
        r["acc_w"][l][...] += dot(r["xh"][...], high, NT) + dot(r["xh"][...], low, NT)
        r["acc_w"][l][0:depth] += dot(r["xl"][...], high, NT)

    chains = [(l, s) for l in range(count) for s in spans]
    for o in fresh:
        r[f"c{o}"][0] = r[f"cot{o}"][0].T * r["valid"][...]
    for stage in ORDER:
        if isinstance(stage, tuple):
            name, k = stage
            if name == "go":
                grad_out(k)
            elif name == "gi":
                grad_in(k)
            else:
                at = {
                    "in": project_in, "norm": normalise, "out": project_out, "comb": combine, "back": back_out,
                    "bnorm": back_norm,
                }[name]
                at(*chains[k])
                if name == "in" and first and chains[k][0] == 0:
                    gate_weights(chains[k][1])

    if last:
        for o in used:
            r["out"][o] = r[f"mix{o}"][...].T
    if last:
        for k, g in enumerate(GROUPS[:-1]):
            at = 0
            for e in g:
                for _, row in uses(e):
                    r["all_dp"][row : row + 1] = r[f"dp{k}"][at : at + 1]
                    at += 1
        for lower, upper in ((0, 4), (4, 8), (8, 14)):
            p, d = r["prob"][lower:upper], r["all_dp"][lower:upper]
            r["dl"][lower:upper] = p * (d - jnp.sum(p * d, axis=0, keepdims=True))
        r["dl"][14:16] = jnp.zeros((2, tile), F32)
        high, low = halves(r["dl"][...])
        both = dot(jnp.concatenate([high, low], 0), r["xh"][0:depth], NT)
        r["acc_gate"][...] += both[0:GATES] + both[GATES:] + dot(high, r["xl"][...], NT)

    @pl.when(step == pl.num_programs(0) - 1)
    def _():
        for l in range(count):
            base = l * (rows_all + 8)
            tail = jnp.concatenate([r["acc_g"][l][units : units + 1], r["acc_w"][l][depth : depth + 1]], 0)
            tail = jnp.concatenate([tail] * 4, 0)
            if last:
                places = [
                    (dst, q, q * 2 + at)
                    for q in range(pairs)
                    for dst, at in ((r["keep"], core), (r["send"], 1 - core))
                ]
            else:
                places = [(r["grads"], k, k) for k in range(devices)]
            for dst, q, place in places:
                dst[q, base : base + rows_in] = r["acc_w"][l][pl.ds(place * rows_in, rows_in)]
                dst[q, base + rows_in : base + rows_all] = r["acc_g"][l][pl.ds(place * rows_out, rows_out)]
                dst[q, base + rows_all : base + rows_all + 8] = tail
        if last:
            gate = r["acc_gate"][...]
            base = count * (rows_all + 8)
            for q in range(pairs):
                even = gate[:, 2 * q * rows_in : (2 * q + 1) * rows_in]
                odd = gate[:, (2 * q + 1) * rows_in : (2 * q + 2) * rows_in]
                for dst, at in ((r["keep"], core), (r["send"], 1 - core)):
                    dst[q, base:, 0:rows_in] = jnp.where(at == 0, even, odd)


def expert_call(group, core, own, other, small, xh, xl, cts, valid, cotangent, prob, dps, last, after, skip, mixed):
    first = small is None
    pairs, _, units = own.shape
    depth, rows = xl.shape
    devices = 2 * pairs
    rows_in, rows_out = depth // devices, units // devices
    count = len(group)
    whole = lambda shape: pl.BlockSpec(shape, lambda i: (0,) * len(shape))
    along = lambda n: pl.BlockSpec((n, TILE), lambda i: (0, i))
    used = used_by(group)
    old, fresh = [o for o in used if o in cts], tuple(o for o in used if o not in cts)
    ins = [core, own, other] + ([] if first else [small]) + [xh, xl] + [cts[o][0] for o in old]
    held = own.shape[1] if first else count * (rows_in + rows_out)
    weights = pl.BlockSpec((pairs, held, units), lambda i: (0, skip, 0))
    in_specs = [
        pl.BlockSpec(memory_space=pltpu.SMEM),
        weights,
        weights,
        *([] if first else [whole((4 * EXPERTS, units))]),
        along(xh.shape[0]),
        along(depth),
    ]
    in_specs += [pl.BlockSpec((1, units, TILE), lambda i, k=cts[o][1]: (k, 0, i)) for o in old]
    if fresh:
        ins += [valid] + [cotangent] * len(fresh)
        in_specs.append(along(1))
        in_specs += [pl.BlockSpec((1, TILE, units), lambda i, o=o: (o, i, 0)) for o in fresh]
    if not first:
        ins.append(prob)
        in_specs.append(along(GATES))
    if last:
        ins += dps
        in_specs += [along(8)] * len(dps)
    ins += [mixed[o] for o in sorted(mixed)]
    in_specs += [along(units)] * len(mixed)
    ins += pinned(after)
    in_specs += [pl.BlockSpec(memory_space=pltpu.HBM)] * len(after)
    packed = count * (rows_in + rows_out + 8)
    shape = jax.ShapeDtypeStruct
    if last:
        mixes = [
            (pl.BlockSpec((len(used), TILE, units), lambda i: (0, i, 0)), shape((len(used), rows, units), F32))
        ]
    else:
        mixes = [(along(units), shape((units, rows), F32))] * len(used)
    outs = [
        *[(along(units), shape((units, rows), BF16))] * (2 * count),
        *mixes,
        (whole((count, depth, units)), shape((count, depth, units), BF16)),
        (whole((count, depth, units)), shape((count, depth, units), BF16)),
    ]
    if last:
        packed += GATES
        outs += [(whole((pairs, packed, units)), shape((pairs, packed, units), F32))] * 2
    else:
        outs.append((whole((devices, packed, units)), shape((devices, packed, units), F32)))
    if first:
        outs.append((along(GATES), shape((GATES, rows), F32)))
        outs += [
            (whole((n, lanes)), shape((n, lanes), F32)) for n, lanes in ((4 * EXPERTS, units), (GATES, depth))
        ]
    if last:
        outs.append((along(GATES), shape((GATES, rows), F32)))
    else:
        outs.append((along(8), shape((8, rows), F32)))
    outs.append((whole(TOKEN), shape(TOKEN, F32)))
    outs += [
        (pl.BlockSpec((1, units, TILE), lambda i: (0, 0, i)), shape((1, units, rows), F32)) for _ in fresh
    ]
    top = units + (GATES if first else 0)
    kinds = [
        ((2 * top, depth), BF16),
        ((2 * units, units), BF16),
        ((2 * units, units), BF16),
        ((units, LANES), F32),
        ((units, LANES), F32),
        ((depth + STEP, units), F32),
        ((units + STEP, units), F32),
        ((top, TILE), F32),
        ((units, TILE), F32),
        ((units, TILE), F32),
        ((units, TILE), F32),
        ((units, TILE), F32),
        ((units, TILE), F32),
        ((units, TILE), F32),
        ((units + STEP, TILE), BF16),
        ((units, TILE), BF16),
        ((units, TILE), BF16),
        ((units, TILE), BF16),
    ]
    scratch = [pltpu.VMEM(*kind) for kind in kinds for _ in group]
    if last:
        scratch += [pltpu.VMEM((GATES, TILE), F32), pltpu.VMEM((GATES, depth), F32)]
        scratch += [pltpu.VMEM((units, TILE), F32)] * len(used)
    return pl.pallas_call(
        functools.partial(expert_kernel, group, first, last, len(after), tuple(sorted(mixed)), fresh),
        grid=(rows // TILE,),
        in_specs=in_specs,
        out_specs=[o[0] for o in outs],
        out_shape=[o[1] for o in outs],
        scratch_shapes=scratch,
        compiler_params=pltpu.CompilerParams(vmem_limit_bytes=58 << 20),
        cost_estimate=pl.CostEstimate(
            flops=20000000000 * count // 2, bytes_accessed=30000000, transcendentals=0
        ),
    )(*ins)


def final_kernel(steps, *refs):
    n = EXPERTS
    dahs, dals = refs[:n], refs[n : 2 * n]
    wihs, wils = refs[2 * n : 2 * n + len(GROUPS)], refs[2 * n + len(GROUPS) : 2 * n + 2 * len(GROUPS)]
    dl_ref, gates_ref = refs[2 * n + 2 * len(GROUPS) : 2 * n + 2 * len(GROUPS) + 2]
    gf_ref, done_ref, gate_ref = refs[-3:]
    done_ref[...] = jnp.zeros_like(done_ref)

    @pl.when(pl.program_id(0) == 0)
    def _():
        high, low = halves(gates_ref[...])
        gate_ref[0:GATES] = high
        gate_ref[GATES : 2 * GATES] = low
        gate_ref[2 * GATES :] = high

    for k in range(0, TILE, SPAN):
        span = slice(k, k + SPAN)
        high, low = halves(dl_ref[:, span])
        value = dot(gate_ref[...], jnp.concatenate([high, high, low], 0), TN)
        at = 0
        for k, group in enumerate(GROUPS):
            for l in range(len(group)):
                value = value + dot3(wihs[k][l], wils[k][l], dahs[at][:, span], dals[at][:, span], NN)
                at += 1
        gf_ref[span] = value.T


def final_call(dahs, dals, wihs, wils, dl, gates, part, before, after):
    rows = dl.shape[1]
    _, depth, units = wihs[0].shape
    tiles = rows // TILE
    skip, end = (tiles * k // PARTS for k in (part, part + 1))
    steps, parts = end - skip, PARTS
    whole = lambda a: pl.BlockSpec(a.shape, lambda i: (0,) * a.ndim)
    along = lambda a: pl.BlockSpec((a.shape[0], TILE), lambda i: (0, i + skip))
    ins = [*dahs, *dals, *wihs, *wils, dl, gates, *before, *pinned(after)]
    n = 2 * EXPERTS + 2 * len(GROUPS) + 2
    return pl.pallas_call(
        functools.partial(final_kernel, steps),
        grid=(steps,),
        in_specs=[along(a) for a in (*dahs, *dals)]
        + [whole(a) for a in (*wihs, *wils)]
        + [along(dl), whole(gates)]
        + [pl.BlockSpec(memory_space=pltpu.HBM)] * (len(before) + len(after)),
        out_specs=[pl.BlockSpec((TILE, depth), lambda i: (i + skip, 0)), pl.BlockSpec(TOKEN, lambda i: (0, 0))],
        out_shape=[jax.ShapeDtypeStruct((rows, depth), F32), jax.ShapeDtypeStruct(TOKEN, F32)],
        scratch_shapes=[pltpu.VMEM((3 * GATES, depth), BF16)],
        input_output_aliases={n + k: k for k in range(len(before))},
        compiler_params=pltpu.CompilerParams(vmem_limit_bytes=58 << 20),
        cost_estimate=pl.CostEstimate(
            flops=15000000000 // parts, bytes_accessed=25000000 // parts, transcendentals=0
        ),
    )(*ins)


def finish_kernel(me_ref, *refs):
    n = len(GROUPS) + 1
    w_out_ref, gain_ref, shift_ref = refs[n : n + 3]
    g_in, g_in_bias, g_gain, g_shift, g_out, g_out_bias, g_task, g_shared = refs[n + 3 :]
    rows_in, rows_out, units = g_in.shape[1], g_out.shape[1], g_in.shape[2]
    me = me_ref[0]

    def own(row):
        value = row[:, 0:rows_out]
        for p in range(1, units // rows_out):
            value = jnp.where(me == p, row[:, p * rows_out : (p + 1) * rows_out], value)
        return value

    def as_row(col):
        return jnp.broadcast_to(col, (rows_out, LANES)).T[0:1]

    for k, group in enumerate(GROUPS):
        if k < len(GROUPS) - 1:
            add = lambda lower, upper, a=refs[k]: a[lower:upper]
        else:
            add = lambda lower, upper, a=refs[k], b=refs[k + 1]: a[lower:upper] + b[lower:upper]
        at = 0
        for e in group:
            g_in[e] = add(at, at + rows_in)
            at += rows_in
            raw = add(at, at + rows_out)
            at += rows_out
            tail = add(at, at + 8)
            at += 8
            total = tail[0:1]
            gain = wide(column(gain_ref[e : e + 1]), units)
            shift = wide(column(shift_ref[e : e + 1]), units)
            g_out[e] = gain * raw + shift * total
            w = w_out_ref[e]
            g_gain[e : e + 1] = as_row(jnp.sum(w * raw, axis=1, keepdims=True))
            g_shift[e : e + 1] = as_row(jnp.sum(w * total, axis=1, keepdims=True))
            g_in_bias[e : e + 1] = own(tail[1:2])
            g_out_bias[e : e + 1] = own(total)
    gate = add(at, at + GATES)[:, 0:rows_in]
    m = SPEC + SHARED
    for t in range(TASKS):
        g_task[t] = gate[t * m : (t + 1) * m]
    g_shared[...] = gate[TASKS * m : TASKS * m + EXPERTS]


def finish(me, totals, w_in, w_out, gain, shift):
    experts, rows_in, units = w_in.shape
    rows_out = w_out.shape[1]
    shape = lambda *s: jax.ShapeDtypeStruct(s, F32)
    vector = shape(experts, rows_out)
    outs = [
        shape(*w_in.shape),
        vector,
        vector,
        vector,
        shape(*w_out.shape),
        vector,
        shape(TASKS, SPEC + SHARED, rows_in),
        shape(EXPERTS, rows_in),
    ]
    vmem = pl.BlockSpec(memory_space=pltpu.VMEM)
    got = pl.pallas_call(
        finish_kernel,
        in_specs=[pl.BlockSpec(memory_space=pltpu.SMEM)] + [vmem] * (len(totals) + 3),
        out_specs=[vmem] * len(outs),
        out_shape=outs,
        compiler_params=pltpu.CompilerParams(vmem_limit_bytes=16 << 20),
    )(me, *totals, w_out, gain, shift)
    return (*got[:6], got[6].transpose(0, 2, 1), got[7].T)


def make(mesh):
    n_fsdp, n_dp = mesh.shape["fsdp"], mesh.shape["dp"]
    pairs = n_fsdp // 2
    across = [[q * 2 + c for q in range(pairs)] for c in range(2)]
    twin = [(i, i ^ 1) for i in range(n_fsdp)]

    def spread_out(x):
        return lax.all_to_all(x, "fsdp", 0, 0, axis_index_groups=across)

    def swap(x, bit):
        return lax.ppermute(x, "dp", [(i, i ^ bit) for i in range(n_dp)])

    def reduce_some(x, token, some, beside):
        for bit in some:
            x, token = total([x, swap(x, bit)], beside)
        return x, token

    bits = [1 << k for k in reversed(range(n_dp.bit_length() - 1))]

    def on_device(
        features, cotangent, counts, keep, w_in, in_bias, norm_gain, norm_bias, w_out, out_bias, task_gate, shared_gate
    ):
        rows = features.shape[0]
        depth = features.shape[1]
        experts, rows_in, units = w_in.shape
        rows_out = w_out.shape[1]
        valid = (lax.broadcasted_iota(jnp.int32, (1, rows), 1) < counts[0]) & (keep.reshape(1, rows) > 0)
        me = lax.axis_index("fsdp")
        core = (me % 2).astype(jnp.int32).reshape(1)
        valid = valid.astype(F32)
        xh, xl, ct, spread, done = prep(features, cotangent, valid, w_in, w_out, pairs)
        own0 = tie(
            spread_out(
                pack(pairs, w_in, in_bias, norm_gain, norm_bias, w_out, out_bias, task_gate, shared_gate)
            ),
            [done],
        )
        other0 = lax.ppermute(own0, "fsdp", twin)
        cts = {o: (ct, k) for k, o in enumerate(used_by(GROUPS[0]))}

        def parts_of(got, group):
            n = len(group)
            m = 1 if group == GROUPS[-1] else len({o for e in group for o, _ in uses(e)})
            return got[:n], got[n : 2 * n], got[2 * n : 2 * n + m], got[2 * n + m :]

        got = expert_call(GROUPS[0], core, own0, other0, None, xh, xl, cts, valid, cotangent, None, [], False, [], 0, {})
        dah0, dal0, mix0, (wih0, wil0, grads0, prob, small, gates, dp0, done0) = parts_of(got, GROUPS[0])
        own1 = tie(spread_out(spread), [done0])
        other1 = lax.ppermute(own1, "fsdp", twin)
        got = expert_call(
            GROUPS[1], core, own1, other1, small, xh, xl, cts, valid, cotangent, prob, [], False, [], 0, {2: mix0[1]}
        )
        dah1, dal1, mix1, (wih1, wil1, grads1, dp1, done1, *fresh) = parts_of(got, GROUPS[1])
        cts.update(zip([o for o in used_by(GROUPS[1]) if o not in cts], [(c, 0) for c in fresh]))
        sum0, token0 = total([lax.all_to_all(grads0, "fsdp", 0, 0)], [done1])
        got = expert_call(
            GROUPS[2],
            core,
            own1,
            other1,
            small,
            xh,
            xl,
            cts,
            valid,
            cotangent,
            prob,
            [dp0, dp1],
            True,
            [token0],
            1,
            {0: mix0[0], 1: mix1[0], 2: mix1[1]},
        )
        dah2, dal2, (outputs,), (wih2, wil2, keep2, send2, dl, done2) = parts_of(got, GROUPS[2])
        sum1, token1 = total([lax.all_to_all(grads1, "fsdp", 0, 0)], [done2])
        sum0, token0 = reduce_some(sum0, token0, bits[:-1], [done2])
        kept = keep2 + lax.ppermute(tie(send2, [token0, token1]), "fsdp", twin)
        tail = (
            (*dah0, *dah1, *dah2),
            (*dal0, *dal1, *dal2),
            (wih0, wih1, wih2),
            (wil0, wil1, wil2),
            dl,
            gates,
        )
        part, done3 = final_call(*tail, 0, [], [])
        sum2, token2 = total([spread_out(kept)], [done3])
        sum1, token1 = reduce_some(sum1, token1, bits[:-1], [done3])
        part, done4 = final_call(*tail, 1, [part], [token1, token2])
        sum0, token0 = total([sum0, swap(sum0, bits[-1])], [done4])
        sum2, token2 = reduce_some(sum2, token2, bits[:-1], [done4])
        grad_features, done5 = final_call(*tail, 2, [part], [token0, token2])
        sum1, token1 = total([sum1, swap(sum1, bits[-1])], [done5])
        pair2 = (sum2, swap(sum2, bits[-1]))
        rest = finish(me.astype(jnp.int32).reshape(1), (sum0, sum1, *pair2), w_in, w_out, norm_gain, norm_bias)
        return (outputs, grad_features, *rest)

    return on_device


def solution(mesh):
    placed = (
        P(("dp", "fsdp"), None),
        P(None, ("dp", "fsdp"), None),
        P(("dp", "fsdp")),
        P(("dp", "fsdp")),
        P(None, "fsdp", None),
        P(None, "fsdp"),
        P(None, "fsdp"),
        P(None, "fsdp"),
        P(None, "fsdp", None),
        P(None, "fsdp"),
        P(None, "fsdp", None),
        P("fsdp", None),
    )
    return jax.shard_map(
        make(mesh),
        mesh=mesh,
        in_specs=placed,
        out_specs=(
            P(None, ("dp", "fsdp"), None),
            P(("dp", "fsdp"), None),
            P(None, "fsdp", None),
            P(None, "fsdp"),
            P(None, "fsdp"),
            P(None, "fsdp"),
            P(None, "fsdp", None),
            P(None, "fsdp"),
            P(None, "fsdp", None),
            P("fsdp", None),
        ),
        check_vma=False,
    )
```
